32 devices in a mesh: dp: 8 (over y, x, core), mp: 4 (over z).
Axes of the slice: x: 2, y: 2, z: 4, core: 2. Of those that a mesh axis runs over, the one named last changes fastest.
Arguments:
- language: bfloat16 [288, 20, 768], P(('dp', 'mp')), may hold values from -6 to 6
- images: bfloat16 [72, 36, 768], P('dp'), may hold values from -6 to 6
- counts: int32 [8, 9], P('dp'), may hold values from 1 to 10, 36 in all within a row
- language_cot: bfloat16 [288, 20, 768], P(('dp', 'mp')), may hold values from -6 to 6
- vision_cot: bfloat16 [288, 36, 768], P(('dp', 'mp')), may hold values from -6 to 6
- attn_in_weight: float32 [3, 768, 3, 768], P(None, 'dp', None, 'mp')
- attn_in_moment: float32 [3, 768, 3, 768], P(None, 'dp', None, 'mp'), may hold values from -0.00015258789 to 0.00015258789
- attn_in_square: float32 [3, 768, 3, 768], P(None, 'dp', None, 'mp')
- attn_in_average: float32 [3, 768, 3, 768], P(None, 'dp', None, 'mp'), may hold values from -0.15625 to 0.15625
- attn_out_weight: float32 [3, 768, 768], P(None, 'mp', 'dp')
- attn_out_moment: float32 [3, 768, 768], P(None, 'mp', 'dp'), may hold values from -0.00015258789 to 0.00015258789
- attn_out_square: float32 [3, 768, 768], P(None, 'mp', 'dp')
- attn_out_average: float32 [3, 768, 768], P(None, 'mp', 'dp'), may hold values from -0.21875 to 0.21875
- ffn_in_weight: float32 [2, 768, 3072], P(None, 'dp', 'mp')
- ffn_in_moment: float32 [2, 768, 3072], P(None, 'dp', 'mp'), may hold values from -0.00015258789 to 0.00015258789
- ffn_in_square: float32 [2, 768, 3072], P(None, 'dp', 'mp')
- ffn_in_average: float32 [2, 768, 3072], P(None, 'dp', 'mp'), may hold values from -0.21875 to 0.21875
- ffn_out_weight: float32 [2, 3072, 768], P(None, 'mp', 'dp')
- ffn_out_moment: float32 [2, 3072, 768], P(None, 'mp', 'dp'), may hold values from -0.00015258789 to 0.00015258789
- ffn_out_square: float32 [2, 3072, 768], P(None, 'mp', 'dp')
- ffn_out_average: float32 [2, 3072, 768], P(None, 'mp', 'dp'), may hold values from -0.109375 to 0.109375
- norm_weight: float32 [2, 5, 768], replicated
- norm_moment: float32 [2, 5, 768], replicated, may hold values from -0.00061035156 to 0.00061035156
- norm_square: float32 [2, 5, 768], replicated
- norm_average: float32 [2, 5, 768], replicated, may hold values from 0.5 to 1.5
Outputs:
- language_out: bfloat16 [288, 20, 768], P(('dp', 'mp'))
- vision_out: bfloat16 [288, 36, 768], P(('dp', 'mp'))
- language_grad: float32 [288, 20, 768], P(('dp', 'mp'))
- image_grad: float32 [72, 36, 768], P('dp')
- attn_in_grad: float32 [3, 768, 3, 768], P(None, 'dp', None, 'mp')
- attn_in_new_moment: float32 [3, 768, 3, 768], P(None, 'dp', None, 'mp')
- attn_in_new_square: float32 [3, 768, 3, 768], P(None, 'dp', None, 'mp')
- attn_in_new_weight: float32 [3, 768, 3, 768], P(None, 'dp', None, 'mp')
- attn_in_copy: bfloat16 [3, 768, 3, 768], P(None, 'dp', None, 'mp')
- attn_in_new_average: float32 [3, 768, 3, 768], P(None, 'dp', None, 'mp')
- attn_out_grad: float32 [3, 768, 768], P(None, 'mp', 'dp')
- attn_out_new_moment: float32 [3, 768, 768], P(None, 'mp', 'dp')
- attn_out_new_square: float32 [3, 768, 768], P(None, 'mp', 'dp')
- attn_out_new_weight: float32 [3, 768, 768], P(None, 'mp', 'dp')
- attn_out_copy: bfloat16 [3, 768, 768], P(None, 'mp', 'dp')
- attn_out_new_average: float32 [3, 768, 768], P(None, 'mp', 'dp')
- ffn_in_grad: float32 [2, 768, 3072], P(None, 'dp', 'mp')
- ffn_in_new_moment: float32 [2, 768, 3072], P(None, 'dp', 'mp')
- ffn_in_new_square: float32 [2, 768, 3072], P(None, 'dp', 'mp')
- ffn_in_new_weight: float32 [2, 768, 3072], P(None, 'dp', 'mp')
- ffn_in_copy: bfloat16 [2, 768, 3072], P(None, 'dp', 'mp')
- ffn_in_new_average: float32 [2, 768, 3072], P(None, 'dp', 'mp')
- ffn_out_grad: float32 [2, 3072, 768], P(None, 'mp', 'dp')
- ffn_out_new_moment: float32 [2, 3072, 768], P(None, 'mp', 'dp')
- ffn_out_new_square: float32 [2, 3072, 768], P(None, 'mp', 'dp')
- ffn_out_new_weight: float32 [2, 3072, 768], P(None, 'mp', 'dp')
- ffn_out_copy: bfloat16 [2, 3072, 768], P(None, 'mp', 'dp')
- ffn_out_new_average: float32 [2, 3072, 768], P(None, 'mp', 'dp')
- norm_grad: float32 [2, 5, 768], replicated
- norm_new_moment: float32 [2, 5, 768], replicated
- norm_new_square: float32 [2, 5, 768], replicated
- norm_new_weight: float32 [2, 5, 768], replicated
- norm_new_average: float32 [2, 5, 768], replicated
- grad_norm: float32 [], replicated
The draws below stay inside these ranges and needn't reach their ends.
Inputs may be any that keep to these rules, and one draw needn't show every extreme that they name: `counts`: row g gives the number of items of group g that show each of its 9 images, in image order; items of a group are sorted by image; each row sums to 36 and its largest entry is 10.
All inputs are finite; a program needn't handle non-finite values.
Results may differ from the reference program's by a relative error of at most 0.035.
Values may be sent and summed in bfloat16 or wider, within the bound.
No kernel may reach another device: no remote copies, remote signals or barrier semaphores. Data moves between devices by JAX's collectives and lax.ppermute only.
A program may use at most 192 MiB of HBM per device.

```python
import functools
import math
import jax
import jax.numpy as jnp
import numpy as np
from jax import lax

HEAD_DIM = 64
FF = 3072
WORDS = 20
REGIONS = 36
STEP = 10
D = 768
GROUP_ITEMS = 36
ITEMS = 288
IMG_GRP = 9
IMAGES = 72
MOST = 10
PARAMS = 16522752
N_DP = 8
N_MP = 4


def rising(length, start_value, end_value):
    fraction = jnp.arange(length, dtype=jnp.float32) / (length - 1)
    return start_value + (end_value - start_value) * fraction


def second_moment(key, shape, factor):
    spread = jax.random.uniform(key, shape, jnp.float32, 0.0, math.log(4.0))
    return jnp.exp(spread) * (factor * 0.001 / PARAMS)


def draw_attn_in_weight(key, part):
    key = jax.random.fold_in(key, 1)
    ramp = rising(D, 0.6, 1.8)
    noise = jax.random.normal(key, (3, D, 3, D), jnp.float32)
    kinds = jnp.stack([jnp.ones((D,), jnp.float32), jnp.ones((D,), jnp.float32), ramp])
    return noise * kinds[None, None, :, :] * (0.9 / math.sqrt(D))


def draw_attn_out_weight(key, part):
    key = jax.random.fold_in(key, 2)
    ramp = rising(D, 0.6, 1.8)
    noise = jax.random.normal(key, (3, D, D), jnp.float32)
    return noise * ramp[None, :, None] * (3.0 / math.sqrt(D))


def draw_ffn_in_weight(key, part):
    key = jax.random.fold_in(key, 3)
    ramp = rising(FF, 0.6, 1.8)
    noise = jax.random.normal(key, (2, D, FF), jnp.float32)
    return noise * ramp[None, None, :] * (1.0 / math.sqrt(D))


def draw_ffn_out_weight(key, part):
    key = jax.random.fold_in(key, 4)
    ramp = rising(FF, 0.6, 1.8)
    noise = jax.random.normal(key, (2, FF, D), jnp.float32)
    return noise * ramp[None, :, None] * (1.0 / math.sqrt(FF))


def draw_norm_weight(key, part):
    key = jax.random.fold_in(key, 5)
    ramp = rising(D, 0.6, 1.8)
    gain_key, shift_key = jax.random.split(key)
    gains = ramp[None, :] * (1.0 + 0.1 * jax.random.normal(gain_key, (5, D), jnp.float32))
    shifts = 0.3 * jax.random.normal(shift_key, (5, D), jnp.float32)
    return jnp.stack([gains, shifts])


def draw_attn_in_square(key, part):
    key = jax.random.fold_in(key, 6)
    return second_moment(key, (3, D, 3, D), 1.0)


def draw_attn_out_square(key, part):
    key = jax.random.fold_in(key, 7)
    return second_moment(key, (3, D, D), 1.0)


def draw_ffn_in_square(key, part):
    key = jax.random.fold_in(key, 8)
    return second_moment(key, (2, D, FF), 1.0)


def draw_ffn_out_square(key, part):
    key = jax.random.fold_in(key, 9)
    return second_moment(key, (2, FF, D), 1.0)


def draw_norm_square(key, part):
    key = jax.random.fold_in(key, 10)
    return second_moment(key, (2, 5, D), 16.0)


def shard_levels(stream_key, shape, shards, smallest, largest):
    def one(position, parts):
        draws = jax.random.uniform(jax.random.fold_in(jax.random.fold_in(stream_key, 6), position), (parts,), jnp.float32, smallest / len(shards), largest / len(shards))
        return jnp.repeat(jnp.exp(draws), shape[position] // parts).reshape((-1,) + (1,) * (len(shape) - position - 1))

    level = one(*shards[0])
    for cut in shards[1:]:
        level = level * one(*cut)
    return level


def length_profile(amount, total, bound, lean):
    weights = [(1 << 20) // math.isqrt(rank ** lean) + 1 for rank in range(2, amount + 1)]
    surplus, given = total - bound - (amount - 1), [1] * (amount - 1)
    while surplus > 0:
        candidates = [i for i in range(amount - 1) if given[i] < bound]
        whole, budget = sum([weights[i] for i in candidates]), surplus
        for i in candidates:
            addition = min(bound - given[i], max(1, budget * weights[i] // whole), surplus)
            given[i] = given[i] + addition
            surplus = surplus - addition
    return np.array([bound] + given)


def ragged(own_key, number_of, total, most, skew):
    if number_of == 2:
        one = jax.random.randint(own_key, (), max(1, total - most), min(most, total - 1) + 1)
        return jnp.stack([one, total - one])
    lengths = jnp.asarray(length_profile(number_of, total, most, skew), jnp.int32)
    pairs = (number_of - 1) // 2
    donor, taker = lengths[1:1 + 2 * pairs:2], lengths[2:2 + 2 * pairs:2]
    slack = jnp.minimum(donor - 1, most - taker)
    shifted = jax.random.randint(jax.random.fold_in(own_key, 1), (pairs,), 0, 1 << 20) % (slack + 1)
    lengths = lengths.at[1:1 + 2 * pairs:2].set(donor - shifted).at[2:2 + 2 * pairs:2].set(taker + shifted)
    return lengths[jax.random.permutation(jax.random.fold_in(own_key, 2), number_of)]


def centred(stream_key, dims, deviation, limit, pieces=(), kind=jnp.bfloat16):
    values = deviation * jax.random.normal(stream_key, dims, jnp.float32)
    if pieces:
        values = values * shard_levels(stream_key, dims, pieces, -0.22, 0.18)
    return jnp.clip(values, -limit, limit).astype(kind)


def setup_inputs(seed: int = 0) -> dict:
    key_of = jax.random.split(jax.random.key(seed), 26)
    return {
        "language": centred(key_of[0], (ITEMS, WORDS, D), 1.0, 6.0, ((0, 32),)),
        "images": centred(key_of[1], (IMAGES, REGIONS, D), 1.0, 6.0, ((0, 8),)),
        "counts": jax.vmap(lambda own: ragged(own, IMG_GRP, GROUP_ITEMS, MOST, 1))(jax.random.split(key_of[2], N_DP)).reshape((N_DP, IMG_GRP)).astype(jnp.int32),
        "language_cot": centred(key_of[3], (ITEMS, WORDS, D), 1.0, 6.0, ((0, 32),)),
        "vision_cot": centred(key_of[4], (ITEMS, REGIONS, D), 1.0, 6.0, ((0, 32),)),
        "attn_in_weight": draw_attn_in_weight(jax.random.fold_in(key_of[25], 71), 0),
        "attn_in_moment": centred(key_of[6], (3, D, 3, D), (100 * PARAMS) ** -0.5, 0.00015258789, ((1, 8), (3, 4)), jnp.float32),
        "attn_in_square": draw_attn_in_square(jax.random.fold_in(key_of[25], 71), 0),
        "attn_in_average": centred(key_of[8], (3, D, 3, D), (2 * D) ** -0.5, 0.15625, ((1, 8), (3, 4)), jnp.float32),
        "attn_out_weight": draw_attn_out_weight(jax.random.fold_in(key_of[25], 71), 0),
        "attn_out_moment": centred(key_of[10], (3, D, D), (100 * PARAMS) ** -0.5, 0.00015258789, ((1, 4), (2, 8)), jnp.float32),
        "attn_out_square": draw_attn_out_square(jax.random.fold_in(key_of[25], 71), 0),
        "attn_out_average": centred(key_of[12], (3, D, D), D ** -0.5, 0.21875, ((1, 4), (2, 8)), jnp.float32),
        "ffn_in_weight": draw_ffn_in_weight(jax.random.fold_in(key_of[25], 71), 0),
        "ffn_in_moment": centred(key_of[14], (2, D, FF), (100 * PARAMS) ** -0.5, 0.00015258789, ((1, 8), (2, 4)), jnp.float32),
        "ffn_in_square": draw_ffn_in_square(jax.random.fold_in(key_of[25], 71), 0),
        "ffn_in_average": centred(key_of[16], (2, D, FF), D ** -0.5, 0.21875, ((1, 8), (2, 4)), jnp.float32),
        "ffn_out_weight": draw_ffn_out_weight(jax.random.fold_in(key_of[25], 71), 0),
        "ffn_out_moment": centred(key_of[18], (2, FF, D), (100 * PARAMS) ** -0.5, 0.00015258789, ((1, 4), (2, 8)), jnp.float32),
        "ffn_out_square": draw_ffn_out_square(jax.random.fold_in(key_of[25], 71), 0),
        "ffn_out_average": centred(key_of[20], (2, FF, D), FF ** -0.5, 0.109375, ((1, 4), (2, 8)), jnp.float32),
        "norm_weight": draw_norm_weight(jax.random.fold_in(key_of[25], 71), 0),
        "norm_moment": centred(key_of[22], (2, 5, D), (5 * PARAMS) ** -0.5, 0.00061035156, (), jnp.float32),
        "norm_square": draw_norm_square(jax.random.fold_in(key_of[25], 71), 0),
        "norm_average": jnp.clip(1.0 + 0.1 * jax.random.normal(key_of[24], (2, 5, D), jnp.float32), 0.5, 1.5),
    }


NORM_EPS = 1e-05
CLIP_NORM = 1.0
BETA_FIRST = 0.9
BETA_SECOND = 0.999
ADAM_EPS = 1e-08
WEIGHT_DECAY = 0.01
MATRIX_RATE = 0.12
NORM_RATE = 0.8
AVERAGE_CEILING = 0.999
HIGHEST_PRECISION = lax.Precision.HIGHEST

@jax.custom_vjp
def low(v):
    return lax.optimization_barrier(v.astype(jnp.bfloat16)).astype(jnp.float32)

@jax.custom_vjp
def low_back(v):
    return v

def low_keep(v):
    return (low(v), None)

def low_pass(kept, grad):
    return (grad,)

def back_keep(v):
    return (v, None)

def back_low(kept, grad):
    return (low(grad),)
low.defvjp(low_keep, low_pass)
low_back.defvjp(back_keep, back_low)

def layer_norm(summed, gain, shift):
    centre = lax.optimization_barrier(jnp.mean(summed, axis=-1, keepdims=True))
    offset = summed - centre
    spread = lax.optimization_barrier(jnp.mean(offset * offset, axis=-1, keepdims=True))
    return offset * lax.rsqrt(spread + NORM_EPS) * gain + shift

def heads_view(row_block):
    return row_block.reshape(row_block.shape[0], row_block.shape[1], row_block.shape[2] // HEAD_DIM, HEAD_DIM)

def attend(queries, keyset, values):
    score_scale = 1.0 / math.sqrt(HEAD_DIM)
    raw_scores = low_back(jnp.einsum('jqhe,jkhe->jhqk', heads_view(queries), heads_view(keyset), precision=HIGHEST_PRECISION))
    scores = raw_scores * score_scale
    highest = lax.optimization_barrier(jnp.max(scores, axis=-1, keepdims=True))
    powered = jnp.exp(scores - highest)
    weights = low(powered / lax.optimization_barrier(jnp.sum(powered, axis=-1, keepdims=True)))
    context = jnp.einsum('jhqk,jkhe->jqhe', weights, heads_view(values), precision=HIGHEST_PRECISION)
    return low_back(low(context.reshape(queries.shape)))

def attention_sublayer(streams, pairs, weight_in, weight_out):
    group_width = D // N_MP
    totals = [jnp.zeros_like(streams[source]) for source, target in pairs]
    for head_part in range(N_MP):
        columns = slice(head_part * group_width, (head_part + 1) * group_width)
        rounded = [low_back(low(stream)) for stream in streams]
        triples = [[low_back(low(jnp.einsum('jld,de->jle', member, weight_in[:, kind_index, columns], precision=HIGHEST_PRECISION))) for kind_index in range(3)] for member in rounded]
        for number, (source, target) in enumerate(pairs):
            context = attend(triples[source][0], triples[target][1], triples[target][2])
            totals[number] = totals[number] + low(jnp.einsum('jle,ed->jld', context, weight_out[columns, :], precision=HIGHEST_PRECISION))
    return [low_back(branch_sum) for branch_sum in totals]

def feed_forward(stream, weight_up, weight_down):
    group_width = FF // N_MP
    branch_sum = jnp.zeros_like(stream)
    for head_part in range(N_MP):
        columns = slice(head_part * group_width, (head_part + 1) * group_width)
        rounded = low_back(low(stream))
        hidden = low_back(jnp.einsum('jld,df->jlf', rounded, weight_up[:, columns], precision=HIGHEST_PRECISION))
        active = low(jax.nn.gelu(hidden, approximate=False))
        branch_sum = branch_sum + low(jnp.einsum('jlf,fd->jld', active, weight_down[columns, :], precision=HIGHEST_PRECISION))
    return low_back(branch_sum)

def group_layer(weights, lang_rows, image_rows, selector):
    attend_in, attend_out, expand_in, expand_out, norm_table = weights
    vis_rows = jnp.einsum('ji,ird->jrd', selector, image_rows, precision=HIGHEST_PRECISION)
    lang_mix, vis_mix = attention_sublayer([lang_rows, vis_rows], [(0, 1), (1, 0)], attend_in[0], attend_out[0])
    lang_one = layer_norm(lang_rows + lang_mix, norm_table[0, 0], norm_table[1, 0])
    vis_one = layer_norm(vis_rows + vis_mix, norm_table[0, 0], norm_table[1, 0])
    lang_self = attention_sublayer([lang_one], [(0, 0)], attend_in[1], attend_out[1])[0]
    vis_self = attention_sublayer([vis_one], [(0, 0)], attend_in[2], attend_out[2])[0]
    lang_two = layer_norm(lang_one + lang_self, norm_table[0, 1], norm_table[1, 1])
    vis_two = layer_norm(vis_one + vis_self, norm_table[0, 2], norm_table[1, 2])
    lang_three = layer_norm(lang_two + feed_forward(lang_two, expand_in[0], expand_out[0]), norm_table[0, 3], norm_table[1, 3])
    vis_three = layer_norm(vis_two + feed_forward(vis_two, expand_in[1], expand_out[1]), norm_table[0, 4], norm_table[1, 4])
    return (lang_three, vis_three)

def item_selector(counts_row):
    bounds = jnp.cumsum(counts_row)
    positions = jnp.arange(GROUP_ITEMS, dtype=jnp.int32)
    item_image = lax.optimization_barrier(jnp.sum((bounds[None, :] <= positions[:, None]).astype(jnp.int32), axis=1))
    return (item_image[:, None] == jnp.arange(IMG_GRP, dtype=jnp.int32)[None, :]).astype(jnp.float32)

def adamw_step(gradient, moment, square, weight, average, rate, clip_scale):
    average_decay = min(AVERAGE_CEILING, (1.0 + STEP) / (10.0 + STEP))
    clipped = gradient * clip_scale
    moment_new = BETA_FIRST * moment + (1.0 - BETA_FIRST) * clipped
    square_new = BETA_SECOND * square + (1.0 - BETA_SECOND) * clipped * clipped
    corrected = moment_new / (1.0 - BETA_FIRST ** STEP)
    denominator = jnp.sqrt(square_new / (1.0 - BETA_SECOND ** STEP)) + ADAM_EPS
    weight_new = weight - rate * (corrected / denominator + WEIGHT_DECAY * weight)
    average_new = average_decay * average + (1.0 - average_decay) * weight_new
    return (clipped, moment_new, square_new, weight_new, average_new)

def reference(language, images, counts, language_cot, vision_cot, attn_in_weight, attn_in_moment, attn_in_square, attn_in_average, attn_out_weight, attn_out_moment, attn_out_square, attn_out_average, ffn_in_weight, ffn_in_moment, ffn_in_square, ffn_in_average, ffn_out_weight, ffn_out_moment, ffn_out_square, ffn_out_average, norm_weight, norm_moment, norm_square, norm_average):
    weights = (low(attn_in_weight), low(attn_out_weight), low(ffn_in_weight), low(ffn_out_weight), norm_weight)
    lang_groups = language.astype(jnp.float32).reshape(N_DP, GROUP_ITEMS, WORDS, D)
    image_groups = images.astype(jnp.float32).reshape(N_DP, IMG_GRP, REGIONS, D)
    lang_backs = language_cot.astype(jnp.float32).reshape(N_DP, GROUP_ITEMS, WORDS, D)
    vis_backs = vision_cot.astype(jnp.float32).reshape(N_DP, GROUP_ITEMS, REGIONS, D)

    def one_group(totals, inputs):
        lang_rows, image_rows, counts_row, lang_back, vis_back = inputs
        selector = item_selector(counts_row)

        def forward(layer_weights, lang_in, image_in):
            return group_layer(layer_weights, lang_in, image_in, selector)
        outputs, pullback = jax.vjp(forward, weights, lang_rows, image_rows)
        weight_grads, lang_grad, image_grad = pullback((lang_back, vis_back))
        totals = jax.tree.map(jnp.add, totals, weight_grads)
        return (totals, (outputs[0].astype(jnp.bfloat16), outputs[1].astype(jnp.bfloat16), lang_grad, image_grad))
    zero_grads = jax.tree.map(jnp.zeros_like, weights)
    totals, stacked = lax.scan(one_group, zero_grads, (lang_groups, image_groups, counts, lang_backs, vis_backs))
    squares = [jnp.sum(gradient * gradient) for gradient in totals]
    total_squares = functools.reduce(jnp.add, squares)
    grad_norm = jnp.sqrt(total_squares)
    clip_scale = CLIP_NORM / jnp.maximum(grad_norm, CLIP_NORM)
    attn_in_new = adamw_step(totals[0], attn_in_moment, attn_in_square, attn_in_weight, attn_in_average, MATRIX_RATE, clip_scale)
    attn_out_new = adamw_step(totals[1], attn_out_moment, attn_out_square, attn_out_weight, attn_out_average, MATRIX_RATE, clip_scale)
    ffn_in_new = adamw_step(totals[2], ffn_in_moment, ffn_in_square, ffn_in_weight, ffn_in_average, MATRIX_RATE, clip_scale)
    ffn_out_new = adamw_step(totals[3], ffn_out_moment, ffn_out_square, ffn_out_weight, ffn_out_average, MATRIX_RATE, clip_scale)
    norm_new = adamw_step(totals[4], norm_moment, norm_square, norm_weight, norm_average, NORM_RATE, clip_scale)
    return (stacked[0].reshape(ITEMS, WORDS, D), stacked[1].reshape(ITEMS, REGIONS, D), stacked[2].reshape(ITEMS, WORDS, D), stacked[3].reshape(IMAGES, REGIONS, D), attn_in_new[0], attn_in_new[1], attn_in_new[2], attn_in_new[3], attn_in_new[3].astype(jnp.bfloat16), attn_in_new[4], attn_out_new[0], attn_out_new[1], attn_out_new[2], attn_out_new[3], attn_out_new[3].astype(jnp.bfloat16), attn_out_new[4], ffn_in_new[0], ffn_in_new[1], ffn_in_new[2], ffn_in_new[3], ffn_in_new[3].astype(jnp.bfloat16), ffn_in_new[4], ffn_out_new[0], ffn_out_new[1], ffn_out_new[2], ffn_out_new[3], ffn_out_new[3].astype(jnp.bfloat16), ffn_out_new[4], norm_new[0], norm_new[1], norm_new[2], norm_new[3], norm_new[4], grad_norm)
```

```python
import functools
import math

import jax
import jax.numpy as jnp
from jax import lax
from jax.experimental import pallas as pl
from jax.experimental.pallas import tpu as pltpu
from jax.sharding import PartitionSpec as P

HEAD_DIM = 64
STEP = 10

NORM_EPS = 1e-05
CLIP_NORM = 1.0
BETA_FIRST = 0.9
BETA_SECOND = 0.999
ADAM_EPS = 1e-08
WEIGHT_DECAY = 0.01
MATRIX_RATE = 0.12
NORM_RATE = 0.8
AVERAGE_CEILING = 0.999
BF = jnp.bfloat16
F32 = jnp.float32
HIGHEST = lax.Precision.HIGHEST
SCALE = 1.0 / math.sqrt(HEAD_DIM)
VMEM_LIMIT = 56 * 1024 * 1024


def dot_nn(a, b):
    return lax.dot_general(a, b, (((1,), (0,)), ((), ())), preferred_element_type=F32)


def dot_nt(a, b):
    return lax.dot_general(a, b, (((1,), (1,)), ((), ())), preferred_element_type=F32)


def dot_tn(a, b):
    return lax.dot_general(a, b, (((0,), (0,)), ((), ())), preferred_element_type=F32)


def norm_forward(summed, gain, shift):
    centre = jnp.mean(summed, axis=-1, keepdims=True)
    offset = summed - centre
    spread = jnp.mean(offset * offset, axis=-1, keepdims=True)
    inverse = lax.rsqrt(spread + NORM_EPS)
    normed = offset * inverse
    return normed * gain + shift, normed, inverse


def norm_backward(upstream, gain, normed, inverse):
    scaled = upstream * gain
    first_mean = jnp.mean(scaled, axis=-1, keepdims=True)
    second_mean = jnp.mean(scaled * normed, axis=-1, keepdims=True)
    inward = inverse * (scaled - first_mean - normed * second_mean)
    gain_term = jnp.sum(upstream * normed, axis=0, keepdims=True)
    shift_term = jnp.sum(upstream, axis=0, keepdims=True)
    return inward, gain_term, shift_term


def head(block, kind, index, width):
    start = kind * width + index * HEAD_DIM
    return block[:, start : start + HEAD_DIM]


def attend(query, key, value, mask):
    scores = jnp.where(mask, dot_nt(query, key) * SCALE, -1e30)
    powered = jnp.exp(scores - jnp.max(scores, axis=-1, keepdims=True))
    probs = (powered * (1.0 / jnp.sum(powered, axis=-1, keepdims=True))).astype(BF)
    return probs, dot_nn(probs, value).astype(BF)


def attend_back(query, key, value, probs, grad_context):
    grad_probs = dot_nt(grad_context, value)
    grad_value = dot_tn(probs, grad_context).astype(BF)
    wide = probs.astype(F32)
    inner = jnp.sum(grad_probs * wide, axis=-1, keepdims=True)
    grad_scores = (wide * (grad_probs - inner) * SCALE).astype(BF)
    grad_query = dot_nn(grad_scores, key).astype(BF)
    grad_key = dot_tn(grad_scores, query).astype(BF)
    return grad_query, grad_key, grad_value


def load_weight(pieces, weight):
    row = 0
    for piece in pieces:
        for part in range(piece.shape[0]):
            block = piece[part, 0]
            weight[row : row + block.shape[0], :] = block
            row += block.shape[0]


def store_weight(value, pieces):
    row = 0
    for piece in pieces:
        for part in range(piece.shape[0]):
            rows = piece.shape[2]
            piece[part, 0] = value[row : row + rows, :].astype(piece.dtype)
            row += rows


def cross_forward_kernel(width, lang, vis, norm, lang_col, lang_row, vis_col, vis_row, *refs):
    pieces, refs = refs[:8], refs[8:]
    lang_one, lang_n, lang_r, vis_one, vis_n, vis_r = refs[:6]
    lang_qkv, vis_qkv, lang_ctx, vis_ctx, lang_p, vis_p = refs[6:12]
    weight, lang_acc, vis_acc = refs[12:]
    load_weight(pieces, weight)
    step = pl.program_id(0)

    @pl.when(step == 0)
    def _():
        lang_acc[...] = lang[...].astype(F32)
        vis_acc[...] = vis[...].astype(F32)

    full = weight[...]
    in_part, out_part = full[:, : 3 * width], full[:, 3 * width :]
    lang_triple = dot_nn(lang[...], in_part).astype(BF)
    vis_triple = dot_nn(vis[...], in_part).astype(BF)
    lang_qkv[0] = lang_triple
    vis_qkv[0] = vis_triple
    for source, target, probs_ref, ctx_ref, acc, mask in (
        (lang_triple, vis_triple, lang_p, lang_ctx, lang_acc, lang_col[...] == vis_row[...]),
        (vis_triple, lang_triple, vis_p, vis_ctx, vis_acc, vis_col[...] == lang_row[...]),
    ):
        contexts = []
        for index in range(width // HEAD_DIM):
            probs, context = attend(
                head(source, 0, index, width),
                head(target, 1, index, width),
                head(target, 2, index, width),
                mask,
            )
            probs_ref[0, index] = probs
            contexts.append(context)
        context = jnp.concatenate(contexts, axis=1)
        ctx_ref[0] = context
        acc[...] += dot_nt(context, out_part)

    @pl.when(step == pl.num_programs(0) - 1)
    def _():
        for acc, one, n_ref, r_ref in (
            (lang_acc, lang_one, lang_n, lang_r),
            (vis_acc, vis_one, vis_n, vis_r),
        ):
            out, normed, inverse = norm_forward(acc[...], norm[0:1, :], norm[1:2, :])
            one[...] = out.astype(BF)
            n_ref[...] = normed
            r_ref[...] = inverse


def self_forward_kernel(width, slot, rows, norm, col, row, *refs):
    pieces, refs = refs[:4], refs[4:]
    two, n_ref, r_ref, qkv, ctx, probs_ref, weight, acc = refs
    load_weight(pieces, weight)
    step = pl.program_id(0)

    @pl.when(step == 0)
    def _():
        acc[...] = rows[...].astype(F32)

    full = weight[...]
    in_part, out_part = full[:, : 3 * width], full[:, 3 * width :]
    triple = dot_nn(rows[...], in_part).astype(BF)
    qkv[0] = triple
    mask = col[...] == row[...]
    slots = []
    for place in range(rows.shape[0] // slot):
        part = triple[place * slot : (place + 1) * slot]
        contexts = []
        for index in range(width // HEAD_DIM):
            probs, context = attend(
                head(part, 0, index, width),
                head(part, 1, index, width),
                head(part, 2, index, width),
                mask,
            )
            probs_ref[0, place, index] = probs
            contexts.append(context)
        slots.append(jnp.concatenate(contexts, axis=1))
    context = jnp.concatenate(slots, axis=0)
    ctx[0] = context
    acc[...] += dot_nt(context, out_part)

    @pl.when(step == pl.num_programs(0) - 1)
    def _():
        out, normed, inverse = norm_forward(acc[...], norm[0:1, :], norm[1:2, :])
        two[...] = out.astype(BF)
        n_ref[...] = normed
        r_ref[...] = inverse


def feed_forward_kernel(rows, normed_two, cot, norm, *refs):
    in_pieces, out_pieces, refs = refs[:4], refs[4:8], refs[8:]
    three, inward_ref, gain_ref, shift_ref, active_ref, slope_ref = refs[:6]
    weight_in, weight_out, acc = refs[6:]
    load_weight(in_pieces, weight_in)
    load_weight(out_pieces, weight_out)
    step = pl.program_id(0)

    @pl.when(step == 0)
    def _():
        acc[...] = normed_two[...] * norm[0:1, :] + norm[1:2, :]

    hidden = dot_nn(rows[...], weight_in[...])
    normal = 0.5 * (1.0 + lax.erf(hidden * 0.7071067811865476))
    active = (hidden * normal).astype(BF)
    slope = normal + hidden * jnp.exp(-0.5 * hidden * hidden) * 0.3989422804014327
    active_ref[0] = active
    slope_ref[0] = slope.astype(slope_ref.dtype)
    acc[...] += dot_nt(active, weight_out[...])

    @pl.when(step == pl.num_programs(0) - 1)
    def _():
        gain = norm[2:3, :]
        out, normed, inverse = norm_forward(acc[...], gain, norm[3:4, :])
        three[...] = out.astype(BF)
        inward, gain_term, shift_term = norm_backward(cot[...].astype(F32), gain, normed, inverse)
        inward_ref[...] = inward
        gain_ref[...] = gain_term
        shift_ref[...] = shift_term


def feed_backward_kernel(inward, rows, active, slope, normed, inverse, norm, *refs):
    in_pieces, out_pieces, refs = refs[:4], refs[4:8], refs[8:]
    grad_in, grad_out, refs = refs[:4], refs[4:8], refs[8:]
    down_ref, gain_ref, shift_ref, weight_in, weight_out, acc, branch = refs
    load_weight(in_pieces, weight_in)
    load_weight(out_pieces, weight_out)
    step = pl.program_id(0)

    @pl.when(step == 0)
    def _():
        acc[...] = inward[...]
        branch[...] = inward[...].astype(BF)

    store_weight(dot_tn(branch[...], active[0]), grad_out)
    grad_active = dot_nn(branch[...], weight_out[...])
    grad_hidden = (grad_active * slope[0].astype(F32)).astype(BF)
    store_weight(dot_tn(rows[...], grad_hidden), grad_in)
    acc[...] += dot_nt(grad_hidden, weight_in[...])

    @pl.when(step == pl.num_programs(0) - 1)
    def _():
        down, gain_term, shift_term = norm_backward(
            acc[...], norm[0:1, :], normed[...], inverse[...]
        )
        down_ref[...] = down
        gain_ref[...] = gain_term
        shift_ref[...] = shift_term


def self_backward_kernel(width, slot, inward, rows, qkv, ctx, probs, *refs):
    pieces, grads, refs = refs[:4], refs[4:8], refs[8:]
    down_ref, weight, acc, branch = refs
    load_weight(pieces, weight)
    step = pl.program_id(0)

    @pl.when(step == 0)
    def _():
        acc[...] = inward[...]
        branch[...] = inward[...].astype(BF)

    full = weight[...]
    in_part, out_part = full[:, : 3 * width], full[:, 3 * width :]
    grad_context = dot_nn(branch[...], out_part).astype(BF)
    slots = []
    for place in range(rows.shape[0] // slot):
        span = slice(place * slot, (place + 1) * slot)
        part, grad_part = qkv[0, span], grad_context[span]
        found = [
            attend_back(
                head(part, 0, index, width),
                head(part, 1, index, width),
                head(part, 2, index, width),
                probs[0, place, index],
                head(grad_part, 0, index, width),
            )
            for index in range(width // HEAD_DIM)
        ]
        slots.append(
            jnp.concatenate([entry[kind] for kind in range(3) for entry in found], axis=1)
        )
    grad_triple = jnp.concatenate(slots, axis=0)
    store_weight(
        jnp.concatenate(
            [dot_tn(rows[...], grad_triple).astype(BF), dot_tn(branch[...], ctx[0]).astype(BF)],
            axis=1,
        ),
        grads,
    )
    acc[...] += dot_nt(grad_triple, in_part)

    @pl.when(step == pl.num_programs(0) - 1)
    def _():
        down_ref[...] = acc[...]


def cross_backward_kernel(width, lang_up, vis_up, lang, vis, lang_n, lang_r, vis_n, vis_r, norm, *refs):
    lang_qkv, vis_qkv, lang_ctx, vis_ctx, lang_p, vis_p = refs[:6]
    pieces, grads, refs = refs[6:14], refs[14:22], refs[22:]
    lang_out, vis_out, gain_ref, shift_ref = refs[:4]
    weight, lang_acc, vis_acc, lang_branch, vis_branch = refs[4:]
    load_weight(pieces, weight)
    step = pl.program_id(0)

    @pl.when(step == 0)
    def _():
        gain_total, shift_total = 0.0, 0.0
        for up, n_ref, r_ref, acc, branch in (
            (lang_up, lang_n, lang_r, lang_acc, lang_branch),
            (vis_up, vis_n, vis_r, vis_acc, vis_branch),
        ):
            inward, gain_term, shift_term = norm_backward(
                up[...], norm[0:1, :], n_ref[...], r_ref[...]
            )
            acc[...] = inward
            branch[...] = inward.astype(BF)
            gain_total += gain_term
            shift_total += shift_term
        gain_ref[...] = gain_total
        shift_ref[...] = shift_total

    full = weight[...]
    in_part, out_part = full[:, : 3 * width], full[:, 3 * width :]
    lang_gc = dot_nn(lang_branch[...], out_part).astype(BF)
    vis_gc = dot_nn(vis_branch[...], out_part).astype(BF)
    lang_triple, vis_triple = lang_qkv[0], vis_qkv[0]
    found = []
    for source, target, probs, grad_context in (
        (lang_triple, vis_triple, lang_p, lang_gc),
        (vis_triple, lang_triple, vis_p, vis_gc),
    ):
        found.append(
            [
                attend_back(
                    head(source, 0, index, width),
                    head(target, 1, index, width),
                    head(target, 2, index, width),
                    probs[0, index],
                    head(grad_context, 0, index, width),
                )
                for index in range(width // HEAD_DIM)
            ]
        )
    lang_grad = jnp.concatenate(
        [e[0] for e in found[0]] + [e[1] for e in found[1]] + [e[2] for e in found[1]], axis=1
    )
    vis_grad = jnp.concatenate(
        [e[0] for e in found[1]] + [e[1] for e in found[0]] + [e[2] for e in found[0]], axis=1
    )
    in_grad = dot_tn(lang[...], lang_grad) + dot_tn(vis[...], vis_grad)
    out_grad = dot_tn(lang_branch[...], lang_ctx[0]) + dot_tn(vis_branch[...], vis_ctx[0])
    store_weight(jnp.concatenate([in_grad.astype(BF), out_grad.astype(BF)], axis=1), grads)
    lang_acc[...] += dot_nt(lang_grad, in_part)
    vis_acc[...] += dot_nt(vis_grad, in_part)

    @pl.when(step == pl.num_programs(0) - 1)
    def _():
        lang_out[...] = lang_acc[...].astype(lang_out.dtype)
        vis_out[...] = vis_acc[...].astype(vis_out.dtype)


def whole(shape):
    return pl.BlockSpec(shape, lambda m: (0,) * len(shape))


def per_step(shape):
    rest = (0,) * (len(shape) - 1)
    return pl.BlockSpec((1,) + tuple(shape[1:]), lambda m: (m,) + rest)


def piece_spec(shape):
    return pl.BlockSpec((shape[0], 1) + tuple(shape[2:]), lambda m: (0, m, 0, 0))


def call(kernel, steps, ins, outs, scratch, name, flops):
    spec = {"whole": whole, "step": per_step, "piece": piece_spec}
    moved = sum(a.size * a.dtype.itemsize for _, a in ins)
    moved += sum(math.prod(s) * jnp.dtype(t).itemsize for _, s, t in outs)
    return pl.pallas_call(
        kernel,
        grid=(steps,),
        in_specs=[spec[kind](a.shape) for kind, a in ins],
        out_specs=[spec[kind](s) for kind, s, _ in outs],
        out_shape=[jax.ShapeDtypeStruct(s, t) for _, s, t in outs],
        scratch_shapes=[pltpu.VMEM(s, t) for s, t in scratch],
        compiler_params=pltpu.CompilerParams(
            vmem_limit_bytes=VMEM_LIMIT, dimension_semantics=("arbitrary",)
        ),
        cost_estimate=pl.CostEstimate(flops=flops, bytes_accessed=moved, transcendentals=0),
        name=name,
    )(*[a for _, a in ins])


def swap_dp(value, bit):
    count = lax.axis_size("dp")
    return lax.ppermute(value, "dp", [(i, i ^ (1 << bit)) for i in range(count)])


def swap_mp(value, mask):
    count = lax.axis_size("mp")
    return lax.ppermute(value, "mp", [(i, i ^ mask) for i in range(count)])


def extra_bits():
    return range(3, int(math.log2(lax.axis_size("dp"))))


def gather_home(shard):
    current = jnp.stack([shard] + [swap_mp(shard, j) for j in range(1, lax.axis_size("mp"))])
    for bit in extra_bits():
        current = jnp.concatenate([current, swap_dp(current, bit)], axis=1)
    found = {(0, 0, 0): current[None]}
    for place, bit in ((0, 2), (1, 1), (2, 0)):
        for key in list(found):
            new = list(key)
            new[place] = 1
            found[tuple(new)] = swap_dp(found[key], bit)
    return [found[(hi, mid, lo)] for hi in (0, 1) for lo in (0, 1) for mid in (0, 1)]


def gather_stream(own, other):
    pair = jnp.stack([own, swap_dp(other, 1)])
    current = jnp.stack(
        [pair] + [swap_mp(pair, j) for j in range(1, lax.axis_size("mp"))], axis=1
    )
    for bit in extra_bits():
        current = jnp.concatenate([current, swap_dp(current, bit)], axis=2)
    found = {(0, 0): current}
    for place, bit in ((0, 2), (1, 0)):
        for key in list(found):
            new = list(key)
            new[place] = 1
            found[tuple(new)] = swap_dp(found[key], bit)
    return [found[(hi, lo)] for hi in (0, 1) for lo in (0, 1)]


def added(mine, theirs):
    return (mine.astype(F32) + theirs.astype(F32)).astype(BF)


def scatter_rows(current, axis):
    for bit in reversed(extra_bits()):
        low, high = jnp.split(current, 2, axis=axis)
        current = added(low, swap_dp(high, bit))
    return current


def scatter_home(grads):
    found = {}
    for index, grad in enumerate(grads):
        found[(index >> 2, index & 1, (index >> 1) & 1)] = grad[0]
    for place, bit in ((2, 0), (1, 1), (0, 2)):
        for key in [k for k in found if k[place] == 0]:
            far = list(key)
            far[place] = 1
            found[key] = added(found[key], swap_dp(found.pop(tuple(far)), bit))
    current = scatter_rows(found[(0, 0, 0)], 1)
    total = current[0].astype(F32)
    for j in range(1, current.shape[0]):
        total += swap_mp(current[j], j).astype(F32)
    return total


def scatter_stream(grads):
    found = {(index >> 1, index & 1): grad for index, grad in enumerate(grads)}
    for place, bit in ((1, 0), (0, 2)):
        for key in [k for k in found if k[place] == 0]:
            far = list(key)
            far[place] = 1
            found[key] = added(found[key], swap_dp(found.pop(tuple(far)), bit))
    current = scatter_rows(found[(0, 0)], 2)
    total = current[:, 0].astype(F32)
    for j in range(1, current.shape[1]):
        total += swap_mp(current[:, j], j).astype(F32)
    return total[0], swap_dp(total[1].astype(BF), 1).astype(F32)


def adamw_step(gradient, moment, square, weight, average, rate, clip_scale):
    average_decay = min(AVERAGE_CEILING, (1.0 + STEP) / (10.0 + STEP))
    clipped = gradient * clip_scale
    moment_new = BETA_FIRST * moment + (1.0 - BETA_FIRST) * clipped
    square_new = BETA_SECOND * square + (1.0 - BETA_SECOND) * clipped * clipped
    corrected = moment_new / (1.0 - BETA_FIRST**STEP)
    denominator = jnp.sqrt(square_new / (1.0 - BETA_SECOND**STEP)) + ADAM_EPS
    weight_new = weight - rate * (corrected / denominator + WEIGHT_DECAY * weight)
    average_new = average_decay * average + (1.0 - average_decay) * weight_new
    return (clipped, moment_new, square_new, weight_new, average_new)


def pad_rows(block, rows):
    return jnp.pad(block, ((0, rows - block.shape[0]), (0, 0)))


def local(
    language,
    images,
    counts,
    language_cot,
    vision_cot,
    attn_in_weight,
    attn_in_moment,
    attn_in_square,
    attn_in_average,
    attn_out_weight,
    attn_out_moment,
    attn_out_square,
    attn_out_average,
    ffn_in_weight,
    ffn_in_moment,
    ffn_in_square,
    ffn_in_average,
    ffn_out_weight,
    ffn_out_moment,
    ffn_out_square,
    ffn_out_average,
    norm_weight,
    norm_moment,
    norm_square,
    norm_average,
):
    n_dp, n_mp = lax.axis_size("dp"), lax.axis_size("mp")
    me = lax.axis_index("dp")
    stream = (me >> 1) & 1
    is_vis = stream == 1
    own_items, words, dim = language.shape
    regions = images.shape[1]
    lang_rows, vis_rows = own_items * words, own_items * regions
    lang_pad, slot = -(-lang_rows // 16) * 16, -(-vis_rows // 16) * 16
    total = 2 * slot
    shard_rows = attn_in_weight.shape[1]
    width = attn_in_weight.shape[3]
    units = ffn_in_weight.shape[2]
    heads = width // HEAD_DIM

    attn_shards = [
        jnp.concatenate(
            [attn_in_weight[b].reshape(shard_rows, 3 * width), attn_out_weight[b].T], axis=1
        ).astype(BF)
        for b in range(3)
    ]
    up_shards = [ffn_in_weight[s].astype(BF) for s in range(2)]
    down_shards = [ffn_out_weight[s].T.astype(BF) for s in range(2)]

    def mine_first(pair):
        return jnp.where(is_vis, pair[1], pair[0]), jnp.where(is_vis, pair[0], pair[1])

    cross_w = gather_home(attn_shards[0])
    self_w = gather_stream(*mine_first(attn_shards[1:]))
    up_w = gather_stream(*mine_first(up_shards))
    down_w = gather_stream(*mine_first(down_shards))

    place = jnp.arange(dim, dtype=jnp.int32)
    block = place // shard_rows
    sub, eighth = block % (n_dp // 8), block // (n_dp // 8)
    relative = 8 * sub + 4 * (eighth >> 2) + ((eighth >> 1) & 1) + 2 * (eighth & 1)
    origin = (relative ^ me) * shard_rows + place % shard_rows
    order = (place[:, None] == origin[None, :]).astype(BF)

    def to_order(value):
        return lax.dot_general(
            value, order, (((1,), (0,)), ((), ())), preferred_element_type=F32
        ).astype(BF)

    def from_order(value, precision=None):
        return lax.dot_general(
            value, order, (((1,), (1,)), ((), ())), preferred_element_type=F32, precision=precision
        )

    def flip(value):
        parts = value.reshape(value.shape[0], 4, 2, dim // 8)
        return parts[:, :, ::-1, :].reshape(value.shape)

    norm_ordered = lax.dot_general(
        norm_weight.reshape(-1, dim),
        order.astype(F32),
        (((1,), (0,)), ((), ())),
        precision=HIGHEST,
        preferred_element_type=F32,
    ).reshape(norm_weight.shape)
    norm_cross = norm_ordered[:, 0]
    norm_self = jnp.where(is_vis, norm_ordered[:, 2], norm_ordered[:, 1])
    norm_feed = jnp.where(is_vis, norm_ordered[:, 4], norm_ordered[:, 3])

    first_item = lax.axis_index("mp") * own_items
    bounds = jnp.cumsum(counts[0])
    positions = first_item + jnp.arange(own_items, dtype=jnp.int32)
    item_image = jnp.sum((bounds[None, :] <= positions[:, None]).astype(jnp.int32), axis=1)
    region = jnp.arange(regions, dtype=jnp.int32)
    row_source = pad_rows((item_image[:, None] * regions + region[None, :]).reshape(-1, 1) + 1, slot)
    picker = (
        row_source == 1 + jnp.arange(images.shape[0] * regions, dtype=jnp.int32)[None, :]
    ).astype(BF)
    lang = to_order(pad_rows(language.reshape(lang_rows, dim), lang_pad))
    image_rows = to_order(images.reshape(-1, dim))
    vis = dot_nn(picker, image_rows).astype(BF)

    lang_cot = pad_rows(language_cot.reshape(lang_rows, dim), slot)
    vis_cot = pad_rows(vision_cot.reshape(vis_rows, dim), slot)
    cot_own, cot_other = mine_first((lang_cot, vis_cot))
    cot = to_order(jnp.concatenate([cot_own, swap_dp(cot_other, 1)], axis=0))

    lang_ids = jnp.arange(lang_pad, dtype=jnp.int32) // words
    vis_ids = jnp.arange(slot, dtype=jnp.int32) // regions
    slot_ids = jnp.where(is_vis, vis_ids, jnp.arange(slot, dtype=jnp.int32) // words)

    pieces = lambda arrays: [("piece", a) for a in arrays]
    ins = [("whole", a) for a in (lang, vis, norm_cross)]
    ins += [("whole", a) for a in (lang_ids[:, None], lang_ids[None, :], vis_ids[:, None], vis_ids[None, :])]
    outs = []
    for rows in (lang_pad, slot):
        outs += [
            ("whole", (rows, dim), BF),
            ("whole", (rows, dim), F32),
            ("whole", (rows, 1), F32),
        ]
    outs += [("step", (n_mp, rows, 3 * width), BF) for rows in (lang_pad, slot)]
    outs += [("step", (n_mp, rows, width), BF) for rows in (lang_pad, slot)]
    outs += [
        ("step", (n_mp, heads, lang_pad, slot), BF),
        ("step", (n_mp, heads, slot, lang_pad), BF),
    ]
    both = lang_pad + slot
    found = call(
        functools.partial(cross_forward_kernel, width),
        n_mp,
        ins + pieces(cross_w),
        outs,
        [((dim, 4 * width), BF), ((lang_pad, dim), F32), ((slot, dim), F32)],
        "cross_forward",
        2 * both * dim * 4 * width * n_mp,
    )
    lang_one, lang_n, lang_r, vis_one, vis_n, vis_r = found[:6]
    cross_saved = found[6:]

    own_one, other_one = mine_first((pad_rows(lang_one, slot), vis_one))
    rows_one = jnp.concatenate([own_one, flip(swap_dp(other_one, 1))], axis=0)
    rows_two, normed_two, inverse_two, self_qkv, self_ctx, self_probs = call(
        functools.partial(self_forward_kernel, width, slot),
        n_mp,
        [("whole", a) for a in (rows_one, norm_self, slot_ids[:, None], slot_ids[None, :])]
        + pieces(self_w),
        [
            ("whole", (total, dim), BF),
            ("whole", (total, dim), F32),
            ("whole", (total, 1), F32),
            ("step", (n_mp, total, 3 * width), BF),
            ("step", (n_mp, total, width), BF),
            ("step", (n_mp, 2, heads, slot, slot), BF),
        ],
        [((dim, 4 * width), BF), ((total, dim), F32)],
        "self_forward",
        2 * total * dim * 4 * width * n_mp,
    )
    norm_pair = jnp.concatenate([norm_self, norm_feed], axis=0)
    rows_three, inward, feed_gain, feed_shift, active, slope = call(
        feed_forward_kernel,
        n_mp,
        [("whole", a) for a in (rows_two, normed_two, cot, norm_pair)]
        + pieces(up_w)
        + pieces(down_w),
        [
            ("whole", (total, dim), BF),
            ("whole", (total, dim), F32),
            ("whole", (1, dim), F32),
            ("whole", (1, dim), F32),
            ("step", (n_mp, total, units), BF),
            ("step", (n_mp, total, units), BF),
        ],
        [((dim, units), BF), ((dim, units), BF), ((total, dim), F32)],
        "feed_forward",
        4 * total * dim * units * n_mp,
    )

    final = from_order(rows_three).astype(BF)
    final_other = swap_dp(final[slot:], 1)
    language_out = jnp.where(is_vis, final_other[:lang_rows], final[:lang_rows])
    vision_out = jnp.where(is_vis, final[:vis_rows], final_other[:vis_rows])

    stream_grad = [("piece", (2, n_mp, dim // 8, units), BF)] * 4
    found = call(
        feed_backward_kernel,
        n_mp,
        [("whole", inward), ("whole", rows_two), ("step", active), ("step", slope)]
        + [("whole", a) for a in (normed_two, inverse_two, norm_self)]
        + pieces(up_w)
        + pieces(down_w),
        stream_grad
        + stream_grad
        + [("whole", (total, dim), F32), ("whole", (1, dim), F32), ("whole", (1, dim), F32)],
        [
            ((dim, units), BF),
            ((dim, units), BF),
            ((total, dim), F32),
            ((total, dim), BF),
        ],
        "feed_backward",
        8 * total * dim * units * n_mp,
    )
    up_grads = scatter_stream(found[:4])
    down_grads = scatter_stream(found[4:8])
    inward, self_gain, self_shift = found[8:]
    found = call(
        functools.partial(self_backward_kernel, width, slot),
        n_mp,
        [("whole", inward), ("whole", rows_one)]
        + [("step", a) for a in (self_qkv, self_ctx, self_probs)]
        + pieces(self_w),
        [("piece", (2, n_mp, dim // 8, 4 * width), BF)] * 4 + [("whole", (total, dim), F32)],
        [((dim, 4 * width), BF), ((total, dim), F32), ((total, dim), BF)],
        "self_backward",
        4 * total * dim * 4 * width * n_mp,
    )
    self_grads = scatter_stream(found[:4])
    back = found[4]
    back_other = swap_dp(flip(back[slot:].astype(BF)), 1).astype(F32)
    lang_up = jnp.where(is_vis, back_other[:lang_pad], back[:lang_pad])
    vis_up = jnp.where(is_vis, back[:slot], back_other)
    found = call(
        functools.partial(cross_backward_kernel, width),
        n_mp,
        [("whole", a) for a in (lang_up, vis_up, lang, vis, lang_n, lang_r, vis_n, vis_r, norm_cross)]
        + [("step", a) for a in cross_saved]
        + pieces(cross_w),
        [("piece", (1, n_mp, dim // 8, 4 * width), BF)] * 8
        + [
            ("whole", (lang_pad, dim), BF),
            ("whole", (slot, dim), BF),
            ("whole", (1, dim), F32),
            ("whole", (1, dim), F32),
        ],
        [
            ((dim, 4 * width), BF),
            ((lang_pad, dim), F32),
            ((slot, dim), F32),
            ((lang_pad, dim), BF),
            ((slot, dim), BF),
        ],
        "cross_backward",
        4 * both * dim * 4 * width * n_mp,
    )
    cross_grad = scatter_home(found[:8])
    lang_back, vis_back, cross_gain, cross_shift = found[8:]

    language_grad = from_order(lang_back[:lang_rows]).reshape(language.shape)
    image_term = lax.dot_general(
        picker, vis_back, (((0,), (0,)), ((), ())), preferred_element_type=F32
    ).astype(BF)
    image_term = from_order(image_term).astype(BF)
    image_grad = lax.psum(image_term, "mp").astype(F32).reshape(images.shape)

    here = (jnp.arange(2, dtype=jnp.int32) == stream).astype(F32)[None, :, None]
    norm_partial = jnp.concatenate(
        [
            jnp.stack([cross_gain, cross_shift]),
            here * jnp.stack([self_gain, self_shift]),
            here * jnp.stack([feed_gain, feed_shift]),
        ],
        axis=1,
    )
    norm_partial = from_order(norm_partial.reshape(-1, dim).astype(F32), HIGHEST)
    norm_total = lax.psum(norm_partial.reshape(norm_weight.shape), ("dp", "mp"))

    def by_stream(pair):
        return [jnp.where(is_vis, pair[1], pair[0]), jnp.where(is_vis, pair[0], pair[1])]

    attn_total = [cross_grad] + by_stream(self_grads)
    up_total, down_total = by_stream(up_grads), by_stream(down_grads)
    local_squares = sum(jnp.sum(g * g) for g in attn_total + up_total + down_total)
    total_squares = lax.psum(local_squares, ("dp", "mp")) + jnp.sum(norm_total * norm_total)
    grad_norm = jnp.sqrt(total_squares)
    clip_scale = CLIP_NORM / jnp.maximum(grad_norm, CLIP_NORM)

    shards = (
        jnp.stack([g[:, : 3 * width].reshape(shard_rows, 3, width) for g in attn_total]),
        jnp.stack([g[:, 3 * width :].T for g in attn_total]),
        jnp.stack(up_total),
        jnp.stack([g.T for g in down_total]),
    )
    states = (
        (attn_in_moment, attn_in_square, attn_in_weight, attn_in_average),
        (attn_out_moment, attn_out_square, attn_out_weight, attn_out_average),
        (ffn_in_moment, ffn_in_square, ffn_in_weight, ffn_in_average),
        (ffn_out_moment, ffn_out_square, ffn_out_weight, ffn_out_average),
    )
    results = [
        language_out.reshape(language.shape),
        vision_out.reshape(vision_cot.shape),
        language_grad,
        image_grad,
    ]
    for shard, state in zip(shards, states):
        new = adamw_step(shard, *state, MATRIX_RATE, clip_scale)
        results += [new[0], new[1], new[2], new[3], new[3].astype(BF), new[4]]
    results += adamw_step(
        norm_total, norm_moment, norm_square, norm_weight, norm_average, NORM_RATE, clip_scale
    )
    return tuple(results) + (grad_norm,)


def solution(mesh):
    rows = P(("dp", "mp"), None, None)
    attn_in, attn_out = P(None, "dp", None, "mp"), P(None, "mp", "dp")
    ffn_in, ffn_out = P(None, "dp", "mp"), P(None, "mp", "dp")
    in_specs = (rows, P("dp", None, None), P("dp", None), rows, rows)
    in_specs += (attn_in,) * 4 + (attn_out,) * 4 + (ffn_in,) * 4 + (ffn_out,) * 4 + (P(),) * 4
    out_specs = (rows, rows, rows, P("dp", None, None))
    out_specs += (attn_in,) * 6 + (attn_out,) * 6 + (ffn_in,) * 6 + (ffn_out,) * 6 + (P(),) * 6
    return jax.shard_map(local, mesh=mesh, in_specs=in_specs, out_specs=out_specs, check_vma=False)
```

```python
import functools
import math

import jax
import jax.numpy as jnp
from jax import lax
from jax.experimental import pallas as pl
from jax.experimental.pallas import tpu as pltpu
from jax.sharding import PartitionSpec as P

HEAD_DIM = 64
STEP = 10

NORM_EPS = 1e-05
CLIP_NORM = 1.0
BETA_FIRST = 0.9
BETA_SECOND = 0.999
ADAM_EPS = 1e-08
WEIGHT_DECAY = 0.01
MATRIX_RATE = 0.12
NORM_RATE = 0.8
AVERAGE_CEILING = 0.999
BF = jnp.bfloat16
F32 = jnp.float32
HIGHEST = lax.Precision.HIGHEST
SCALE = 1.0 / math.sqrt(HEAD_DIM)
VMEM_LIMIT = 56 * 1024 * 1024
GROUP = 3


def dot_nn(a, b):
    return lax.dot_general(a, b, (((1,), (0,)), ((), ())), preferred_element_type=F32)


def dot_nt(a, b):
    return lax.dot_general(a, b, (((1,), (1,)), ((), ())), preferred_element_type=F32)


def dot_tn(a, b):
    return lax.dot_general(a, b, (((0,), (0,)), ((), ())), preferred_element_type=F32)


def norm_forward(summed, gain, shift):
    centre = jnp.mean(summed, axis=-1, keepdims=True)
    offset = summed - centre
    spread = jnp.mean(offset * offset, axis=-1, keepdims=True)
    inverse = lax.rsqrt(spread + NORM_EPS)
    normed = offset * inverse
    return normed * gain + shift, normed, inverse


def norm_backward(upstream, gain, normed, inverse):
    scaled = upstream * gain
    first_mean = jnp.mean(scaled, axis=-1, keepdims=True)
    second_mean = jnp.mean(scaled * normed, axis=-1, keepdims=True)
    inward = inverse * (scaled - first_mean - normed * second_mean)
    gain_term = jnp.sum(upstream * normed, axis=0, keepdims=True)
    shift_term = jnp.sum(upstream, axis=0, keepdims=True)
    return inward, gain_term, shift_term


def cut(block, blocks):
    rows = block.shape[0] // blocks
    return [block[i * rows : (i + 1) * rows] for i in range(blocks)]


def stack_rows(parts):
    return jnp.concatenate(parts, axis=0)


def thirds(triple, width):
    return [triple[:, i * width : (i + 1) * width] for i in range(triple.shape[1] // width)]


def lane_head(block):
    return lax.broadcasted_iota(jnp.int32, block.shape, 1) // HEAD_DIM


def spread(block):
    lanes = lane_head(block)
    zero = jnp.zeros_like(block)
    heads = block.shape[1] // HEAD_DIM
    return stack_rows([jnp.where(lanes == h, block, zero) for h in range(heads)])


def gathered(block):
    parts = cut(block, block.shape[1] // HEAD_DIM)
    lanes = lane_head(parts[0])
    out = parts[0]
    for h in range(1, len(parts)):
        out = jnp.where(lanes == h, parts[h], out)
    return out


def attend(query, key, value, mask, blocks):
    pairs = zip(cut(query, blocks), cut(key, blocks))
    scores = stack_rows([jnp.where(mask, dot_nt(spread(q), k) * SCALE, -1e30) for q, k in pairs])
    powered = jnp.exp(scores - jnp.max(scores, axis=-1, keepdims=True))
    probs = (powered * (1.0 / jnp.sum(powered, axis=-1, keepdims=True))).astype(BF)
    mixed = [gathered(dot_nn(p, v)) for p, v in zip(cut(probs, blocks), cut(value, blocks))]
    return probs, stack_rows(mixed).astype(BF)


def attend_back(query, key, value, probs, grad_context, blocks):
    queries, keys, values = cut(query, blocks), cut(key, blocks), cut(value, blocks)
    contexts, weights = [spread(g) for g in cut(grad_context, blocks)], cut(probs, blocks)
    grad_probs = stack_rows([dot_nt(g, v) for g, v in zip(contexts, values)])
    grad_value = stack_rows([dot_tn(p, g) for p, g in zip(weights, contexts)]).astype(BF)
    wide = probs.astype(F32)
    inner = jnp.sum(grad_probs * wide, axis=-1, keepdims=True)
    grad_scores = cut((wide * (grad_probs - inner) * SCALE).astype(BF), blocks)
    grad_query = stack_rows([gathered(dot_nn(s, k)) for s, k in zip(grad_scores, keys)])
    grad_key = stack_rows([dot_tn(s, spread(q)) for s, q in zip(grad_scores, queries)])
    return grad_query.astype(BF), grad_key.astype(BF), grad_value


def load_weight(pieces, weight, column=0):
    row = 0
    for piece in pieces:
        for part in range(piece.shape[1]):
            rows, columns = piece.shape[2:]
            weight[row : row + rows, column : column + columns] = piece[0, part]
            row += rows


def store_weight(value, pieces):
    row = 0
    for piece in pieces:
        for part in range(piece.shape[1]):
            rows = piece.shape[2]
            piece[0, part] = value[row : row + rows, :].astype(piece.dtype)
            row += rows


def cross_forward_kernel(width, blocks, lang, vis, norm, lang_col, lang_row, vis_col, vis_row, *refs):
    first, second, refs = refs[:8], refs[8:16], refs[16:]
    lang_one, lang_n, lang_r, vis_one, vis_n, vis_r = refs[:6]
    lang_qkv, vis_qkv, lang_ctx, vis_ctx, lang_p, vis_p = refs[6:12]
    weight, lang_acc, vis_acc = refs[12:]
    load_weight(first, weight)
    load_weight(second, weight, first[0].shape[3])
    step = pl.program_id(0)

    @pl.when(step == 0)
    def _():
        lang_acc[...] = lang[...].astype(F32)
        vis_acc[...] = vis[...].astype(F32)

    full = weight[...]
    in_part, out_part = full[:, : 3 * width], full[:, 3 * width :]
    lang_triple = dot_nn(lang[...], in_part).astype(BF)
    vis_triple = dot_nn(vis[...], in_part).astype(BF)
    lang_qkv[0] = lang_triple
    vis_qkv[0] = vis_triple
    lang_query, lang_key, lang_value = thirds(lang_triple, width)
    vis_query, vis_key, vis_value = thirds(vis_triple, width)
    for query, key, value, probs_ref, ctx_ref, acc, mask in (
        (lang_query, vis_key, vis_value, lang_p, lang_ctx, lang_acc, lang_col[...] == vis_row[...]),
        (vis_query, lang_key, lang_value, vis_p, vis_ctx, vis_acc, vis_col[...] == lang_row[...]),
    ):
        probs, context = attend(query, key, value, mask, blocks)
        probs_ref[0] = probs
        ctx_ref[0] = context
        acc[...] += dot_nt(context, out_part)

    @pl.when(step == pl.num_programs(0) - 1)
    def _():
        for acc, one, n_ref, r_ref in (
            (lang_acc, lang_one, lang_n, lang_r),
            (vis_acc, vis_one, vis_n, vis_r),
        ):
            out, normed, inverse = norm_forward(acc[...], norm[0:1, :], norm[1:2, :])
            one[...] = out.astype(BF)
            n_ref[...] = normed
            r_ref[...] = inverse


def self_forward_kernel(width, blocks, rows, norm, col, row, *refs):
    pieces, refs = refs[:4], refs[4:]
    two, n_ref, r_ref, qkv, ctx, probs_ref, weight, acc = refs
    load_weight(pieces, weight)
    step = pl.program_id(0)

    @pl.when(step == 0)
    def _():
        acc[...] = rows[...].astype(F32)

    full = weight[...]
    in_part, out_part = full[:, : 3 * width], full[:, 3 * width :]
    triple = dot_nn(rows[...], in_part).astype(BF)
    qkv[0] = triple
    probs, context = attend(*thirds(triple, width), col[...] == row[...], blocks)
    probs_ref[0] = probs
    ctx[0] = context
    acc[...] += dot_nt(context, out_part)

    @pl.when(step == pl.num_programs(0) - 1)
    def _():
        out, normed, inverse = norm_forward(acc[...], norm[0:1, :], norm[1:2, :])
        two[...] = out.astype(BF)
        n_ref[...] = normed
        r_ref[...] = inverse


def feed_up_kernel(rows, *refs):
    pieces, refs = refs[:4], refs[4:]
    active_ref, slope_ref, weight = refs
    load_weight(pieces, weight)
    hidden = dot_nn(rows[...], weight[...])
    normal = 0.5 * (1.0 + lax.erf(hidden * 0.7071067811865476))
    slope = normal + hidden * jnp.exp(-0.5 * hidden * hidden) * 0.3989422804014327
    active_ref[0] = (hidden * normal).astype(BF)
    slope_ref[0] = slope.astype(slope_ref.dtype)


def feed_down_kernel(active, normed_two, cot, norm, *refs):
    pieces, grads, refs = refs[:4], refs[4:8], refs[8:]
    three, inward_ref, gain_ref, shift_ref, weight, acc, turned = refs
    step, groups = pl.program_id(0), pl.num_programs(0) // 2

    @pl.when(step == 0)
    def _():
        acc[...] = normed_two[...] * norm[0:1, :] + norm[1:2, :]

    @pl.when(step < groups)
    def _():
        load_weight(pieces, weight)
        acc[...] += dot_nt(active[0], weight[...])

    @pl.when(step == groups - 1)
    def _():
        gain = norm[2:3, :]
        out, normed, inverse = norm_forward(acc[...], gain, norm[3:4, :])
        three[...] = out.astype(BF)
        inward, gain_term, shift_term = norm_backward(cot[...].astype(F32), gain, normed, inverse)
        inward_ref[...] = inward
        turned[...] = inward.astype(BF).T
        gain_ref[...] = gain_term
        shift_ref[...] = shift_term

    @pl.when(step >= groups)
    def _():
        store_weight(dot_nn(turned[...], active[0]), grads)


def feed_back_kernel(inward, rows, slope, normed, inverse, norm, *refs):
    in_pieces, out_pieces, grads, refs = refs[:4], refs[4:8], refs[8:12], refs[12:]
    down_ref, gain_ref, shift_ref, weight_in, weight_out, acc, branch, turned = refs
    load_weight(in_pieces, weight_in)
    load_weight(out_pieces, weight_out)
    step = pl.program_id(0)

    @pl.when(step == 0)
    def _():
        acc[...] = inward[...]
        branch[...] = inward[...].astype(BF)
        turned[...] = rows[...].T

    grad_active = dot_nn(branch[...], weight_out[...])
    grad_hidden = (grad_active * slope[0].astype(F32)).astype(BF)
    store_weight(dot_nn(turned[...], grad_hidden), grads)
    acc[...] += dot_nt(grad_hidden, weight_in[...])

    @pl.when(step == pl.num_programs(0) - 1)
    def _():
        down, gain_term, shift_term = norm_backward(
            acc[...], norm[0:1, :], normed[...], inverse[...]
        )
        down_ref[...] = down
        gain_ref[...] = gain_term
        shift_ref[...] = shift_term


def self_backward_kernel(width, blocks, inward, rows, qkv, ctx, probs, *refs):
    pieces, grads, refs = refs[:4], refs[4:8], refs[8:]
    down_ref, weight, acc, branch, turned, branch_turned = refs
    load_weight(pieces, weight)
    step = pl.program_id(0)

    @pl.when(step == 0)
    def _():
        acc[...] = inward[...]
        gradient = inward[...].astype(BF)
        branch[...] = gradient
        branch_turned[...] = gradient.T
        turned[...] = rows[...].T

    full = weight[...]
    in_part, out_part = full[:, : 3 * width], full[:, 3 * width :]
    grad_context = dot_nn(branch[...], out_part).astype(BF)
    grads_of = attend_back(*thirds(qkv[0], width), probs[0], grad_context, blocks)
    grad_triple = jnp.concatenate(grads_of, axis=1)
    in_grad = dot_nn(turned[...], grad_triple).astype(BF)
    out_grad = dot_nn(branch_turned[...], ctx[0]).astype(BF)
    store_weight(jnp.concatenate([in_grad, out_grad], axis=1), grads)
    acc[...] += dot_nt(grad_triple, in_part)

    @pl.when(step == pl.num_programs(0) - 1)
    def _():
        down_ref[...] = acc[...].astype(down_ref.dtype)


def cross_backward_kernel(
    width, blocks, lang_up, vis_up, lang, vis, lang_n, lang_r, vis_n, vis_r, norm, *refs
):
    lang_qkv, vis_qkv, lang_ctx, vis_ctx, lang_p, vis_p = refs[:6]
    first, second, refs = refs[6:14], refs[14:22], refs[22:]
    first_grads, second_grads, refs = refs[:8], refs[8:16], refs[16:]
    lang_out, vis_out, gain_ref, shift_ref = refs[:4]
    weight, lang_acc, vis_acc, lang_branch, vis_branch, turned, branch_turned = refs[4:]
    load_weight(first, weight)
    load_weight(second, weight, first[0].shape[3])
    step = pl.program_id(0)

    @pl.when(step == 0)
    def _():
        gain_total, shift_total = 0.0, 0.0
        for up, n_ref, r_ref, acc, branch in (
            (lang_up, lang_n, lang_r, lang_acc, lang_branch),
            (vis_up, vis_n, vis_r, vis_acc, vis_branch),
        ):
            inward, gain_term, shift_term = norm_backward(
                up[...].astype(F32), norm[0:1, :], n_ref[...], r_ref[...]
            )
            acc[...] = inward
            branch[...] = inward.astype(BF)
            gain_total += gain_term
            shift_total += shift_term
        gain_ref[...] = gain_total
        shift_ref[...] = shift_total
        turned[...] = stack_rows([lang[...], vis[...]]).T
        branch_turned[...] = stack_rows([lang_branch[...], vis_branch[...]]).T

    full = weight[...]
    in_part, out_part = full[:, : 3 * width], full[:, 3 * width :]
    lang_gc = dot_nn(lang_branch[...], out_part).astype(BF)
    vis_gc = dot_nn(vis_branch[...], out_part).astype(BF)
    lang_query, lang_key, lang_value = thirds(lang_qkv[0], width)
    vis_query, vis_key, vis_value = thirds(vis_qkv[0], width)
    lang_dq, vis_dk, vis_dv = attend_back(
        lang_query, vis_key, vis_value, lang_p[0], lang_gc, blocks
    )
    vis_dq, lang_dk, lang_dv = attend_back(
        vis_query, lang_key, lang_value, vis_p[0], vis_gc, blocks
    )
    lang_grad = jnp.concatenate([lang_dq, lang_dk, lang_dv], axis=1)
    vis_grad = jnp.concatenate([vis_dq, vis_dk, vis_dv], axis=1)
    in_grad = dot_nn(turned[...], stack_rows([lang_grad, vis_grad]))
    out_grad = dot_nn(branch_turned[...], stack_rows([lang_ctx[0], vis_ctx[0]]))
    grad = jnp.concatenate([in_grad.astype(BF), out_grad.astype(BF)], axis=1)
    middle = first[0].shape[3]
    store_weight(grad[:, :middle], first_grads)
    store_weight(grad[:, middle:], second_grads)
    lang_acc[...] += dot_nt(lang_grad, in_part)
    vis_acc[...] += dot_nt(vis_grad, in_part)

    @pl.when(step == pl.num_programs(0) - 1)
    def _():
        lang_out[...] = lang_acc[...].astype(lang_out.dtype)
        vis_out[...] = vis_acc[...].astype(vis_out.dtype)


def store_step(state, clip, outs):
    new = adamw_step(*state, MATRIX_RATE, clip[0, 0])
    for (ref, place), value in zip(outs, new[:4] + (new[3], new[4])):
        ref[place] = value.astype(ref.dtype)


def attn_step_kernel(width, clip, grad, *refs):
    ins, outs, refs = refs[:4], refs[4:8], refs[8:]
    for kind in range(3):
        part = grad[0, :, kind * width : (kind + 1) * width]
        store_step([part] + [ref[0, kind] for ref in ins], clip, [(r, (0, kind)) for r in refs[:6]])
    part = grad[0, :, 3 * width :].T
    store_step([part] + [ref[0] for ref in outs], clip, [(r, 0) for r in refs[6:]])


def feed_step_kernel(clip, up, down, *refs):
    ins, outs, refs = refs[:4], refs[4:8], refs[8:]
    store_step([up[0]] + [ref[0] for ref in ins], clip, [(r, 0) for r in refs[:6]])
    store_step([down[0]] + [ref[0] for ref in outs], clip, [(r, 0) for r in refs[6:]])


def whole(shape):
    return pl.BlockSpec(shape, lambda m: (0,) * len(shape))


def per_step(shape):
    rest = (0,) * (len(shape) - 1)
    return pl.BlockSpec((1,) + tuple(shape[1:]), lambda m: (m,) + rest)


def held(shape, steps):
    rest = (0,) * (len(shape) - 1)
    last = shape[0] - 1
    return pl.BlockSpec((1,) + tuple(shape[1:]), lambda m: (jnp.minimum(m, last),) + rest)


def again(shape, steps):
    rest = (0,) * (len(shape) - 1)
    groups = shape[0]
    return pl.BlockSpec((1,) + tuple(shape[1:]), lambda m: (lax.rem(m, groups),) + rest)


def late(shape, steps):
    rest = (0,) * (len(shape) - 1)
    skip = steps - shape[0]
    return pl.BlockSpec((1,) + tuple(shape[1:]), lambda m: (jnp.maximum(m - skip, 0),) + rest)


def call(kernel, steps, ins, outs, scratch, name, flops):
    spec = {
        "whole": lambda s: whole(s),
        "step": lambda s: per_step(s),
        "held": lambda s: held(s, steps),
        "again": lambda s: again(s, steps),
        "late": lambda s: late(s, steps),
        "scalar": lambda s: pl.BlockSpec(memory_space=pltpu.SMEM),
    }
    moved = sum(a.size * a.dtype.itemsize for _, a in ins)
    moved += sum(math.prod(s) * jnp.dtype(t).itemsize for _, s, t in outs)
    return pl.pallas_call(
        kernel,
        grid=(steps,),
        in_specs=[spec[kind](a.shape) for kind, a in ins],
        out_specs=[spec[kind](s) for kind, s, _ in outs],
        out_shape=[jax.ShapeDtypeStruct(s, t) for _, s, t in outs],
        scratch_shapes=[pltpu.VMEM(s, t) for s, t in scratch],
        compiler_params=pltpu.CompilerParams(
            vmem_limit_bytes=VMEM_LIMIT, dimension_semantics=("arbitrary",)
        ),
        cost_estimate=pl.CostEstimate(flops=flops, bytes_accessed=moved, transcendentals=0),
        name=name,
    )(*[a for _, a in ins])


def swap_dp(value, bit):
    count = lax.axis_size("dp")
    return lax.ppermute(value, "dp", [(i, i ^ (1 << bit)) for i in range(count)])


def swap_mp(value, bit):
    count = lax.axis_size("mp")
    return lax.ppermute(value, "mp", [(i, i ^ (1 << bit)) for i in range(count)])


def after(value, *others):
    flat, tree = jax.tree.flatten(value)
    kept = lax.optimization_barrier((flat, jax.tree.leaves(others)))[0]
    return jax.tree.unflatten(tree, kept)


def extra_bits():
    return range(3, int(math.log2(lax.axis_size("dp"))))


def mp_bits():
    return range(int(math.log2(lax.axis_size("mp"))))


def gather_mp(current):
    for bit in reversed(mp_bits()):
        current = jnp.concatenate([current, swap_mp(current, bit)], axis=0)
    return current


def gather_extra(current):
    for bit in extra_bits():
        current = jnp.concatenate([current, swap_dp(current, bit)], axis=2)
    return current


def scatter_mp(current):
    for bit in mp_bits():
        half = current.shape[0] // 2
        current = added(current[:half], swap_mp(current[half:], bit))
    return current


def scatter_extra(current):
    for bit in reversed(extra_bits()):
        half = current.shape[2] // 2
        current = added(current[:, :, :half], swap_dp(current[:, :, half:], bit))
    return current


def added(mine, theirs):
    return (mine.astype(F32) + theirs.astype(F32)).astype(BF)


def grow(found, place, bit):
    for key in list(found):
        new = list(key)
        new[place] = 1
        found[tuple(new)] = swap_dp(found[key], bit)


def shrink(found, place, bit):
    for key in [k for k in found if k[place] == 0]:
        far = list(key)
        far[place] = 1
        found[key] = added(found[key], swap_dp(found.pop(tuple(far)), bit))


def home_list(found):
    return [found[(hi, mid, lo)] for hi in (0, 1) for lo in (0, 1) for mid in (0, 1)]


def stream_list(found):
    return [found[(hi, lo)] for hi in (0, 1) for lo in (0, 1)]


def home_keys(arrays):
    return {(i >> 2, i & 1, (i >> 1) & 1): a for i, a in enumerate(arrays)}


def stream_keys(arrays):
    return {(i >> 1, i & 1): a for i, a in enumerate(arrays)}


def adamw_step(gradient, moment, square, weight, average, rate, clip_scale):
    average_decay = min(AVERAGE_CEILING, (1.0 + STEP) / (10.0 + STEP))
    clipped = gradient * clip_scale
    moment_new = BETA_FIRST * moment + (1.0 - BETA_FIRST) * clipped
    square_new = BETA_SECOND * square + (1.0 - BETA_SECOND) * clipped * clipped
    corrected = moment_new / (1.0 - BETA_FIRST**STEP)
    denominator = jnp.sqrt(square_new / (1.0 - BETA_SECOND**STEP)) + ADAM_EPS
    weight_new = weight - rate * (corrected / denominator + WEIGHT_DECAY * weight)
    average_new = average_decay * average + (1.0 - average_decay) * weight_new
    return (clipped, moment_new, square_new, weight_new, average_new)


def pad_rows(block, rows):
    return jnp.pad(block, ((0, rows - block.shape[0]), (0, 0)))


def local(
    language,
    images,
    counts,
    language_cot,
    vision_cot,
    attn_in_weight,
    attn_in_moment,
    attn_in_square,
    attn_in_average,
    attn_out_weight,
    attn_out_moment,
    attn_out_square,
    attn_out_average,
    ffn_in_weight,
    ffn_in_moment,
    ffn_in_square,
    ffn_in_average,
    ffn_out_weight,
    ffn_out_moment,
    ffn_out_square,
    ffn_out_average,
    norm_weight,
    norm_moment,
    norm_square,
    norm_average,
):
    n_dp, n_mp = lax.axis_size("dp"), lax.axis_size("mp")
    me = lax.axis_index("dp")
    stream = (me >> 1) & 1
    is_vis = stream == 1
    own_items, words, dim = language.shape
    regions = images.shape[1]
    blocks = own_items // GROUP
    lang_block, vis_block = (-(-GROUP * rows // 16) * 16 for rows in (words, regions))
    lang_pad, slot = blocks * lang_block, blocks * vis_block
    total = 2 * slot
    shard_rows = attn_in_weight.shape[1]
    width = attn_in_weight.shape[3]
    units = ffn_in_weight.shape[2]
    heads = width // HEAD_DIM
    half = 2 * width
    eighth = dim // 8

    def mine_first(pair):
        return jnp.where(is_vis, pair[1], pair[0]), jnp.where(is_vis, pair[0], pair[1])

    attn_shards = [
        jnp.concatenate(
            [attn_in_weight[b].reshape(shard_rows, 3 * width), attn_out_weight[b].T], axis=1
        ).astype(BF)[None, None]
        for b in range(3)
    ]
    up_shards = [ffn_in_weight[s].astype(BF)[None, None] for s in range(2)]
    down_shards = [ffn_out_weight[s].T.astype(BF)[None, None] for s in range(2)]

    def pair_up(shards):
        own, other = mine_first(shards)
        return jnp.concatenate([own, swap_dp(other, 1)], axis=1)

    first, second = (gather_extra(gather_mp(attn_shards[0][..., c : c + half])) for c in (0, half))
    first, second = {(0, 0, 0): first}, {(0, 0, 0): second}
    down_pair = pair_up(down_shards)
    self_pair = pair_up(attn_shards[1:])
    up_pair = pair_up(up_shards)
    down_pair = jnp.stack([down_pair, swap_dp(down_pair, 2)], axis=1)
    grow(first, 0, 2)
    grow(second, 1, 1)
    self_w = {(0, 0): gather_extra(gather_mp(self_pair))}
    grow(first, 1, 1)
    grow(second, 0, 2)
    grow(first, 2, 0)
    grow(second, 2, 0)

    place = jnp.arange(dim, dtype=jnp.int32)
    block = place // shard_rows
    sub, high = block % (n_dp // 8), block // (n_dp // 8)
    relative = 8 * sub + 4 * (high >> 2) + ((high >> 1) & 1) + 2 * (high & 1)
    origin = (relative ^ me) * shard_rows + place % shard_rows
    order = (place[:, None] == origin[None, :]).astype(BF)

    def to_order(value):
        return dot_nn(value, order).astype(BF)

    def from_order(value, precision=None):
        return lax.dot_general(
            value, order, (((1,), (1,)), ((), ())), preferred_element_type=F32, precision=precision
        )

    def flip(value):
        parts = value.reshape(value.shape[0], 4, 2, eighth)
        return parts[:, :, ::-1, :].reshape(value.shape)

    norm_ordered = lax.dot_general(
        norm_weight.reshape(-1, dim),
        order.astype(F32),
        (((1,), (0,)), ((), ())),
        precision=HIGHEST,
        preferred_element_type=F32,
    ).reshape(norm_weight.shape)
    norm_cross = norm_ordered[:, 0]
    norm_self = jnp.where(is_vis, norm_ordered[:, 2], norm_ordered[:, 1])
    norm_feed = jnp.where(is_vis, norm_ordered[:, 4], norm_ordered[:, 3])
    norm_pair = jnp.concatenate([norm_self, norm_feed], axis=0)

    def in_blocks(value, rows, target):
        value = value.reshape(blocks, rows, dim)
        value = jnp.pad(value, ((0, 0), (0, target - rows), (0, 0)))
        return value.reshape(blocks * target, dim)

    def out_of_blocks(value, rows):
        return value.reshape(blocks, -1, dim)[:, :rows].reshape(blocks * rows, dim)

    lang_rows, vis_rows = GROUP * words, GROUP * regions
    first_item = lax.axis_index("mp") * own_items
    bounds = jnp.cumsum(counts[0])
    positions = first_item + jnp.arange(own_items, dtype=jnp.int32)
    item_image = jnp.sum((bounds[None, :] <= positions[:, None]).astype(jnp.int32), axis=1)
    region = jnp.arange(regions, dtype=jnp.int32)
    row_source = (item_image[:, None] * regions + region[None, :]).reshape(blocks, vis_rows) + 1
    row_source = jnp.pad(row_source, ((0, 0), (0, vis_block - vis_rows))).reshape(slot, 1)
    picker = (
        row_source == 1 + jnp.arange(images.shape[0] * regions, dtype=jnp.int32)[None, :]
    ).astype(BF)
    lang = to_order(in_blocks(language, lang_rows, lang_block))
    image_rows = to_order(images.reshape(-1, dim))
    vis = dot_nn(picker, image_rows).astype(BF)

    lang_cot = in_blocks(language_cot, lang_rows, vis_block)
    vis_cot = in_blocks(vision_cot, vis_rows, vis_block)
    cot_own, cot_other = mine_first((lang_cot, vis_cot))

    lang_ids = jnp.arange(lang_block, dtype=jnp.int32) // words
    vis_ids = jnp.arange(vis_block, dtype=jnp.int32) // regions
    slot_ids = jnp.where(is_vis, vis_ids, jnp.arange(vis_block, dtype=jnp.int32) // words)

    def tall(ids):
        return jnp.tile(ids, heads)[:, None]

    pieces = lambda arrays: [("step", a) for a in arrays]
    ins = [("whole", a) for a in (lang, vis, norm_cross)]
    ins += [
        ("whole", a)
        for a in (tall(lang_ids), lang_ids[None, :], tall(vis_ids), vis_ids[None, :])
    ]
    outs = []
    for rows in (lang_pad, slot):
        outs += [
            ("whole", (rows, dim), BF),
            ("whole", (rows, dim), F32),
            ("whole", (rows, 1), F32),
        ]
    outs += [("step", (n_mp, rows, 3 * width), BF) for rows in (lang_pad, slot)]
    outs += [("step", (n_mp, rows, width), BF) for rows in (lang_pad, slot)]
    outs += [
        ("step", (n_mp, heads * lang_pad, vis_block), BF),
        ("step", (n_mp, heads * slot, lang_block), BF),
    ]
    both = lang_pad + slot
    cross_w = home_list(first) + home_list(second)
    cross_w = after(cross_w, down_pair, self_w, up_pair)
    found = call(
        functools.partial(cross_forward_kernel, width, blocks),
        n_mp,
        ins + pieces(cross_w),
        outs,
        [((dim, 4 * width), BF), ((lang_pad, dim), F32), ((slot, dim), F32)],
        "cross_forward",
        12 * both * dim * 4 * width * n_mp,
    )
    lang_one, lang_n, lang_r, vis_one, vis_n, vis_r = found[:6]
    cross_saved = found[6:]

    grow(self_w, 0, 2)
    up_pair = gather_mp(up_pair)
    lang_wide = lang_one.reshape(blocks, lang_block, dim)
    lang_wide = jnp.pad(lang_wide, ((0, 0), (0, vis_block - lang_block), (0, 0)))
    own_one, other_one = mine_first((lang_wide.reshape(slot, dim), vis_one))
    rows_one = jnp.concatenate([own_one, flip(swap_dp(other_one, 1))], axis=0)
    grow(self_w, 1, 0)
    self_pieces = after(stream_list(self_w), up_pair)
    rows_two, normed_two, inverse_two, self_qkv, self_ctx, self_probs = call(
        functools.partial(self_forward_kernel, width, 2 * blocks),
        n_mp,
        [("whole", a) for a in (rows_one, norm_self, tall(slot_ids), slot_ids[None, :])]
        + pieces(self_pieces),
        [
            ("whole", (total, dim), BF),
            ("whole", (total, dim), F32),
            ("whole", (total, 1), F32),
            ("step", (n_mp, total, 3 * width), BF),
            ("step", (n_mp, total, width), BF),
            ("step", (n_mp, heads * total, vis_block), BF),
        ],
        [((dim, 4 * width), BF), ((total, dim), F32)],
        "self_forward",
        12 * total * dim * 4 * width * n_mp,
    )
    up_w = {(0, 0): gather_extra(up_pair)}
    grow(up_w, 0, 2)
    grow(up_w, 1, 0)
    up_w = stream_list(up_w)
    down_all = gather_mp(down_pair)
    down_w = {(h, 0): gather_extra(down_all[:, h]) for h in range(2)}
    grow(down_w, 1, 0)
    cot = to_order(jnp.concatenate([cot_own, swap_dp(cot_other, 1)], axis=0))

    active, slope = call(
        feed_up_kernel,
        n_mp,
        [("whole", rows_two)] + pieces(up_w),
        [("step", (n_mp, total, units), BF), ("step", (n_mp, total, units), BF)],
        [((dim, units), BF)],
        "feed_up",
        10 * total * dim * units * n_mp,
    )
    down_w = stream_list(down_w)
    stream_grad = [("step", (n_mp, 2, eighth, units), BF)] * 4
    found = call(
        feed_down_kernel,
        2 * n_mp,
        [("again", active)]
        + [("whole", a) for a in (normed_two, cot, norm_pair)]
        + [("held", a) for a in down_w],
        [("late", s, t) for _, s, t in stream_grad]
        + [
            ("whole", (total, dim), BF),
            ("whole", (total, dim), F32),
            ("whole", (1, dim), F32),
            ("whole", (1, dim), F32),
        ],
        [((dim, units), BF), ((total, dim), F32), ((dim, total), BF)],
        "feed_down",
        8 * total * dim * units * n_mp,
    )
    down_g = stream_keys(found[:4])
    rows_three, inward, feed_gain, feed_shift = found[4:]

    found = call(
        feed_back_kernel,
        n_mp,
        [("whole", inward), ("whole", rows_two), ("step", slope)]
        + [("whole", a) for a in (normed_two, inverse_two, norm_self)]
        + pieces(up_w)
        + pieces(down_w),
        stream_grad
        + [("whole", (total, dim), F32), ("whole", (1, dim), F32), ("whole", (1, dim), F32)],
        [
            ((dim, units), BF),
            ((dim, units), BF),
            ((total, dim), F32),
            ((total, dim), BF),
            ((dim, total), BF),
        ],
        "feed_back",
        12 * total * dim * units * n_mp,
    )
    up_g = stream_keys(found[:4])
    inward, self_gain, self_shift = found[4:]
    shrink(down_g, 1, 0)
    found = call(
        functools.partial(self_backward_kernel, width, 2 * blocks),
        n_mp,
        [("whole", after(inward, down_g)), ("whole", rows_one)]
        + [("step", a) for a in (self_qkv, self_ctx, self_probs)]
        + pieces(self_pieces),
        [("step", (n_mp, 2, eighth, 4 * width), BF)] * 4 + [("whole", (total, dim), BF)],
        [((dim, 4 * width), BF), ((total, dim), F32), ((total, dim), BF)] + [((dim, total), BF)] * 2,
        "self_backward",
        20 * total * dim * 4 * width * n_mp,
    )
    self_g = stream_keys(found[:4])
    back = found[4]
    shrink(up_g, 1, 0)
    down_g = {k: scatter_mp(scatter_extra(v)) for k, v in down_g.items()}
    back_other = swap_dp(flip(back[slot:]), 1)
    lang_up = jnp.where(is_vis, back_other, back[:slot])
    lang_up = lang_up.reshape(blocks, vis_block, dim)[:, :lang_block].reshape(lang_pad, dim)
    vis_up = jnp.where(is_vis, back[:slot], back_other)
    lang_up = after(lang_up, up_g)
    found = call(
        functools.partial(cross_backward_kernel, width, blocks),
        n_mp,
        [("whole", a) for a in (lang_up, vis_up, lang, vis, lang_n, lang_r, vis_n, vis_r, norm_cross)]
        + [("step", a) for a in cross_saved]
        + pieces(cross_w),
        [("step", (n_mp, 1, eighth, half), BF)] * 16
        + [
            ("whole", (lang_pad, dim), BF),
            ("whole", (slot, dim), BF),
            ("whole", (1, dim), F32),
            ("whole", (1, dim), F32),
        ],
        [
            ((dim, 4 * width), BF),
            ((lang_pad, dim), F32),
            ((slot, dim), F32),
            ((lang_pad, dim), BF),
            ((slot, dim), BF),
            ((dim, both), BF),
            ((dim, both), BF),
        ],
        "cross_backward",
        20 * both * dim * 4 * width * n_mp,
    )
    first_g, second_g = home_keys(found[:8]), home_keys(found[8:16])
    lang_back, vis_back, cross_gain, cross_shift = found[16:]
    shrink(self_g, 1, 0)
    shrink(up_g, 0, 2)
    shrink(first_g, 2, 0)
    shrink(second_g, 2, 0)
    shrink(first_g, 1, 1)
    shrink(second_g, 0, 2)
    shrink(down_g, 0, 2)
    shrink(self_g, 0, 2)
    shrink(first_g, 0, 2)
    shrink(second_g, 1, 1)

    def finish_home(found):
        return scatter_mp(scatter_extra(found[(0, 0, 0)]))[0, 0].astype(F32)

    def finish_stream(pair):
        mine, theirs = pair[0, 0].astype(F32), swap_dp(pair[0, 1], 1).astype(F32)
        return [jnp.where(is_vis, theirs, mine), jnp.where(is_vis, mine, theirs)]

    up_total = finish_stream(scatter_mp(scatter_extra(up_g[(0, 0)])))
    down_total = finish_stream(down_g[(0, 0)])
    self_total = finish_stream(scatter_mp(scatter_extra(self_g[(0, 0)])))
    attn_total = [jnp.concatenate([finish_home(first_g), finish_home(second_g)], axis=1)]
    attn_total += self_total

    final = from_order(rows_three).astype(BF)
    final_other = swap_dp(final[slot:], 1)
    language_out = out_of_blocks(jnp.where(is_vis, final_other, final[:slot]), lang_rows)
    vision_out = out_of_blocks(jnp.where(is_vis, final[:slot], final_other), vis_rows)
    language_grad = from_order(out_of_blocks(lang_back, lang_rows)).reshape(language.shape)
    image_term = lax.dot_general(
        picker, vis_back, (((0,), (0,)), ((), ())), preferred_element_type=F32
    ).astype(BF)
    image_term = from_order(image_term).astype(BF)
    image_grad = lax.psum(image_term, "mp")

    here = (jnp.arange(2, dtype=jnp.int32) == stream).astype(F32)[None, :, None]
    norm_partial = jnp.concatenate(
        [
            jnp.stack([cross_gain, cross_shift]),
            here * jnp.stack([self_gain, self_shift]),
            here * jnp.stack([feed_gain, feed_shift]),
        ],
        axis=1,
    )
    norm_partial = from_order(norm_partial.reshape(-1, dim).astype(F32), HIGHEST)

    squares = sum(jnp.sum(g * g) for g in attn_total + up_total + down_total)
    sums = jnp.concatenate([norm_partial, jnp.full((1, dim), squares)], axis=0)
    for bit in reversed(mp_bits()):
        sums += swap_mp(sums, bit)
    for bit in reversed(range(int(math.log2(n_dp)))):
        sums += swap_dp(sums, bit)
    norm_total = sums[:-1].reshape(norm_weight.shape)
    total_squares = sums[-1, 0] + jnp.sum(norm_total * norm_total)
    grad_norm = jnp.sqrt(total_squares)
    clip_scale = CLIP_NORM / jnp.maximum(grad_norm, CLIP_NORM)
    image_grad = after(image_grad, clip_scale).astype(F32).reshape(images.shape)

    clip = clip_scale.reshape(1, 1)
    kinds = [("step", t) for t in (F32, F32, F32, F32, BF, F32)]
    wide_in = [jnp.swapaxes(a, 1, 2) for a in (attn_in_moment, attn_in_square, attn_in_weight, attn_in_average)]
    wide_out = [attn_out_moment, attn_out_square, attn_out_weight, attn_out_average]
    attn_new = call(
        functools.partial(attn_step_kernel, width),
        3,
        [("scalar", clip), ("step", jnp.stack(attn_total))] + [("step", a) for a in wide_in + wide_out],
        [(k, wide_in[0].shape, t) for k, t in kinds] + [(k, wide_out[0].shape, t) for k, t in kinds],
        [],
        "attn_step",
        20 * 4 * dim * width,
    )
    attn_new = [jnp.swapaxes(a, 1, 2) for a in attn_new[:6]] + list(attn_new[6:])
    feed_in = [ffn_in_moment, ffn_in_square, ffn_in_weight, ffn_in_average]
    feed_out = [jnp.swapaxes(a, 1, 2) for a in (ffn_out_moment, ffn_out_square, ffn_out_weight, ffn_out_average)]
    feed_new = call(
        feed_step_kernel,
        2,
        [("scalar", clip), ("step", jnp.stack(up_total)), ("step", jnp.stack(down_total))]
        + [("step", a) for a in feed_in + feed_out],
        [(k, feed_in[0].shape, t) for k, t in kinds * 2],
        [],
        "feed_step",
        20 * 4 * dim * units,
    )
    feed_new = list(feed_new[:6]) + [jnp.swapaxes(a, 1, 2) for a in feed_new[6:]]

    results = [
        language_out.reshape(language.shape),
        vision_out.reshape(vision_cot.shape),
        language_grad,
        image_grad,
    ]
    results += attn_new + feed_new
    results += adamw_step(
        norm_total, norm_moment, norm_square, norm_weight, norm_average, NORM_RATE, clip_scale
    )
    return tuple(results) + (grad_norm,)


def solution(mesh):
    rows = P(("dp", "mp"), None, None)
    attn_in, attn_out = P(None, "dp", None, "mp"), P(None, "mp", "dp")
    ffn_in, ffn_out = P(None, "dp", "mp"), P(None, "mp", "dp")
    in_specs = (rows, P("dp", None, None), P("dp", None), rows, rows)
    in_specs += (attn_in,) * 4 + (attn_out,) * 4 + (ffn_in,) * 4 + (ffn_out,) * 4 + (P(),) * 4
    out_specs = (rows, rows, rows, P("dp", None, None))
    out_specs += (attn_in,) * 6 + (attn_out,) * 6 + (ffn_in,) * 6 + (ffn_out,) * 6 + (P(),) * 6
    return jax.shard_map(local, mesh=mesh, in_specs=in_specs, out_specs=out_specs, check_vma=False)
```

```python
import functools
import math

import jax
import jax.numpy as jnp
from jax import lax
from jax.experimental import pallas as pl
from jax.experimental.pallas import tpu as pltpu
from jax.sharding import Mesh
from jax.sharding import PartitionSpec as P

HEAD_DIM = 64
STEP = 10

NORM_EPS = 1e-05
CLIP_NORM = 1.0
BETA_FIRST = 0.9
BETA_SECOND = 0.999
ADAM_EPS = 1e-08
WEIGHT_DECAY = 0.01
MATRIX_RATE = 0.12
NORM_RATE = 0.8
AVERAGE_CEILING = 0.999
BF = jnp.bfloat16
F32 = jnp.float32
HIGHEST = lax.Precision.HIGHEST
SCALE = 1.0 / math.sqrt(HEAD_DIM)
DP = ("dq", "stream", "core")
VMEM_LIMIT = 56 * 1024 * 1024
GROUP = 3
MOST_ITEMS = 6


def dot_nn(a, b):
    return lax.dot_general(a, b, (((1,), (0,)), ((), ())), preferred_element_type=F32)


def dot_nt(a, b):
    return lax.dot_general(a, b, (((1,), (1,)), ((), ())), preferred_element_type=F32)


def dot_tn(a, b):
    return lax.dot_general(a, b, (((0,), (0,)), ((), ())), preferred_element_type=F32)


def norm_forward(summed, gain, shift):
    centre = jnp.mean(summed, axis=-1, keepdims=True)
    offset = summed - centre
    spread = jnp.mean(offset * offset, axis=-1, keepdims=True)
    inverse = lax.rsqrt(spread + NORM_EPS)
    normed = offset * inverse
    return normed * gain + shift, normed, inverse


def norm_backward(upstream, gain, normed, inverse):
    scaled = upstream * gain
    first_mean = jnp.mean(scaled, axis=-1, keepdims=True)
    second_mean = jnp.mean(scaled * normed, axis=-1, keepdims=True)
    inward = inverse * (scaled - first_mean - normed * second_mean)
    gain_term = jnp.sum(upstream * normed, axis=0, keepdims=True)
    shift_term = jnp.sum(upstream, axis=0, keepdims=True)
    return inward, gain_term, shift_term


def cut(block, blocks):
    rows = block.shape[0] // blocks
    return [block[i * rows : (i + 1) * rows] for i in range(blocks)]


def stack_rows(parts):
    return jnp.concatenate(parts, axis=0)


def thirds(triple, width):
    return [triple[:, i * width : (i + 1) * width] for i in range(triple.shape[1] // width)]


def lane_head(block):
    return lax.broadcasted_iota(jnp.int32, block.shape, 1) // HEAD_DIM


def spread(block):
    lanes = lane_head(block)
    zero = jnp.zeros_like(block)
    heads = block.shape[1] // HEAD_DIM
    return stack_rows([jnp.where(lanes == h, block, zero) for h in range(heads)])


def gathered(block):
    parts = cut(block, block.shape[1] // HEAD_DIM)
    lanes = lane_head(parts[0])
    out = parts[0]
    for h in range(1, len(parts)):
        out = jnp.where(lanes == h, parts[h], out)
    return out


def item_of(shape, axis, rows):
    place = lax.broadcasted_iota(jnp.int32, shape, axis)
    item = jnp.zeros(shape, jnp.int32)
    for border in range(1, MOST_ITEMS):
        item += (place >= border * rows).astype(jnp.int32)
    return item


def same_item(shape, query_rows, key_rows, heads):
    mask = item_of(shape, 0, query_rows) == item_of(shape, 1, key_rows)
    return stack_rows([mask] * heads)


def attend(query, key, value, mask, blocks):
    pairs = zip(cut(query, blocks), cut(key, blocks))
    scores = stack_rows([jnp.where(mask, dot_nt(spread(q), k) * SCALE, -1e30) for q, k in pairs])
    powered = jnp.exp(scores - jnp.max(scores, axis=-1, keepdims=True))
    probs = (powered * (1.0 / jnp.sum(powered, axis=-1, keepdims=True))).astype(BF)
    mixed = [gathered(dot_nn(p, v)) for p, v in zip(cut(probs, blocks), cut(value, blocks))]
    return probs, stack_rows(mixed).astype(BF)


def attend_back(query, key, value, probs, grad_context, blocks):
    queries, keys, values = cut(query, blocks), cut(key, blocks), cut(value, blocks)
    contexts, weights = [spread(g) for g in cut(grad_context, blocks)], cut(probs, blocks)
    grad_probs = stack_rows([dot_nt(g, v) for g, v in zip(contexts, values)])
    grad_value = stack_rows([dot_tn(p, g) for p, g in zip(weights, contexts)]).astype(BF)
    wide = probs.astype(F32)
    inner = jnp.sum(grad_probs * wide, axis=-1, keepdims=True)
    grad_scores = cut((wide * (grad_probs - inner) * SCALE).astype(BF), blocks)
    grad_query = stack_rows([gathered(dot_nn(s, k)) for s, k in zip(grad_scores, keys)])
    grad_key = stack_rows([dot_tn(s, spread(q)) for s, q in zip(grad_scores, queries)])
    return grad_query.astype(BF), grad_key.astype(BF), grad_value


def load_weight(pieces, weight, column=0):
    row = 0
    for piece in pieces:
        for part in range(piece.shape[1]):
            rows, columns = piece.shape[2:]
            weight[row : row + rows, column : column + columns] = piece[0, part]
            row += rows


def load_halves(pieces, weight):
    middle = len(pieces) // 2
    lower = pl.program_id(0) < pl.num_programs(0) // 2

    @pl.when(lower)
    def _():
        load_weight(pieces[:middle], weight)

    @pl.when(jnp.logical_not(lower))
    def _():
        load_weight(pieces[middle:], weight)


def store_weight(value, pieces):
    row = 0
    for piece in pieces:
        for part in range(piece.shape[1]):
            rows = piece.shape[2]
            piece[0, part] = value[row : row + rows, :].astype(piece.dtype)
            row += rows


def wide_spots(place, piece, shard_rows):
    groups, _, _, streams = piece.shape[:4]
    inner = max(groups // 2, 1)
    row = 0
    for high in range(groups // inner):
        for core in range(2):
            for part in range(streams):
                for sub in range(inner):
                    group = (sub * (groups // inner) + high) ^ place[0, 0]
                    yield row, (group, core ^ place[0, 1], 0, part)
                    row += shard_rows


def load_wide(place, piece, kind, weight):
    rows = piece.shape[5]
    for row, spot in wide_spots(place, piece, rows):
        weight[row : row + rows, :] = piece[spot + (kind,)]


def store_wide(place, value, piece, kind):
    rows = piece.shape[5]
    for row, spot in wide_spots(place, piece, rows):
        piece[spot + (kind,)] = value[row : row + rows, :].astype(piece.dtype)


def partner_order(value):
    dim = value.shape[1]
    eighth = dim // 8
    row = lax.broadcasted_iota(jnp.int32, (dim, dim), 0)
    column = lax.broadcasted_iota(jnp.int32, (dim, dim), 1)
    same = jnp.ones((dim, dim), jnp.bool_)
    for border in range(2 * eighth, dim, 2 * eighth):
        same &= (row >= border) == (column >= border)
    pick = same & (jnp.abs(row - column) == eighth)
    return dot_nn(value, jnp.where(pick, 1.0, 0.0).astype(BF)).astype(BF)


def widen(value, blocks, rows):
    empty = jnp.zeros((rows - value.shape[0] // blocks, value.shape[1]), value.dtype)
    return stack_rows([part for block in cut(value, blocks) for part in (block, empty)])


def cross_forward_kernel(width, blocks, words, regions, stream, lang, vis, norm, *refs):
    first, second, refs = refs[:8], refs[8:16], refs[16:]
    own_one, other_one, lang_n, lang_r, vis_n, vis_r = refs[:6]
    lang_qkv, vis_qkv, lang_ctx, vis_ctx, lang_p, vis_p = refs[6:12]
    weight, lang_acc, vis_acc = refs[12:]
    load_weight(first, weight)
    load_weight(second, weight, first[0].shape[3])
    step = pl.program_id(0)

    @pl.when(step == 0)
    def _():
        lang_acc[...] = lang[...].astype(F32)
        vis_acc[...] = vis[...].astype(F32)

    full = weight[...]
    in_part, out_part = full[:, : 3 * width], full[:, 3 * width :]
    lang_triple = dot_nn(lang[...], in_part).astype(BF)
    vis_triple = dot_nn(vis[...], in_part).astype(BF)
    lang_qkv[0] = lang_triple
    vis_qkv[0] = vis_triple
    lang_query, lang_key, lang_value = thirds(lang_triple, width)
    vis_query, vis_key, vis_value = thirds(vis_triple, width)
    heads = width // HEAD_DIM
    lang_block, vis_block = lang.shape[0] // blocks, vis.shape[0] // blocks
    lang_mask = same_item((lang_block, vis_block), words, regions, heads)
    vis_mask = same_item((vis_block, lang_block), regions, words, heads)
    for query, key, value, probs_ref, ctx_ref, acc, mask in (
        (lang_query, vis_key, vis_value, lang_p, lang_ctx, lang_acc, lang_mask),
        (vis_query, lang_key, lang_value, vis_p, vis_ctx, vis_acc, vis_mask),
    ):
        probs, context = attend(query, key, value, mask, blocks)
        probs_ref[0] = probs
        ctx_ref[0] = context
        acc[...] += dot_nt(context, out_part)

    @pl.when(step == pl.num_programs(0) - 1)
    def _():
        ones = []
        for acc, n_ref, r_ref in ((lang_acc, lang_n, lang_r), (vis_acc, vis_n, vis_r)):
            out, normed, inverse = norm_forward(acc[...], norm[0:1, :], norm[1:2, :])
            ones.append(out.astype(BF))
            n_ref[...] = normed
            r_ref[...] = inverse
        lang_one, vis_one = widen(ones[0], blocks, vis_block), ones[1]
        is_vis = stream[0, 0] == 1
        own_one[...] = jnp.where(is_vis, vis_one, lang_one)
        other_one[...] = partner_order(jnp.where(is_vis, lang_one, vis_one))


def self_forward_kernel(width, blocks, length, own, other, norm, *refs):
    pieces, refs = refs[:8], refs[8:]
    two, n_ref, r_ref, qkv, ctx, probs_ref, weight, acc, rows = refs
    step = pl.program_id(0)
    load_halves(pieces, weight)

    @pl.when(step == 0)
    def _():
        rows[...] = stack_rows([own[...], other[...]])
        acc[...] = rows[...].astype(F32)

    full = weight[...]
    in_part, out_part = full[:, : 3 * width], full[:, 3 * width :]
    triple = dot_nn(rows[...], in_part).astype(BF)
    qkv[0] = triple
    block = rows.shape[0] // blocks
    mask = same_item((block, block), length[0, 0], length[0, 0], width // HEAD_DIM)
    probs, context = attend(*thirds(triple, width), mask, blocks)
    probs_ref[0] = probs
    ctx[0] = context
    acc[...] += dot_nt(context, out_part)

    @pl.when(step == pl.num_programs(0) - 1)
    def _():
        out, normed, inverse = norm_forward(acc[...], norm[0:1, :], norm[1:2, :])
        two[...] = out.astype(BF)
        n_ref[...] = normed
        r_ref[...] = inverse


def feed_kernel(place, rows, normed_two, inverse, cot, norm, piece, *refs):
    three, grads, down_ref, self_gain, self_shift, feed_gain, feed_shift, refs = refs[:7] + (refs[7:],)
    weight_in, weight_out, active, slope, acc, branch, branch_turned, turned = refs
    step, groups = pl.program_id(0), pl.num_programs(0) // 2
    group = lax.rem(step, groups)

    @pl.when(step == 0)
    def _():
        acc[...] = normed_two[...] * norm[0:1, :] + norm[1:2, :]
        turned[...] = rows[...].T

    @pl.when(step < groups)
    def _():
        load_wide(place, piece, 0, weight_in.at[group])
        load_wide(place, piece, 1, weight_out.at[group])
        hidden = dot_nn(rows[...], weight_in[group])
        normal = 0.5 * (1.0 + lax.erf(hidden * 0.7071067811865476))
        slopes = normal + hidden * jnp.exp(-0.5 * hidden * hidden) * 0.3989422804014327
        actives = (hidden * normal).astype(BF)
        active[group] = actives
        slope[group] = slopes.astype(BF)
        acc[...] += dot_nt(actives, weight_out[group])

    @pl.when(step == groups - 1)
    def _():
        gain = norm[2:3, :]
        out, normed, inverse_three = norm_forward(acc[...], gain, norm[3:4, :])
        three[...] = out.astype(BF)
        inward, gain_term, shift_term = norm_backward(
            cot[...].astype(F32), gain, normed, inverse_three
        )
        acc[...] = inward
        branch[...] = inward.astype(BF)
        branch_turned[...] = inward.astype(BF).T
        feed_gain[...] = gain_term
        feed_shift[...] = shift_term

    @pl.when(step >= groups)
    def _():
        store_wide(place, dot_nn(branch_turned[...], active[group]), grads, 1)
        grad_active = dot_nn(branch[...], weight_out[group])
        grad_hidden = (grad_active * slope[group].astype(F32)).astype(BF)
        store_wide(place, dot_nn(turned[...], grad_hidden), grads, 0)
        acc[...] += dot_nt(grad_hidden, weight_in[group])

    @pl.when(step == 2 * groups - 1)
    def _():
        down, gain_term, shift_term = norm_backward(
            acc[...], norm[0:1, :], normed_two[...], inverse[...]
        )
        down_ref[...] = down
        self_gain[...] = gain_term
        self_shift[...] = shift_term


def self_backward_kernel(width, blocks, inward, own, other, qkv, ctx, probs, *refs):
    pieces, grads, refs = refs[:8], refs[8:12], refs[12:]
    down_own, down_other, weight, acc, branch, turned, branch_turned = refs
    load_halves(pieces, weight)
    step = pl.program_id(0)

    @pl.when(step == 0)
    def _():
        acc[...] = inward[...]
        gradient = inward[...].astype(BF)
        branch[...] = gradient
        branch_turned[...] = gradient.T
        turned[...] = stack_rows([own[...], other[...]]).T

    full = weight[...]
    in_part, out_part = full[:, : 3 * width], full[:, 3 * width :]
    grad_context = dot_nn(branch[...], out_part).astype(BF)
    grads_of = attend_back(*thirds(qkv[0], width), probs[0], grad_context, blocks)
    grad_triple = jnp.concatenate(grads_of, axis=1)
    in_grad = dot_nn(turned[...], grad_triple).astype(BF)
    out_grad = dot_nn(branch_turned[...], ctx[0]).astype(BF)
    store_weight(jnp.concatenate([in_grad, out_grad], axis=1), grads)
    acc[...] += dot_nt(grad_triple, in_part)

    @pl.when(step == pl.num_programs(0) - 1)
    def _():
        slot = own.shape[0]
        down_own[...] = acc[:slot].astype(BF)
        down_other[...] = partner_order(acc[slot:].astype(BF))


def cross_backward_kernel(
    width, blocks, stream, own_up, other_up, lang, vis, lang_n, lang_r, vis_n, vis_r, norm, *refs
):
    lang_qkv, vis_qkv, lang_ctx, vis_ctx, lang_p, vis_p = refs[:6]
    first, second, refs = refs[6:14], refs[14:22], refs[22:]
    first_grads, second_grads, refs = refs[:8], refs[8:16], refs[16:]
    lang_out, vis_out, gain_ref, shift_ref = refs[:4]
    weight, lang_acc, vis_acc, lang_branch, vis_branch, turned, branch_turned = refs[4:]
    load_weight(first, weight)
    load_weight(second, weight, first[0].shape[3])
    step = pl.program_id(0)

    @pl.when(step == 0)
    def _():
        is_vis = stream[0, 0] == 1
        own, other = own_up[...].astype(F32), other_up[...].astype(F32)
        lang_block = lang.shape[0] // blocks
        lang_up = cut(jnp.where(is_vis, other, own), blocks)
        lang_up = stack_rows([block[:lang_block] for block in lang_up])
        vis_up = jnp.where(is_vis, own, other)
        gain_total, shift_total = 0.0, 0.0
        for up, n_ref, r_ref, acc, branch in (
            (lang_up, lang_n, lang_r, lang_acc, lang_branch),
            (vis_up, vis_n, vis_r, vis_acc, vis_branch),
        ):
            inward, gain_term, shift_term = norm_backward(
                up, norm[0:1, :], n_ref[...], r_ref[...]
            )
            acc[...] = inward
            branch[...] = inward.astype(BF)
            gain_total += gain_term
            shift_total += shift_term
        gain_ref[...] = gain_total
        shift_ref[...] = shift_total
        turned[...] = stack_rows([lang[...], vis[...]]).T
        branch_turned[...] = stack_rows([lang_branch[...], vis_branch[...]]).T

    full = weight[...]
    in_part, out_part = full[:, : 3 * width], full[:, 3 * width :]
    lang_gc = dot_nn(lang_branch[...], out_part).astype(BF)
    vis_gc = dot_nn(vis_branch[...], out_part).astype(BF)
    lang_query, lang_key, lang_value = thirds(lang_qkv[0], width)
    vis_query, vis_key, vis_value = thirds(vis_qkv[0], width)
    lang_dq, vis_dk, vis_dv = attend_back(
        lang_query, vis_key, vis_value, lang_p[0], lang_gc, blocks
    )
    vis_dq, lang_dk, lang_dv = attend_back(
        vis_query, lang_key, lang_value, vis_p[0], vis_gc, blocks
    )
    lang_grad = jnp.concatenate([lang_dq, lang_dk, lang_dv], axis=1)
    vis_grad = jnp.concatenate([vis_dq, vis_dk, vis_dv], axis=1)
    in_grad = dot_nn(turned[...], stack_rows([lang_grad, vis_grad]))
    out_grad = dot_nn(branch_turned[...], stack_rows([lang_ctx[0], vis_ctx[0]]))
    grad = jnp.concatenate([in_grad.astype(BF), out_grad.astype(BF)], axis=1)
    middle = first[0].shape[3]
    store_weight(grad[:, :middle], first_grads)
    store_weight(grad[:, middle:], second_grads)
    lang_acc[...] += dot_nt(lang_grad, in_part)
    vis_acc[...] += dot_nt(vis_grad, in_part)

    @pl.when(step == pl.num_programs(0) - 1)
    def _():
        lang_out[...] = lang_acc[...].astype(lang_out.dtype)
        vis_out[...] = vis_acc[...].astype(vis_out.dtype)


def store_step(state, clip, outs):
    new = adamw_step(*state, MATRIX_RATE, clip)
    for (ref, place), value in zip(outs, new[:4] + (new[3], new[4])):
        ref[place] = value.astype(ref.dtype)


def step_kernel(width, sums, theirs, home_low, home_high, stream_one, stream_two, feed, *refs):
    ins, outs, feed_in, feed_out, norm_in = (refs[4 * i : 4 * i + 4] for i in range(5))
    refs = refs[20:]
    step = pl.program_id(0)
    total = sums[...] + theirs[...]
    norm_grad = total[:-1]
    squares = jnp.sum(norm_grad * norm_grad, keepdims=True) + total[-1:, 0:1]
    grad_norm = jnp.sqrt(squares)
    clip = CLIP_NORM / jnp.maximum(grad_norm, CLIP_NORM)
    refs[-1][...] = grad_norm
    for place in range(norm_in[0].shape[0]):
        state = [ref[place] for ref in norm_in]
        new = adamw_step(norm_grad[2 * place : 2 * place + 2], *state, NORM_RATE, clip)
        for ref, value in zip(refs[24:29], new):
            ref[place] = value
    home = jnp.concatenate([home_low[...], home_high[...]], axis=1)
    grad = jnp.where(step == 0, home, jnp.where(step == 1, stream_one[...], stream_two[...]))
    for kind in range(3):
        part = grad[:, kind * width : (kind + 1) * width]
        store_step([part] + [ref[0, kind] for ref in ins], clip, [(r, (0, kind)) for r in refs[:6]])
    part = grad[:, 3 * width :].T
    store_step([part] + [ref[0] for ref in outs], clip, [(r, 0) for r in refs[6:12]])
    for stream in range(feed.shape[0]):
        part = feed[stream, 0]
        state = [part] + [ref[stream] for ref in feed_in]
        store_step(state, clip, [(r, stream) for r in refs[12:18]])
        state = [feed[stream, 1]] + [ref[stream] for ref in feed_out]
        store_step(state, clip, [(r, stream) for r in refs[18:24]])


def whole(shape):
    return pl.BlockSpec(shape, lambda m: (0,) * len(shape))


def per_step(shape):
    rest = (0,) * (len(shape) - 1)
    return pl.BlockSpec((1,) + tuple(shape[1:]), lambda m: (m,) + rest)


def part_of(shape, pick):
    rest = (0,) * (len(shape) - 1)
    return pl.BlockSpec((1,) + tuple(shape[1:]), lambda m: (pick(m),) + rest)


def group_of(shape, pick):
    block = (shape[0], shape[1], 1) + tuple(shape[3:])
    return pl.BlockSpec(block, lambda m: (0, 0, pick(m), 0, 0, 0, 0))


def call(kernel, steps, ins, outs, scratch, name, flops):
    spec = {
        "whole": lambda s: whole(s),
        "step": lambda s: per_step(s),
        "early": lambda s: group_of(s, lambda m: jnp.minimum(m, s[2] - 1)),
        "late": lambda s: group_of(s, lambda m: jnp.maximum(m - s[2], 0)),
        "low": lambda s: part_of(s, lambda m: jnp.minimum(m, s[0] - 1)),
        "high": lambda s: part_of(s, lambda m: jnp.maximum(m - s[0], 0)),
        "rows": lambda s: pl.BlockSpec(
            tuple(s[:-2]) + (s[-2] // steps, s[-1]), lambda m: (0,) * (len(s) - 2) + (m, 0)
        ),
        "scalar": lambda s: pl.BlockSpec(memory_space=pltpu.SMEM),
    }
    moved = sum(a.size * a.dtype.itemsize for _, a in ins)
    moved += sum(math.prod(s) * jnp.dtype(t).itemsize for _, s, t in outs)
    return pl.pallas_call(
        kernel,
        grid=(steps,),
        in_specs=[spec[kind](a.shape) for kind, a in ins],
        out_specs=[spec[kind](s) for kind, s, _ in outs],
        out_shape=[jax.ShapeDtypeStruct(s, t) for _, s, t in outs],
        scratch_shapes=[pltpu.VMEM(s, t) for s, t in scratch],
        compiler_params=pltpu.CompilerParams(
            vmem_limit_bytes=VMEM_LIMIT, dimension_semantics=("arbitrary",)
        ),
        cost_estimate=pl.CostEstimate(flops=flops, bytes_accessed=moved, transcendentals=0),
        name=name,
    )(*[a for _, a in ins])


def swap_dp(value, bit):
    axis, place = (("core", 0), ("stream", 0), ("dq", bit - 2))[min(bit, 2)]
    count = lax.axis_size(axis)
    return lax.ppermute(value, axis, [(i, i ^ (1 << place)) for i in range(count)])


def swap_mp(value, bit):
    count = lax.axis_size("mp")
    return lax.ppermute(value, "mp", [(i, i ^ (1 << bit)) for i in range(count)])


def after(value, *others):
    flat, tree = jax.tree.flatten(value)
    kept = lax.optimization_barrier((flat, jax.tree.leaves(others)))[0]
    return jax.tree.unflatten(tree, kept)


def swap_mask(value, axis, mask):
    count = lax.axis_size(axis)
    return lax.ppermute(value, axis, [(i, i ^ mask) for i in range(count)])


def sum_up(value):
    count = lax.axis_size("mp")
    mask = 1
    while mask < count:
        if 2 * mask < count:
            theirs = [swap_mask(value, "mp", mask * k) for k in (1, 2, 3)]
            value = (value + theirs[0]) + (theirs[1] + theirs[2])
            mask *= 4
        else:
            value += swap_mask(value, "mp", mask)
            mask *= 2
    both = ("dq", "stream")
    count = lax.axis_size(both)
    mask = 1
    while mask < count:
        if 2 * mask < count:
            theirs = [swap_mask(value, both, mask * k) for k in (1, 2, 3)]
            value = (value + theirs[0]) + (theirs[1] + theirs[2])
            mask *= 4
        else:
            value += swap_mask(value, both, mask)
            mask *= 2
    return value, swap_dp(value, 0)


def extra_bits():
    return range(3, 2 + int(math.log2(lax.axis_size("dq"))))


def mp_bits():
    return range(int(math.log2(lax.axis_size("mp"))))


def gather_mp(current):
    for bit in reversed(mp_bits()):
        current = jnp.concatenate([current, swap_mp(current, bit)], axis=0)
    return current


def gather_extra(current):
    for bit in extra_bits():
        current = jnp.concatenate([current, swap_dp(current, bit)], axis=2)
    return current


def scatter_mp(current):
    for bit in mp_bits():
        half = current.shape[0] // 2
        current = added(current[:half], swap_mp(current[half:], bit))
    return current


def scatter_extra(current):
    for bit in reversed(extra_bits()):
        half = current.shape[2] // 2
        current = added(current[:, :, :half], swap_dp(current[:, :, half:], bit))
    return current


def added(mine, theirs):
    return (mine.astype(F32) + theirs.astype(F32)).astype(BF)


def grow(found, place, bit):
    for key in list(found):
        new = list(key)
        new[place] = 1
        found[tuple(new)] = swap_dp(found[key], bit)


def shrink(found, place, bit):
    for key in [k for k in found if k[place] == 0]:
        far = list(key)
        far[place] = 1
        found[key] = added(found[key], swap_dp(found.pop(tuple(far)), bit))


def home_list(found):
    return [found[(hi, mid, lo)] for hi in (0, 1) for lo in (0, 1) for mid in (0, 1)]


def stream_list(found):
    return [found[(hi, lo)] for hi in (0, 1) for lo in (0, 1)]


def home_keys(arrays):
    return {(i >> 2, i & 1, (i >> 1) & 1): a for i, a in enumerate(arrays)}


def stream_keys(arrays):
    return {(i >> 1, i & 1): a for i, a in enumerate(arrays)}


def adamw_step(gradient, moment, square, weight, average, rate, clip_scale):
    average_decay = min(AVERAGE_CEILING, (1.0 + STEP) / (10.0 + STEP))
    clipped = gradient * clip_scale
    moment_new = BETA_FIRST * moment + (1.0 - BETA_FIRST) * clipped
    square_new = BETA_SECOND * square + (1.0 - BETA_SECOND) * clipped * clipped
    corrected = moment_new / (1.0 - BETA_FIRST**STEP)
    denominator = jnp.sqrt(square_new / (1.0 - BETA_SECOND**STEP)) + ADAM_EPS
    weight_new = weight - rate * (corrected / denominator + WEIGHT_DECAY * weight)
    average_new = average_decay * average + (1.0 - average_decay) * weight_new
    return (clipped, moment_new, square_new, weight_new, average_new)


def pad_rows(block, rows):
    return jnp.pad(block, ((0, rows - block.shape[0]), (0, 0)))


def local(
    language,
    images,
    counts,
    language_cot,
    vision_cot,
    attn_in_weight,
    attn_in_moment,
    attn_in_square,
    attn_in_average,
    attn_out_weight,
    attn_out_moment,
    attn_out_square,
    attn_out_average,
    ffn_in_weight,
    ffn_in_moment,
    ffn_in_square,
    ffn_in_average,
    ffn_out_weight,
    ffn_out_moment,
    ffn_out_square,
    ffn_out_average,
    norm_weight,
    norm_moment,
    norm_square,
    norm_average,
):
    n_dp, n_mp = lax.axis_size(DP), lax.axis_size("mp")
    me = lax.axis_index(DP)
    stream = (me >> 1) & 1
    is_vis = stream == 1
    own_items, words, dim = language.shape
    regions = images.shape[1]
    blocks = own_items // GROUP
    lang_block, vis_block = (-(-GROUP * rows // 16) * 16 for rows in (words, regions))
    lang_pad, slot = blocks * lang_block, blocks * vis_block
    total = 2 * slot
    shard_rows = attn_in_weight.shape[1]
    width = attn_in_weight.shape[3]
    units = ffn_in_weight.shape[2]
    heads = width // HEAD_DIM
    half = 2 * width
    eighth = dim // 8

    def mine_first(pair):
        return jnp.where(is_vis, pair[1], pair[0]), jnp.where(is_vis, pair[0], pair[1])

    attn_shards = [
        jnp.concatenate(
            [attn_in_weight[b].reshape(shard_rows, 3 * width), attn_out_weight[b].T], axis=1
        ).astype(BF)[None, None]
        for b in range(3)
    ]
    def pair_up(shards, *pins):
        own, other = mine_first(shards)
        return jnp.concatenate([own, swap_dp(after(other, *pins), 1)], axis=1)

    halves = [attn_shards[0][..., c : c + half] for c in (0, half)]
    self_pair = pair_up(attn_shards[1:])
    for bit in reversed(mp_bits()):
        halves = [jnp.concatenate([h, swap_mp(h, bit)], axis=0) for h in halves]
        if bit == mp_bits()[-1]:
            feed_own, feed_other = mine_first(
                [jnp.stack([ffn_in_weight[s].astype(BF), ffn_out_weight[s].T.astype(BF)]) for s in range(2)]
            )
            feed_pair = jnp.stack([feed_own, swap_dp(feed_other, 1)])
            feed_w = lax.all_gather(after(feed_pair, halves), ("dq", "core", "mp"), axis=0)
            feed_w = feed_w.reshape((n_dp // 4, 2, n_mp) + feed_pair.shape)
    first, second = ({(0, 0, 0): gather_extra(h)} for h in halves)

    def gather_step(current, index):
        return jnp.concatenate([current, swap_mp(current, mp_bits()[-1 - index])], axis=0)

    n_bits = len(mp_bits())
    self_low = self_pair
    for index in range(n_bits - 1):
        self_low = gather_step(self_low, index)
    grow(first, 0, 2)
    grow(second, 1, 1)

    place = jnp.arange(dim, dtype=jnp.int32)
    block = place // shard_rows
    sub, high = block % (n_dp // 8), block // (n_dp // 8)
    relative = 8 * sub + 4 * (high >> 2) + ((high >> 1) & 1) + 2 * (high & 1)
    origin = (relative ^ me) * shard_rows + place % shard_rows
    order = (place[:, None] == origin[None, :]).astype(BF)

    def to_order(value):
        return dot_nn(value, order).astype(BF)

    def from_order(value, precision=None):
        return lax.dot_general(
            value, order, (((1,), (1,)), ((), ())), preferred_element_type=F32, precision=precision
        )

    norm_ordered = lax.dot_general(
        norm_weight.reshape(-1, dim),
        order.astype(F32),
        (((1,), (0,)), ((), ())),
        precision=HIGHEST,
        preferred_element_type=F32,
    ).reshape(norm_weight.shape)
    norm_cross = norm_ordered[:, 0]
    norm_self = jnp.where(is_vis, norm_ordered[:, 2], norm_ordered[:, 1])
    norm_feed = jnp.where(is_vis, norm_ordered[:, 4], norm_ordered[:, 3])
    norm_pair = jnp.concatenate([norm_self, norm_feed], axis=0)

    def in_blocks(value, rows, target):
        value = value.reshape(blocks, rows, dim)
        value = jnp.pad(value, ((0, 0), (0, target - rows), (0, 0)))
        return value.reshape(blocks * target, dim)

    def out_of_blocks(value, rows):
        return value.reshape(blocks, -1, dim)[:, :rows].reshape(blocks * rows, dim)

    lang_rows, vis_rows = GROUP * words, GROUP * regions
    first_item = lax.axis_index("mp") * own_items
    bounds = jnp.cumsum(counts[0])
    positions = first_item + jnp.arange(own_items, dtype=jnp.int32)
    item_image = jnp.sum((bounds[None, :] <= positions[:, None]).astype(jnp.int32), axis=1)
    region = jnp.arange(regions, dtype=jnp.int32)
    row_source = (item_image[:, None] * regions + region[None, :]).reshape(blocks, vis_rows) + 1
    row_source = jnp.pad(row_source, ((0, 0), (0, vis_block - vis_rows))).reshape(slot, 1)
    image_count = images.shape[0] * regions
    picker = (row_source == 1 + jnp.arange(image_count, dtype=jnp.int32)[None, :]).astype(BF)
    lang = to_order(in_blocks(language, lang_rows, lang_block))
    image_rows = to_order(images.reshape(-1, dim))
    vis = dot_nn(picker, image_rows).astype(BF)

    lang_cot = in_blocks(language_cot, lang_rows, vis_block)
    vis_cot = in_blocks(vision_cot, vis_rows, vis_block)
    cot_own, cot_other = mine_first((lang_cot, vis_cot))

    length = jnp.where(is_vis, regions, words).astype(jnp.int32).reshape(1, 1)

    first, second = after((first, second), lang, vis)
    grow(first, 1, 1)
    grow(second, 0, 2)
    self_low = {(0, 0): gather_extra(self_low)}
    self_high = {(0, 0): swap_mp(self_low[(0, 0)], 0)}
    grow(first, 2, 0)
    grow(second, 2, 0)
    pieces = lambda arrays: [("step", a) for a in arrays]
    which = stream.astype(jnp.int32).reshape(1, 1)
    ins = [("scalar", which)] + [("whole", a) for a in (lang, vis, norm_cross)]
    outs = [("whole", (slot, dim), BF)] * 2
    for rows in (lang_pad, slot):
        outs += [("whole", (rows, dim), F32), ("whole", (rows, 1), F32)]
    outs += [("step", (n_mp, rows, 3 * width), BF) for rows in (lang_pad, slot)]
    outs += [("step", (n_mp, rows, width), BF) for rows in (lang_pad, slot)]
    outs += [
        ("step", (n_mp, heads * lang_pad, vis_block), BF),
        ("step", (n_mp, heads * slot, lang_block), BF),
    ]
    both = lang_pad + slot
    cross_w = home_list(first) + home_list(second)
    cross_w = after(cross_w, self_low)
    grow(self_low, 0, 2)
    found = call(
        functools.partial(cross_forward_kernel, width, blocks, words, regions),
        n_mp,
        ins + pieces(cross_w),
        outs,
        [((dim, 4 * width), BF), ((lang_pad, dim), F32), ((slot, dim), F32)],
        "cross_forward",
        12 * both * dim * 4 * width * n_mp,
    )
    own_one, other_one, lang_n, lang_r, vis_n, vis_r = found[:6]
    cross_saved = found[6:]

    other_one = swap_dp(other_one, 1)
    self_high, self_low, cot_other = after((self_high, self_low, cot_other), other_one)
    grow(self_high, 0, 2)
    grow(self_low, 1, 0)
    grow(self_high, 1, 0)
    self_pieces = [("low", a) for a in stream_list(self_low)]
    self_pieces += [("high", a) for a in stream_list(self_high)]
    rows_two, normed_two, inverse_two, self_qkv, self_ctx, self_probs = call(
        functools.partial(self_forward_kernel, width, 2 * blocks),
        n_mp,
        [("scalar", length)] + [("whole", a) for a in (own_one, other_one, norm_self)]
        + self_pieces,
        [
            ("whole", (total, dim), BF),
            ("whole", (total, dim), F32),
            ("whole", (total, 1), F32),
            ("step", (n_mp, total, 3 * width), BF),
            ("step", (n_mp, total, width), BF),
            ("step", (n_mp, heads * total, vis_block), BF),
        ],
        [((dim, 4 * width), BF), ((total, dim), F32), ((total, dim), BF)],
        "self_forward",
        12 * total * dim * 4 * width * n_mp,
    )
    cot = to_order(jnp.concatenate([cot_own, swap_dp(cot_other, 1)], axis=0))
    spot = jnp.stack([me >> 2, me & 1]).astype(jnp.int32).reshape(1, 2)

    whole_row = ("whole", (1, dim), F32)
    rows_three, feed_g, inward, self_gain, self_shift, feed_gain, feed_shift = call(
        feed_kernel,
        2 * n_mp,
        [("scalar", spot)]
        + [("whole", a) for a in (rows_two, normed_two, inverse_two, cot, norm_pair)]
        + [("early", feed_w)],
        [("whole", (total, dim), BF), ("late", feed_w.shape, BF), ("whole", (total, dim), F32)]
        + [whole_row] * 4,
        [((n_mp, dim, units), BF)] * 2
        + [((n_mp, total, units), BF)] * 2
        + [((total, dim), F32), ((total, dim), BF), ((dim, total), BF), ((dim, total), BF)],
        "feed",
        24 * total * dim * units * n_mp,
    )

    feed_sum = lax.psum_scatter(
        (feed_g * (1 + 0 * (me < 0)).astype(BF)).reshape((-1,) + feed_pair.shape), ("dq", "core", "mp"), scatter_dimension=0, tiled=True
    )[0]

    def core_step(found, *pins):
        theirs = [swap_dp(found[(hi, 1)], 0) for hi in (0, 1)]
        return [found[(hi, 0)] for hi in (0, 1)], after(theirs, *pins)

    def split(mine, theirs):
        middle = mine.shape[0] // 2
        return added(mine[:middle], theirs[:middle]), added(mine[middle:], theirs[middle:])

    def send_mp(parts, bit):
        return [(keep, swap_mp(far, bit)) for keep, far in parts]

    found = call(
        functools.partial(self_backward_kernel, width, 2 * blocks),
        n_mp,
        [("whole", a) for a in (inward, own_one, other_one)]
        + [("step", a) for a in (self_qkv, self_ctx, self_probs)]
        + self_pieces,
        [("step", (n_mp, 2, eighth, 4 * width), BF)] * 4 + [("whole", (slot, dim), BF)] * 2,
        [((dim, 4 * width), BF), ((total, dim), F32), ((total, dim), BF)] + [((dim, total), BF)] * 2,
        "self_backward",
        20 * total * dim * 4 * width * n_mp,
    )
    self_g = stream_keys(found[:4])
    own_up, other_up = found[4:]
    other_up = swap_dp(other_up, 1)
    self_core = core_step(self_g)
    self_sums = [added(m, t) for m, t in zip(*self_core)]
    own_up = after(own_up, self_sums)
    found = call(
        functools.partial(cross_backward_kernel, width, blocks),
        n_mp,
        [("scalar", which)]
        + [("whole", a) for a in (own_up, other_up, lang, vis)]
        + [("whole", a) for a in (lang_n, lang_r, vis_n, vis_r, norm_cross)]
        + [("step", a) for a in cross_saved]
        + pieces(cross_w),
        [("step", (n_mp, 1, eighth, half), BF)] * 16
        + [
            ("whole", (lang_pad, dim), BF),
            ("whole", (slot, dim), BF),
            ("whole", (1, dim), F32),
            ("whole", (1, dim), F32),
        ],
        [
            ((dim, 4 * width), BF),
            ((lang_pad, dim), F32),
            ((slot, dim), F32),
            ((lang_pad, dim), BF),
            ((slot, dim), BF),
            ((dim, both), BF),
            ((dim, both), BF),
        ],
        "cross_backward",
        20 * both * dim * 4 * width * n_mp,
    )
    first_g, second_g = home_keys(found[:8]), home_keys(found[8:16])
    lang_back, vis_back, cross_gain, cross_shift = found[16:]
    self_far = swap_dp(self_sums[1], 2)
    self_far = after(self_far, lang_back)
    late = after((first_g, second_g, lang_back, vis_back, cross_gain, cross_shift), self_far)
    first_g, second_g, lang_back, vis_back, cross_gain, cross_shift = late
    shrink(first_g, 2, 0)
    shrink(second_g, 2, 0)
    shrink(first_g, 1, 1)
    shrink(second_g, 0, 2)
    self_part = split(self_sums[0], self_far)
    first_g, second_g = after((first_g, second_g), self_part)
    late = after((lang_back, vis_back, cross_gain, cross_shift, rows_three), first_g, second_g)
    lang_back, vis_back, cross_gain, cross_shift, rows_three = late
    shrink(first_g, 0, 2)
    shrink(second_g, 1, 1)
    first_sum, second_sum = scatter_extra(first_g[(0, 0, 0)]), scatter_extra(second_g[(0, 0, 0)])
    homes, pair = [first_sum, second_sum], None
    for bit in range(n_bits):
        homes = [added(*send_mp([(h[: len(h) // 2], h[len(h) // 2 :])], bit)[0]) for h in homes]
        pair = added(*send_mp([self_part], bit)[0])
        self_part = pair[: len(pair) // 2], pair[len(pair) // 2 :]
        if bit == 0:
            theirs = swap_dp(feed_sum[1], 1)
            homes = after(homes, pair, theirs)
            mine, theirs = feed_sum[0].astype(F32), theirs.astype(F32)
            feed_total = [jnp.where(is_vis, theirs, mine), jnp.where(is_vis, mine, theirs)]
    attn_total = [h[0, 0].astype(F32) for h in homes]
    pair = scatter_extra(pair)
    mine, theirs = pair[0, 0].astype(F32), swap_dp(pair[0, 1], 1).astype(F32)
    attn_total += [jnp.where(is_vis, theirs, mine), jnp.where(is_vis, mine, theirs)]

    final = from_order(rows_three).astype(BF)
    final_other = swap_dp(final[slot:], 1)
    language_out = out_of_blocks(jnp.where(is_vis, final_other, final[:slot]), lang_rows)
    vision_out = out_of_blocks(jnp.where(is_vis, final[:slot], final_other), vis_rows)

    language_grad = from_order(out_of_blocks(lang_back, lang_rows)).reshape(language.shape)
    place_mp = lax.axis_index("mp")
    part = -(-image_count // n_mp // 16) * 16
    index = jnp.arange(n_mp, dtype=jnp.int32)
    far = sum(((index >> b) & 1) << (n_bits - 1 - b) for b in range(n_bits))
    rows = ((far ^ place_mp)[:, None] * part + jnp.arange(part, dtype=jnp.int32)[None, :]).reshape(1, -1)
    chooser = (row_source == 1 + rows).astype(BF)
    image_term = lax.dot_general(
        chooser, vis_back, (((0,), (0,)), ((), ())), preferred_element_type=F32
    ).astype(BF)
    image_term = from_order(image_term).astype(BF).reshape(n_mp, part, dim)
    image_term = gather_mp(scatter_mp(image_term))
    for b in range(n_bits):
        shape = (1 << b, 2, -1, part, dim)
        flipped = image_term.reshape(shape)[:, ::-1].reshape(image_term.shape)
        image_term = jnp.where((place_mp >> b) & 1 == 1, flipped, image_term)
    axes = tuple(reversed(range(n_bits))) + (n_bits, n_bits + 1)
    image_term = image_term.reshape((2,) * n_bits + (part, dim)).transpose(axes)
    image_grad = image_term.reshape(-1, dim)[:image_count].astype(F32).reshape(images.shape)

    here = (jnp.arange(2, dtype=jnp.int32) == stream).astype(F32)[:, None, None]
    norm_partial = jnp.concatenate(
        [
            jnp.concatenate([cross_gain, cross_shift], axis=0)[None],
            here * jnp.concatenate([self_gain, self_shift], axis=0)[None],
            here * jnp.concatenate([feed_gain, feed_shift], axis=0)[None],
        ],
        axis=0,
    )
    norm_partial = from_order(norm_partial.reshape(-1, dim), HIGHEST)

    squares = sum(jnp.sum(g * g) for g in attn_total + feed_total)
    sums, their_sums = sum_up(jnp.concatenate([norm_partial, jnp.full((1, dim), squares)], axis=0))
    kinds = [("step", t) for t in (F32, F32, F32, F32, BF, F32)]
    norm_in = [
        jnp.swapaxes(a, 0, 1)
        for a in (norm_moment, norm_square, norm_weight, norm_average)
    ]
    wide_in = [jnp.swapaxes(a, 1, 2) for a in (attn_in_moment, attn_in_square, attn_in_weight, attn_in_average)]
    wide_out = [attn_out_moment, attn_out_square, attn_out_weight, attn_out_average]
    feed_in = [ffn_in_moment, ffn_in_square, ffn_in_weight, ffn_in_average]
    feed_out = [
        jnp.swapaxes(a, 1, 2)
        for a in (ffn_out_moment, ffn_out_square, ffn_out_weight, ffn_out_average)
    ]
    by_rows = "rows" if shard_rows % 48 == 0 else "whole"
    stepped = call(
        functools.partial(step_kernel, width),
        3,
        [("whole", a) for a in [sums, their_sums] + attn_total]
        + [(by_rows, jnp.stack(feed_total))]
        + [("step", a) for a in wide_in + wide_out]
        + [(by_rows, a) for a in feed_in + feed_out]
        + [("whole", a) for a in norm_in],
        [(k, wide_in[0].shape, t) for k, t in kinds]
        + [(k, wide_out[0].shape, t) for k, t in kinds]
        + [(by_rows, feed_in[0].shape, t) for k, t in kinds * 2]
        + [("whole", norm_in[0].shape, F32)] * 5
        + [("whole", (1, 1), F32)],
        [],
        "step",
        20 * 8 * dim * width,
    )
    stepped = [jnp.swapaxes(a, 1, 2) if i < 6 or 18 <= i < 24 else a for i, a in enumerate(stepped)]
    stepped[24:29] = [jnp.swapaxes(a, 0, 1) for a in stepped[24:29]]

    results = [
        language_out.reshape(language.shape),
        vision_out.reshape(vision_cot.shape),
        language_grad,
        image_grad,
    ]
    results += stepped[:-1]
    return tuple(results) + (stepped[-1][0, 0],)


def solution(mesh):
    shape = (mesh.shape["dp"] // 4, 2, 2, mesh.shape["mp"])
    mesh = Mesh(mesh.devices.reshape(shape), DP + ("mp",))
    rows = P(DP + ("mp",), None, None)
    attn_in, attn_out = P(None, DP, None, "mp"), P(None, "mp", DP)
    ffn_in, ffn_out = P(None, DP, "mp"), P(None, "mp", DP)
    in_specs = (rows, P(DP, None, None), P(DP, None), rows, rows)
    in_specs += (attn_in,) * 4 + (attn_out,) * 4 + (ffn_in,) * 4 + (ffn_out,) * 4 + (P(),) * 4
    out_specs = (rows, rows, rows, P(DP, None, None))
    out_specs += (attn_in,) * 6 + (attn_out,) * 6 + (ffn_in,) * 6 + (ffn_out,) * 6 + (P(),) * 6
    return jax.shard_map(local, mesh=mesh, in_specs=in_specs, out_specs=out_specs, check_vma=False)
```

```python
import functools
import math

import jax
import jax.numpy as jnp
from jax import lax
from jax.experimental import pallas as pl
from jax.experimental.pallas import tpu as pltpu
from jax.sharding import Mesh
from jax.sharding import PartitionSpec as P

HEAD_DIM = 64
STEP = 10

NORM_EPS = 1e-05
CLIP_NORM = 1.0
BETA_FIRST = 0.9
BETA_SECOND = 0.999
ADAM_EPS = 1e-08
WEIGHT_DECAY = 0.01
MATRIX_RATE = 0.12
NORM_RATE = 0.8
AVERAGE_CEILING = 0.999
BF = jnp.bfloat16
F32 = jnp.float32
HIGHEST = lax.Precision.HIGHEST
SCALE = 1.0 / math.sqrt(HEAD_DIM)
DP = ("dq", "stream", "core")
VMEM_LIMIT = 56 * 1024 * 1024
GROUP = 3
MOST_ITEMS = 6


def dot_nn(a, b):
    return lax.dot_general(a, b, (((1,), (0,)), ((), ())), preferred_element_type=F32)


def dot_nt(a, b):
    return lax.dot_general(a, b, (((1,), (1,)), ((), ())), preferred_element_type=F32)


def dot_tn(a, b):
    return lax.dot_general(a, b, (((0,), (0,)), ((), ())), preferred_element_type=F32)


def norm_forward(summed, gain, shift):
    centre = jnp.mean(summed, axis=-1, keepdims=True)
    offset = summed - centre
    spread = jnp.mean(offset * offset, axis=-1, keepdims=True)
    inverse = lax.rsqrt(spread + NORM_EPS)
    normed = offset * inverse
    return normed * gain + shift, normed, inverse


def norm_backward(upstream, gain, normed, inverse):
    scaled = upstream * gain
    first_mean = jnp.mean(scaled, axis=-1, keepdims=True)
    second_mean = jnp.mean(scaled * normed, axis=-1, keepdims=True)
    inward = inverse * (scaled - first_mean - normed * second_mean)
    gain_term = jnp.sum(upstream * normed, axis=0, keepdims=True)
    shift_term = jnp.sum(upstream, axis=0, keepdims=True)
    return inward, gain_term, shift_term


def cut(block, blocks):
    rows = block.shape[0] // blocks
    return [block[i * rows : (i + 1) * rows] for i in range(blocks)]


def stack_rows(parts):
    return jnp.concatenate(parts, axis=0)


def thirds(triple, width):
    return [triple[:, i * width : (i + 1) * width] for i in range(triple.shape[1] // width)]


def lane_head(block):
    return lax.broadcasted_iota(jnp.int32, block.shape, 1) // HEAD_DIM


def spread(block):
    lanes = lane_head(block)
    zero = jnp.zeros_like(block)
    heads = block.shape[1] // HEAD_DIM
    return stack_rows([jnp.where(lanes == h, block, zero) for h in range(heads)])


def gathered(block):
    parts = cut(block, block.shape[1] // HEAD_DIM)
    lanes = lane_head(parts[0])
    out = parts[0]
    for h in range(1, len(parts)):
        out = jnp.where(lanes == h, parts[h], out)
    return out


def item_of(shape, axis, rows):
    place = lax.broadcasted_iota(jnp.int32, shape, axis)
    item = jnp.zeros(shape, jnp.int32)
    for border in range(1, MOST_ITEMS):
        item += (place >= border * rows).astype(jnp.int32)
    return item


def same_item(shape, query_rows, key_rows, heads):
    mask = item_of(shape, 0, query_rows) == item_of(shape, 1, key_rows)
    return stack_rows([mask] * heads)


def attend(query, key, value, mask, blocks):
    pairs = zip(cut(query, blocks), cut(key, blocks))
    scores = stack_rows([jnp.where(mask, dot_nt(spread(q), k) * SCALE, -1e30) for q, k in pairs])
    powered = jnp.exp(scores - jnp.max(scores, axis=-1, keepdims=True))
    probs = (powered * (1.0 / jnp.sum(powered, axis=-1, keepdims=True))).astype(BF)
    mixed = [gathered(dot_nn(p, v)) for p, v in zip(cut(probs, blocks), cut(value, blocks))]
    return probs, stack_rows(mixed).astype(BF)


def attend_back(query, key, value, probs, grad_context, blocks):
    queries, keys, values = cut(query, blocks), cut(key, blocks), cut(value, blocks)
    contexts, weights = [spread(g) for g in cut(grad_context, blocks)], cut(probs, blocks)
    grad_probs = stack_rows([dot_nt(g, v) for g, v in zip(contexts, values)])
    grad_value = stack_rows([dot_tn(p, g) for p, g in zip(weights, contexts)]).astype(BF)
    wide = probs.astype(F32)
    inner = jnp.sum(grad_probs * wide, axis=-1, keepdims=True)
    grad_scores = cut((wide * (grad_probs - inner) * SCALE).astype(BF), blocks)
    grad_query = stack_rows([gathered(dot_nn(s, k)) for s, k in zip(grad_scores, keys)])
    grad_key = stack_rows([dot_tn(s, spread(q)) for s, q in zip(grad_scores, queries)])
    return grad_query.astype(BF), grad_key.astype(BF), grad_value


def load_weight(pieces, weight, column=0):
    row = 0
    for piece in pieces:
        for part in range(piece.shape[1]):
            rows, columns = piece.shape[2:]
            weight[row : row + rows, column : column + columns] = piece[0, part]
            row += rows


def load_halves(pieces, weight):
    middle = len(pieces) // 2
    lower = pl.program_id(0) < pl.num_programs(0) // 2

    @pl.when(lower)
    def _():
        load_weight(pieces[:middle], weight)

    @pl.when(jnp.logical_not(lower))
    def _():
        load_weight(pieces[middle:], weight)


def store_pair(value, near, far, by_group=False):
    rows = near.shape[3]
    for high in range(2):
        for core, piece in enumerate((near, far)):
            for mid in range(2):
                row = (4 * high + 2 * core + mid) * rows
                spot = (high, 0, mid) if by_group else (high, mid, 0)
                piece[spot] = value[row : row + rows, :].astype(piece.dtype)


def wide_spots(place, piece, shard_rows):
    groups, _, _, streams = piece.shape[:4]
    inner = max(groups // 2, 1)
    row = 0
    for high in range(groups // inner):
        for core in range(2):
            for part in range(streams):
                for sub in range(inner):
                    group = (sub * (groups // inner) + high) ^ place[0, 0]
                    yield row, (group, core ^ place[0, 1], 0, part)
                    row += shard_rows


def load_wide(place, piece, kind, weight):
    rows = piece.shape[5]
    for row, spot in wide_spots(place, piece, rows):
        weight[row : row + rows, :] = piece[spot + (kind,)]


def store_wide(place, value, piece, kind):
    rows = piece.shape[5]
    for row, spot in wide_spots(place, piece, rows):
        piece[spot + (kind,)] = value[row : row + rows, :].astype(piece.dtype)


def partner_order(value):
    dim = value.shape[1]
    eighth = dim // 8
    row = lax.broadcasted_iota(jnp.int32, (dim, dim), 0)
    column = lax.broadcasted_iota(jnp.int32, (dim, dim), 1)
    same = jnp.ones((dim, dim), jnp.bool_)
    for border in range(2 * eighth, dim, 2 * eighth):
        same &= (row >= border) == (column >= border)
    pick = same & (jnp.abs(row - column) == eighth)
    return dot_nn(value, jnp.where(pick, 1.0, 0.0).astype(BF)).astype(BF)


def widen(value, blocks, rows):
    empty = jnp.zeros((rows - value.shape[0] // blocks, value.shape[1]), value.dtype)
    return stack_rows([part for block in cut(value, blocks) for part in (block, empty)])


def cross_forward_kernel(width, blocks, words, regions, stream, lang, vis, norm, *refs):
    first, second, refs = refs[:8], refs[8:16], refs[16:]
    own_one, other_one, lang_n, lang_r, vis_n, vis_r = refs[:6]
    lang_qkv, vis_qkv, lang_ctx, vis_ctx, lang_p, vis_p = refs[6:12]
    weight, lang_acc, vis_acc = refs[12:]
    load_weight(first, weight)
    load_weight(second, weight, first[0].shape[3])
    step = pl.program_id(0)

    @pl.when(step == 0)
    def _():
        lang_acc[...] = lang[...].astype(F32)
        vis_acc[...] = vis[...].astype(F32)

    full = weight[...]
    in_part, out_part = full[:, : 3 * width], full[:, 3 * width :]
    lang_triple = dot_nn(lang[...], in_part).astype(BF)
    vis_triple = dot_nn(vis[...], in_part).astype(BF)
    lang_qkv[0] = lang_triple
    vis_qkv[0] = vis_triple
    lang_query, lang_key, lang_value = thirds(lang_triple, width)
    vis_query, vis_key, vis_value = thirds(vis_triple, width)
    heads = width // HEAD_DIM
    lang_block, vis_block = lang.shape[0] // blocks, vis.shape[0] // blocks
    lang_mask = same_item((lang_block, vis_block), words, regions, heads)
    vis_mask = same_item((vis_block, lang_block), regions, words, heads)
    for query, key, value, probs_ref, ctx_ref, acc, mask in (
        (lang_query, vis_key, vis_value, lang_p, lang_ctx, lang_acc, lang_mask),
        (vis_query, lang_key, lang_value, vis_p, vis_ctx, vis_acc, vis_mask),
    ):
        probs, context = attend(query, key, value, mask, blocks)
        probs_ref[0] = probs
        ctx_ref[0] = context
        acc[...] += dot_nt(context, out_part)

    @pl.when(step == pl.num_programs(0) - 1)
    def _():
        ones = []
        for acc, n_ref, r_ref in ((lang_acc, lang_n, lang_r), (vis_acc, vis_n, vis_r)):
            out, normed, inverse = norm_forward(acc[...], norm[0:1, :], norm[1:2, :])
            ones.append(out.astype(BF))
            n_ref[...] = normed
            r_ref[...] = inverse
        lang_one, vis_one = widen(ones[0], blocks, vis_block), ones[1]
        is_vis = stream[0, 0] == 1
        own_one[...] = jnp.where(is_vis, vis_one, lang_one)
        other_one[...] = partner_order(jnp.where(is_vis, lang_one, vis_one))


def self_forward_step(width, blocks, length, rows, pieces, weight, qkv, ctx, probs_ref):
    load_weight(pieces, weight)
    full = weight[...]
    in_part, out_part = full[:, : 3 * width], full[:, 3 * width :]
    triple = dot_nn(rows[...], in_part).astype(BF)
    qkv[0] = triple
    block = rows.shape[0] // blocks
    mask = same_item((block, block), length[0, 0], length[0, 0], width // HEAD_DIM)
    probs, context = attend(*thirds(triple, width), mask, blocks)
    probs_ref[0] = probs
    ctx[0] = context
    return dot_nt(context, out_part)


def self_first_kernel(width, blocks, length, own, other, *refs):
    pieces, (acc, qkv, ctx, probs, weight, rows) = refs[:4], refs[4:]

    @pl.when(pl.program_id(0) == 0)
    def _():
        rows[...] = stack_rows([own[...], other[...]])
        acc[...] = rows[...].astype(F32)

    acc[...] += self_forward_step(width, blocks, length, rows, pieces, weight, qkv, ctx, probs)


def self_second_kernel(width, blocks, length, own, other, norm, summed, *refs):
    pieces, refs = refs[:4], refs[7:]
    two, n_ref, r_ref, qkv, ctx, probs, weight, acc, rows = refs
    step = pl.program_id(0)

    @pl.when(step == 0)
    def _():
        rows[...] = stack_rows([own[...], other[...]])
        acc[...] = summed[...]

    acc[...] += self_forward_step(width, blocks, length, rows, pieces, weight, qkv, ctx, probs)

    @pl.when(step == pl.num_programs(0) - 1)
    def _():
        out, normed, inverse = norm_forward(acc[...], norm[0:1, :], norm[1:2, :])
        two[...] = out.astype(BF)
        n_ref[...] = normed
        r_ref[...] = inverse


def feed_kernel(place, rows, normed_two, inverse, cot, norm, piece, *refs):
    three, grads, down_ref, self_gain, self_shift, feed_gain, feed_shift, refs = refs[:7] + (refs[7:],)
    weight_in, weight_out, active, slope, acc, branch, branch_turned, turned = refs
    step, groups = pl.program_id(0), pl.num_programs(0) // 2
    group = lax.rem(step, groups)

    @pl.when(step == 0)
    def _():
        acc[...] = normed_two[...] * norm[0:1, :] + norm[1:2, :]
        turned[...] = rows[...].T

    @pl.when(step < groups)
    def _():
        load_wide(place, piece, 0, weight_in.at[group])
        load_wide(place, piece, 1, weight_out.at[group])
        hidden = dot_nn(rows[...], weight_in[group])
        normal = 0.5 * (1.0 + lax.erf(hidden * 0.7071067811865476))
        slopes = normal + hidden * jnp.exp(-0.5 * hidden * hidden) * 0.3989422804014327
        actives = (hidden * normal).astype(BF)
        active[group] = actives
        slope[group] = slopes.astype(BF)
        acc[...] += dot_nt(actives, weight_out[group])

    @pl.when(step == groups - 1)
    def _():
        gain = norm[2:3, :]
        out, normed, inverse_three = norm_forward(acc[...], gain, norm[3:4, :])
        three[...] = out.astype(BF)
        inward, gain_term, shift_term = norm_backward(
            cot[...].astype(F32), gain, normed, inverse_three
        )
        acc[...] = inward
        branch[...] = inward.astype(BF)
        branch_turned[...] = inward.astype(BF).T
        feed_gain[...] = gain_term
        feed_shift[...] = shift_term

    @pl.when(step >= groups)
    def _():
        store_wide(place, dot_nn(branch_turned[...], active[group]), grads, 1)
        grad_active = dot_nn(branch[...], weight_out[group])
        grad_hidden = (grad_active * slope[group].astype(F32)).astype(BF)
        store_wide(place, dot_nn(turned[...], grad_hidden), grads, 0)
        acc[...] += dot_nt(grad_hidden, weight_in[group])

    @pl.when(step == 2 * groups - 1)
    def _():
        down, gain_term, shift_term = norm_backward(
            acc[...], norm[0:1, :], normed_two[...], inverse[...]
        )
        down_ref[...] = down
        self_gain[...] = gain_term
        self_shift[...] = shift_term


def self_backward_kernel(width, blocks, inward, own, other, qkv, ctx, probs, *refs):
    pieces, near, far, refs = refs[:8], refs[8], refs[9], refs[10:]
    down_own, down_other, weight, acc, branch, turned, branch_turned = refs
    load_halves(pieces, weight)
    step = pl.program_id(0)

    @pl.when(step == 0)
    def _():
        acc[...] = inward[...]
        gradient = inward[...].astype(BF)
        branch[...] = gradient
        branch_turned[...] = gradient.T
        turned[...] = stack_rows([own[...], other[...]]).T

    full = weight[...]
    in_part, out_part = full[:, : 3 * width], full[:, 3 * width :]
    grad_context = dot_nn(branch[...], out_part).astype(BF)
    grads_of = attend_back(*thirds(qkv[0], width), probs[0], grad_context, blocks)
    grad_triple = jnp.concatenate(grads_of, axis=1)
    in_grad = dot_nn(turned[...], grad_triple).astype(BF)
    out_grad = dot_nn(branch_turned[...], ctx[0]).astype(BF)
    store_pair(jnp.concatenate([in_grad, out_grad], axis=1), near, far, True)
    acc[...] += dot_nt(grad_triple, in_part)

    @pl.when(step == pl.num_programs(0) - 1)
    def _():
        slot = own.shape[0]
        down_own[...] = acc[:slot].astype(BF)
        down_other[...] = partner_order(acc[slot:].astype(BF))


def cross_backward_kernel(
    width,
    blocks,
    stream,
    own_up,
    other_up,
    lang,
    vis,
    lang_n,
    lang_r,
    vis_n,
    vis_r,
    norm,
    order,
    source,
    targets,
    *refs,
):
    lang_qkv, vis_qkv, lang_ctx, vis_ctx, lang_p, vis_p = refs[:6]
    first, second, refs = refs[6:14], refs[14:22], refs[22:]
    near, far, lang_out, image_out, gain_ref, shift_ref = refs[:6]
    weight, lang_acc, vis_acc, lang_branch, vis_branch, turned, branch_turned = refs[6:]
    load_weight(first, weight)
    load_weight(second, weight, first[0].shape[3])
    step = pl.program_id(0)

    @pl.when(step == 0)
    def _():
        is_vis = stream[0, 0] == 1
        own, other = own_up[...].astype(F32), other_up[...].astype(F32)
        lang_block = lang.shape[0] // blocks
        lang_up = cut(jnp.where(is_vis, other, own), blocks)
        lang_up = stack_rows([block[:lang_block] for block in lang_up])
        vis_up = jnp.where(is_vis, own, other)
        gain_total, shift_total = 0.0, 0.0
        for up, n_ref, r_ref, acc, branch in (
            (lang_up, lang_n, lang_r, lang_acc, lang_branch),
            (vis_up, vis_n, vis_r, vis_acc, vis_branch),
        ):
            inward, gain_term, shift_term = norm_backward(
                up, norm[0:1, :], n_ref[...], r_ref[...]
            )
            acc[...] = inward
            branch[...] = inward.astype(BF)
            gain_total += gain_term
            shift_total += shift_term
        gain_ref[...] = gain_total
        shift_ref[...] = shift_total
        turned[...] = stack_rows([lang[...], vis[...]]).T
        branch_turned[...] = stack_rows([lang_branch[...], vis_branch[...]]).T

    full = weight[...]
    in_part, out_part = full[:, : 3 * width], full[:, 3 * width :]
    lang_gc = dot_nn(lang_branch[...], out_part).astype(BF)
    vis_gc = dot_nn(vis_branch[...], out_part).astype(BF)
    lang_query, lang_key, lang_value = thirds(lang_qkv[0], width)
    vis_query, vis_key, vis_value = thirds(vis_qkv[0], width)
    lang_dq, vis_dk, vis_dv = attend_back(
        lang_query, vis_key, vis_value, lang_p[0], lang_gc, blocks
    )
    vis_dq, lang_dk, lang_dv = attend_back(
        vis_query, lang_key, lang_value, vis_p[0], vis_gc, blocks
    )
    lang_grad = jnp.concatenate([lang_dq, lang_dk, lang_dv], axis=1)
    vis_grad = jnp.concatenate([vis_dq, vis_dk, vis_dv], axis=1)
    in_grad = dot_nn(turned[...], stack_rows([lang_grad, vis_grad]))
    out_grad = dot_nn(branch_turned[...], stack_rows([lang_ctx[0], vis_ctx[0]]))
    grad = jnp.concatenate([in_grad.astype(BF), out_grad.astype(BF)], axis=1)
    store_pair(grad, near, far)
    lang_acc[...] += dot_nt(lang_grad, in_part)
    vis_acc[...] += dot_nt(vis_grad, in_part)

    @pl.when(step == pl.num_programs(0) - 1)
    def _():
        lang_out[...] = dot_nt(lang_acc[...].astype(BF), order[...])
        chooser = jnp.where(source[...] == targets[...], 1.0, 0.0).astype(BF)
        image = dot_tn(chooser, vis_acc[...].astype(BF)).astype(BF)
        image_out[...] = dot_nt(image, order[...]).astype(BF)


def store_step(state, clip, outs):
    new = adamw_step(*state, MATRIX_RATE, clip)
    for (ref, place), value in zip(outs, new[:4] + (new[3], new[4])):
        ref[place] = value.astype(ref.dtype)


def prepare_kernel(norms, kept, sent, self_low, self_theirs, feed_sum, feed_theirs, sums):
    home = kept[...].astype(F32) + sent[...].astype(F32)
    squares = jnp.sum(home * home, keepdims=True)[0]
    for value in (self_low[0], self_theirs[...]):
        wide = value.astype(F32)
        squares += jnp.sum(wide * wide, keepdims=True)
    for kind in range(feed_theirs.shape[0]):
        for value in (feed_sum[0, kind], feed_theirs[kind]):
            wide = value.astype(F32)
            squares += jnp.sum(wide * wide, keepdims=True)
    count = norms.shape[0]
    sums[:count, :] = norms[...]
    sums[count:, :] = jnp.broadcast_to(squares, (1, norms.shape[1]))


def step_kernel(
    width, stream, sums, theirs, kept, sent, self_low, self_theirs, feed_sum, feed_theirs, *refs
):
    ins, outs, feed_in, feed_out, norm_in = (refs[4 * i : 4 * i + 4] for i in range(5))
    refs = refs[20:]
    step = pl.program_id(0)
    total = sums[...] + theirs[...]
    norm_grad = total[:-1]
    squares = jnp.sum(norm_grad * norm_grad, keepdims=True) + total[-1:, 0:1]
    grad_norm = jnp.sqrt(squares)
    clip = CLIP_NORM / jnp.maximum(grad_norm, CLIP_NORM)
    refs[-1][...] = grad_norm
    for place in range(norm_in[0].shape[0]):
        state = [ref[place] for ref in norm_in]
        new = adamw_step(norm_grad[2 * place : 2 * place + 2], *state, NORM_RATE, clip)
        for ref, value in zip(refs[24:29], new):
            ref[place] = value
    is_vis = stream[0, 0] == 1

    def by_stream(mine, other):
        mine, other = mine.astype(F32), other.astype(F32)
        return jnp.where(is_vis, other, mine), jnp.where(is_vis, mine, other)

    home = kept[0].astype(F32) + sent[0].astype(F32)
    one, two = by_stream(self_low[0], self_theirs[...])
    grad = jnp.where(step == 0, home, jnp.where(step == 1, one, two))
    for kind in range(3):
        part = grad[:, kind * width : (kind + 1) * width]
        store_step([part] + [ref[0, kind] for ref in ins], clip, [(r, (0, kind)) for r in refs[:6]])
    part = grad[:, 3 * width :].T
    store_step([part] + [ref[0] for ref in outs], clip, [(r, 0) for r in refs[6:12]])
    for kind, state_in, first in ((0, feed_in, 12), (1, feed_out, 18)):
        for place, part in enumerate(by_stream(feed_sum[0, kind], feed_theirs[kind])):
            state = [part] + [ref[place] for ref in state_in]
            store_step(state, clip, [(r, place) for r in refs[first : first + 6]])


def whole(shape):
    return pl.BlockSpec(shape, lambda m: (0,) * len(shape))


def per_step(shape):
    rest = (0,) * (len(shape) - 1)
    return pl.BlockSpec((1,) + tuple(shape[1:]), lambda m: (m,) + rest)


def part_of(shape, pick):
    rest = (0,) * (len(shape) - 1)
    return pl.BlockSpec((1,) + tuple(shape[1:]), lambda m: (pick(m),) + rest)


def group_of(shape, pick):
    block = (shape[0], shape[1], 1) + tuple(shape[3:])
    return pl.BlockSpec(block, lambda m: (0, 0, pick(m), 0, 0, 0, 0))


def call(kernel, steps, ins, outs, scratch, name, flops, aliases=()):
    spec = {
        "whole": lambda s: whole(s),
        "step": lambda s: per_step(s),
        "early": lambda s: group_of(s, lambda m: jnp.minimum(m, s[2] - 1)),
        "late": lambda s: group_of(s, lambda m: jnp.maximum(m - s[2], 0)),
        "low": lambda s: part_of(s, lambda m: jnp.minimum(m, s[0] - 1)),
        "high": lambda s: part_of(s, lambda m: jnp.maximum(m - s[0], 0)),
        "rows": lambda s: pl.BlockSpec(
            tuple(s[:-2]) + (s[-2] // steps, s[-1]), lambda m: (0,) * (len(s) - 2) + (m, 0)
        ),
        "pair": lambda s: pl.BlockSpec(
            tuple(s[:2]) + (1,) + tuple(s[3:]), lambda m: (0, 0, m, 0, 0)
        ),
        "groups": lambda s: pl.BlockSpec(
            (s[0], 1) + tuple(s[2:]), lambda m: (0, m, 0, 0, 0)
        ),
        "upper": lambda s: part_of(s, lambda m: m + s[0] // 2),
        "kept": lambda s: pl.BlockSpec(memory_space=pl.ANY),
        "scalar": lambda s: pl.BlockSpec(memory_space=pltpu.SMEM),
    }
    moved = sum(a.size * a.dtype.itemsize for _, a in ins)
    moved += sum(math.prod(s) * jnp.dtype(t).itemsize for _, s, t in outs)
    return pl.pallas_call(
        kernel,
        grid=(steps,),
        in_specs=[spec[kind](a.shape) for kind, a in ins],
        out_specs=[spec[kind](s) for kind, s, _ in outs],
        out_shape=[jax.ShapeDtypeStruct(s, t) for _, s, t in outs],
        scratch_shapes=[pltpu.VMEM(s, t) for s, t in scratch],
        input_output_aliases=dict(aliases),
        compiler_params=pltpu.CompilerParams(
            vmem_limit_bytes=VMEM_LIMIT, dimension_semantics=("arbitrary",)
        ),
        cost_estimate=pl.CostEstimate(flops=flops, bytes_accessed=moved, transcendentals=0),
        name=name,
    )(*[a for _, a in ins])


def swap_dp(value, bit):
    axis, place = (("core", 0), ("stream", 0), ("dq", bit - 2))[min(bit, 2)]
    count = lax.axis_size(axis)
    return lax.ppermute(value, axis, [(i, i ^ (1 << place)) for i in range(count)])


def swap_mp(value, bit):
    count = lax.axis_size("mp")
    return lax.ppermute(value, "mp", [(i, i ^ (1 << bit)) for i in range(count)])


def after(value, *others):
    flat, tree = jax.tree.flatten(value)
    kept = lax.optimization_barrier((flat, jax.tree.leaves(others)))[0]
    return jax.tree.unflatten(tree, kept)


def together(*values):
    return lax.optimization_barrier(values)


def swap_mask(value, axis, mask):
    count = lax.axis_size(axis)
    return lax.ppermute(value, axis, [(i, i ^ mask) for i in range(count)])


def sum_up(value):
    count = lax.axis_size("mp")
    mask = 1
    while mask < count:
        if 2 * mask < count:
            theirs = [swap_mask(value, "mp", mask * k) for k in (1, 2, 3)]
            value = (value + theirs[0]) + (theirs[1] + theirs[2])
            mask *= 4
        else:
            value += swap_mask(value, "mp", mask)
            mask *= 2
    both = ("dq", "stream")
    count = lax.axis_size(both)
    mask = 1
    while mask < count:
        if 2 * mask < count:
            theirs = [swap_mask(value, both, mask * k) for k in (1, 2, 3)]
            value = (value + theirs[0]) + (theirs[1] + theirs[2])
            mask *= 4
        else:
            value += swap_mask(value, both, mask)
            mask *= 2
    return value, swap_dp(value, 0)


def extra_bits():
    return range(3, 2 + int(math.log2(lax.axis_size("dq"))))


def mp_bits():
    return range(int(math.log2(lax.axis_size("mp"))))


def gather_mp(current):
    for bit in reversed(mp_bits()):
        current = jnp.concatenate([current, swap_mp(current, bit)], axis=0)
    return current


def gather_extra(current):
    for bit in extra_bits():
        current = jnp.concatenate([current, swap_dp(current, bit)], axis=2)
    return current


def scatter_mp(current):
    for bit in mp_bits():
        half = current.shape[0] // 2
        current = added(current[:half], swap_mp(current[half:], bit))
    return current


def scatter_extra(current):
    for bit in reversed(extra_bits()):
        low, high = jnp.split(current, 2, axis=-2)
        current = added(low, swap_dp(high, bit))
    return current


def added(mine, theirs):
    return (mine.astype(F32) + theirs.astype(F32)).astype(BF)


def grow(found, place, bit):
    for key in list(found):
        new = list(key)
        new[place] = 1
        found[tuple(new)] = swap_dp(found[key], bit)


def shrink(found, place, bit):
    for key in [k for k in found if k[place] == 0]:
        far = list(key)
        far[place] = 1
        found[key] = added(found[key], swap_dp(found.pop(tuple(far)), bit))


def home_list(found):
    return [found[(hi, mid, lo)] for hi in (0, 1) for lo in (0, 1) for mid in (0, 1)]


def stream_list(found):
    return [found[(hi, lo)] for hi in (0, 1) for lo in (0, 1)]


def home_keys(arrays):
    return {(i >> 2, i & 1, (i >> 1) & 1): a for i, a in enumerate(arrays)}


def stream_keys(arrays):
    return {(i >> 1, i & 1): a for i, a in enumerate(arrays)}


def adamw_step(gradient, moment, square, weight, average, rate, clip_scale):
    average_decay = min(AVERAGE_CEILING, (1.0 + STEP) / (10.0 + STEP))
    clipped = gradient * clip_scale
    moment_new = BETA_FIRST * moment + (1.0 - BETA_FIRST) * clipped
    square_new = BETA_SECOND * square + (1.0 - BETA_SECOND) * clipped * clipped
    corrected = moment_new / (1.0 - BETA_FIRST**STEP)
    denominator = jnp.sqrt(square_new / (1.0 - BETA_SECOND**STEP)) + ADAM_EPS
    weight_new = weight - rate * (corrected / denominator + WEIGHT_DECAY * weight)
    average_new = average_decay * average + (1.0 - average_decay) * weight_new
    return (clipped, moment_new, square_new, weight_new, average_new)


def pad_rows(block, rows):
    return jnp.pad(block, ((0, rows - block.shape[0]), (0, 0)))


def local(
    language,
    images,
    counts,
    language_cot,
    vision_cot,
    attn_in_weight,
    attn_in_moment,
    attn_in_square,
    attn_in_average,
    attn_out_weight,
    attn_out_moment,
    attn_out_square,
    attn_out_average,
    ffn_in_weight,
    ffn_in_moment,
    ffn_in_square,
    ffn_in_average,
    ffn_out_weight,
    ffn_out_moment,
    ffn_out_square,
    ffn_out_average,
    norm_weight,
    norm_moment,
    norm_square,
    norm_average,
):
    n_dp, n_mp = lax.axis_size(DP), lax.axis_size("mp")
    me = lax.axis_index(DP)
    stream = (me >> 1) & 1
    is_vis = stream == 1
    own_items, words, dim = language.shape
    regions = images.shape[1]
    blocks = own_items // GROUP
    lang_block, vis_block = (-(-GROUP * rows // 16) * 16 for rows in (words, regions))
    lang_pad, slot = blocks * lang_block, blocks * vis_block
    total = 2 * slot
    shard_rows = attn_in_weight.shape[1]
    width = attn_in_weight.shape[3]
    units = ffn_in_weight.shape[2]
    heads = width // HEAD_DIM
    half = 2 * width
    eighth = dim // 8

    def mine_first(pair):
        return jnp.where(is_vis, pair[1], pair[0]), jnp.where(is_vis, pair[0], pair[1])

    attn_shards = [
        jnp.concatenate(
            [attn_in_weight[b].reshape(shard_rows, 3 * width), attn_out_weight[b].T], axis=1
        ).astype(BF)[None, None]
        for b in range(3)
    ]
    def pair_up(shards, *pins):
        own, other = mine_first(shards)
        return jnp.concatenate([own, swap_dp(after(other, *pins), 1)], axis=1)

    halves = [attn_shards[0][..., c : c + half] for c in (0, half)]
    self_pair = pair_up(attn_shards[1:])
    for bit in reversed(mp_bits()):
        halves = [jnp.concatenate([h, swap_mp(h, bit)], axis=0) for h in halves]
        if bit == mp_bits()[-1]:
            feed_own, feed_other = mine_first(
                [jnp.stack([ffn_in_weight[s].astype(BF), ffn_out_weight[s].T.astype(BF)]) for s in range(2)]
            )
            feed_pair = jnp.stack([feed_own, swap_dp(feed_other, 1)])
            feed_w = lax.all_gather(after(feed_pair, halves), ("dq", "core", "mp"), axis=0)
            feed_w = feed_w.reshape((n_dp // 4, 2, n_mp) + feed_pair.shape)
    first, second = ({(0, 0, 0): gather_extra(h)} for h in halves)

    def gather_step(current, index):
        return jnp.concatenate([current, swap_mp(current, mp_bits()[-1 - index])], axis=0)

    n_bits = len(mp_bits())
    self_low = self_pair
    for index in range(n_bits - 1):
        self_low = gather_step(self_low, index)
    grow(first, 0, 2)
    grow(second, 1, 1)

    place = jnp.arange(dim, dtype=jnp.int32)
    block = place // shard_rows
    sub, high = block % (n_dp // 8), block // (n_dp // 8)
    relative = 8 * sub + 4 * (high >> 2) + ((high >> 1) & 1) + 2 * (high & 1)
    origin = (relative ^ me) * shard_rows + place % shard_rows
    order = (place[:, None] == origin[None, :]).astype(BF)

    def to_order(value):
        return dot_nn(value, order).astype(BF)

    def from_order(value, precision=None):
        return lax.dot_general(
            value, order, (((1,), (1,)), ((), ())), preferred_element_type=F32, precision=precision
        )

    norm_ordered = lax.dot_general(
        norm_weight.reshape(-1, dim),
        order.astype(F32),
        (((1,), (0,)), ((), ())),
        precision=HIGHEST,
        preferred_element_type=F32,
    ).reshape(norm_weight.shape)
    norm_cross = norm_ordered[:, 0]
    norm_self = jnp.where(is_vis, norm_ordered[:, 2], norm_ordered[:, 1])
    norm_feed = jnp.where(is_vis, norm_ordered[:, 4], norm_ordered[:, 3])
    norm_pair = jnp.concatenate([norm_self, norm_feed], axis=0)

    def in_blocks(value, rows, target):
        value = value.reshape(blocks, rows, dim)
        value = jnp.pad(value, ((0, 0), (0, target - rows), (0, 0)))
        return value.reshape(blocks * target, dim)

    def out_of_blocks(value, rows):
        return value.reshape(blocks, -1, dim)[:, :rows].reshape(blocks * rows, dim)

    lang_rows, vis_rows = GROUP * words, GROUP * regions
    first_item = lax.axis_index("mp") * own_items
    bounds = jnp.cumsum(counts[0])
    positions = first_item + jnp.arange(own_items, dtype=jnp.int32)
    item_image = jnp.sum((bounds[None, :] <= positions[:, None]).astype(jnp.int32), axis=1)
    region = jnp.arange(regions, dtype=jnp.int32)
    row_source = (item_image[:, None] * regions + region[None, :]).reshape(blocks, vis_rows) + 1
    row_source = jnp.pad(row_source, ((0, 0), (0, vis_block - vis_rows))).reshape(slot, 1)
    image_count = images.shape[0] * regions
    picker = (row_source == 1 + jnp.arange(image_count, dtype=jnp.int32)[None, :]).astype(BF)
    lang = to_order(in_blocks(language, lang_rows, lang_block))
    image_rows = to_order(images.reshape(-1, dim))
    vis = dot_nn(picker, image_rows).astype(BF)

    lang_cot = in_blocks(language_cot, lang_rows, vis_block)
    vis_cot = in_blocks(vision_cot, vis_rows, vis_block)
    cot_own, cot_other = mine_first((lang_cot, vis_cot))

    length = jnp.where(is_vis, regions, words).astype(jnp.int32).reshape(1, 1)

    first, second = after((first, second), lang, vis)
    grow(first, 1, 1)
    grow(second, 0, 2)
    self_low = {(0, 0): gather_extra(self_low)}
    self_high = {(0, 0): swap_mp(self_low[(0, 0)], 0)}
    grow(first, 2, 0)
    grow(second, 2, 0)
    pieces = lambda arrays: [("step", a) for a in arrays]
    which = stream.astype(jnp.int32).reshape(1, 1)
    ins = [("scalar", which)] + [("whole", a) for a in (lang, vis, norm_cross)]
    outs = [("whole", (slot, dim), BF)] * 2
    for rows in (lang_pad, slot):
        outs += [("whole", (rows, dim), F32), ("whole", (rows, 1), F32)]
    outs += [("step", (n_mp, rows, 3 * width), BF) for rows in (lang_pad, slot)]
    outs += [("step", (n_mp, rows, width), BF) for rows in (lang_pad, slot)]
    outs += [
        ("step", (n_mp, heads * lang_pad, vis_block), BF),
        ("step", (n_mp, heads * slot, lang_block), BF),
    ]
    both = lang_pad + slot
    cross_w = home_list(first) + home_list(second)
    cross_w = after(cross_w, self_low)
    grow(self_low, 0, 2)
    found = call(
        functools.partial(cross_forward_kernel, width, blocks, words, regions),
        n_mp,
        ins + pieces(cross_w),
        outs,
        [((dim, 4 * width), BF), ((lang_pad, dim), F32), ((slot, dim), F32)],
        "cross_forward",
        12 * both * dim * 4 * width * n_mp,
    )
    own_one, other_one, lang_n, lang_r, vis_n, vis_r = found[:6]
    cross_saved = found[6:]

    other_one = swap_dp(other_one, 1)
    self_high, self_low, cot_other = after((self_high, self_low, cot_other), other_one)
    grow(self_high, 0, 2)
    grow(self_low, 1, 0)
    half_groups = n_mp // 2
    saved = [
        (n_mp, total, 3 * width),
        (n_mp, total, width),
        (n_mp, heads * total, vis_block),
    ]
    first_half = call(
        functools.partial(self_first_kernel, width, 2 * blocks),
        half_groups,
        [("scalar", length)]
        + [("whole", a) for a in (own_one, other_one)]
        + [("step", a) for a in stream_list(self_low)],
        [("whole", (total, dim), F32)] + [("step", a, BF) for a in saved],
        [((dim, 4 * width), BF), ((total, dim), BF)],
        "self_first",
        6 * total * dim * 4 * width * n_mp,
    )
    self_high, cot_theirs = after((self_high, swap_dp(cot_other, 1)), first_half[0])
    grow(self_high, 1, 0)
    self_pieces = [("low", a) for a in stream_list(self_low)]
    self_pieces += [("high", a) for a in stream_list(self_high)]
    rows_two, normed_two, inverse_two, self_qkv, self_ctx, self_probs = call(
        functools.partial(self_second_kernel, width, 2 * blocks),
        half_groups,
        [("scalar", length)]
        + [("whole", a) for a in (own_one, other_one, norm_self, first_half[0])]
        + [("step", a) for a in stream_list(self_high)]
        + [("kept", a) for a in first_half[1:]],
        [("whole", (total, dim), BF), ("whole", (total, dim), F32), ("whole", (total, 1), F32)]
        + [("upper", a, BF) for a in saved],
        [((dim, 4 * width), BF), ((total, dim), F32), ((total, dim), BF)],
        "self_second",
        6 * total * dim * 4 * width * n_mp,
        [(9 + i, 3 + i) for i in range(3)],
    )
    cot = to_order(jnp.concatenate([cot_own, cot_theirs], axis=0))
    spot = jnp.stack([me >> 2, me & 1]).astype(jnp.int32).reshape(1, 2)

    whole_row = ("whole", (1, dim), F32)
    rows_three, feed_g, inward, self_gain, self_shift, feed_gain, feed_shift = call(
        feed_kernel,
        2 * n_mp,
        [("scalar", spot)]
        + [("whole", a) for a in (rows_two, normed_two, inverse_two, cot, norm_pair)]
        + [("early", feed_w)],
        [("whole", (total, dim), BF), ("late", feed_w.shape, BF), ("whole", (total, dim), F32)]
        + [whole_row] * 4,
        [((n_mp, dim, units), BF)] * 2
        + [((n_mp, total, units), BF)] * 2
        + [((total, dim), F32), ((total, dim), BF), ((dim, total), BF), ((dim, total), BF)],
        "feed",
        24 * total * dim * units * n_mp,
    )

    feed_sum = lax.psum_scatter(
        (feed_g * (1 + 0 * (me < 0)).astype(BF)).reshape((-1,) + feed_pair.shape), ("dq", "core", "mp"), scatter_dimension=0, tiled=True
    )[0]

    def core_step(found, *pins):
        theirs = [swap_dp(found[(hi, 1)], 0) for hi in (0, 1)]
        return [found[(hi, 0)] for hi in (0, 1)], after(theirs, *pins)

    def split(mine, theirs):
        middle = mine.shape[0] // 2
        return added(mine[:middle], theirs[:middle]), added(mine[middle:], theirs[middle:])

    def send_mp(parts, bit):
        return [(keep, swap_mp(far, bit)) for keep, far in parts]

    found = call(
        functools.partial(self_backward_kernel, width, 2 * blocks),
        n_mp,
        [("whole", a) for a in (inward, own_one, other_one)]
        + [("step", a) for a in (self_qkv, self_ctx, self_probs)]
        + self_pieces,
        [("groups", (2, n_mp, 2, eighth, 4 * width), BF)] * 2 + [("whole", (slot, dim), BF)] * 2,
        [((dim, 4 * width), BF), ((total, dim), F32), ((total, dim), BF)] + [((dim, total), BF)] * 2,
        "self_backward",
        20 * total * dim * 4 * width * n_mp,
    )
    self_near, self_far = found[:2]
    own_up, other_up = found[2:]
    other_up = swap_dp(other_up, 1)
    self_far = swap_dp(self_far, 0)
    self_sums = [scatter_extra(added(self_near[hi], self_far[hi])) for hi in (0, 1)]
    own_up = after(own_up, self_sums)
    place_mp = lax.axis_index("mp")
    part = -(-image_count // n_mp // 16) * 16
    index = jnp.arange(n_mp, dtype=jnp.int32)
    far = sum(((index >> b) & 1) << (n_bits - 1 - b) for b in range(n_bits))
    rows = ((far ^ place_mp)[:, None] * part + jnp.arange(part, dtype=jnp.int32)[None, :]).reshape(1, -1)
    found = call(
        functools.partial(cross_backward_kernel, width, blocks),
        n_mp,
        [("scalar", which)]
        + [("whole", a) for a in (own_up, other_up, lang, vis)]
        + [("whole", a) for a in (lang_n, lang_r, vis_n, vis_r, norm_cross)]
        + [("whole", a) for a in (order, row_source, 1 + rows)]
        + [("step", a) for a in cross_saved]
        + pieces(cross_w),
        [("pair", (2, 2, n_mp, eighth, 4 * width), BF)] * 2
        + [
            ("whole", (lang_pad, dim), F32),
            ("whole", (n_mp * part, dim), BF),
            ("whole", (1, dim), F32),
            ("whole", (1, dim), F32),
        ],
        [
            ((dim, 4 * width), BF),
            ((lang_pad, dim), F32),
            ((slot, dim), F32),
            ((lang_pad, dim), BF),
            ((slot, dim), BF),
            ((dim, both), BF),
            ((dim, both), BF),
        ],
        "cross_backward",
        20 * both * dim * 4 * width * n_mp,
    )
    near, far, lang_back, image_term, cross_gain, cross_shift = found

    def parts(value):
        middle = value.shape[0] // 2
        return value[:middle], value[middle:]

    def total_of(*terms):
        return functools.reduce(jnp.add, [t.astype(F32) for t in terms]).astype(BF)

    self_kept = self_sums[0]
    self_far = swap_dp(self_sums[1][1:], 2)
    late = together(near, far, lang_back, image_term, self_far)
    near, far, lang_back, image_term, self_far = late
    far = swap_dp(far, 0)
    self_sent = total_of(self_kept[2:], self_far[1:])
    left, right = (slice(c, c + half) for c in (0, half))
    first = [added(near[:, mid, ..., left], far[:, mid, ..., left]) for mid in (0, 1)]
    second = [added(near[hi, ..., right], far[hi, ..., right]) for hi in (0, 1)]
    first, second, self_sent, lang_back = together(first, second, self_sent, lang_back)

    first_far, second_far, self_sent = swap_dp(first[1], 1), swap_dp(second[1], 2), swap_mp(self_sent, 0)
    late = together(first, second, first_far, second_far, self_sent, rows_three, image_term)
    first, second, first_far, second_far, self_sent, rows_three, image_term = late
    first = [added(first[0][i], first_far[i]) for i in (0, 1)]
    second = [added(second[0][i], second_far[i]) for i in (0, 1)]
    first, second, self_sent = together(first, second, self_sent)
    self_one = total_of(self_kept[1], self_far[0], self_sent[1])

    first_far, second_far = swap_dp(first[1], 2), swap_dp(second[1], 1)
    self_ones = [swap_mp(self_one[1:], 1)]
    self_near = swap_dp(self_sums[1][:1], 2)
    late = together(first[0], second[0], first_far, second_far, self_ones, self_near, image_term)
    first, second, first_far, second_far, self_ones, self_near, image_term = late
    home = jnp.concatenate([added(first, first_far), added(second, second_far)], axis=-1)
    home = scatter_extra(home)
    self_low = total_of(self_kept[0], self_near[0], self_sent[0])

    kept, sent = parts(home)
    sent = swap_mp(sent, 0)
    self_ones = [swap_mp(after(self_one[:1], home), 1)] + self_ones
    image_kept, image_sent = parts(image_term.reshape(n_mp, part, dim))
    image_sent = swap_mp(image_sent, 0)
    late = together(kept, sent, self_low, self_ones, image_kept, image_sent)
    kept, sent, self_low, self_ones, image_kept, image_sent = late
    self_low = added(self_low, jnp.concatenate(self_ones, axis=0))
    home, image_term = added(kept, sent), added(image_kept, image_sent)

    kept, sent = parts(home)
    sent, theirs, feed_theirs = swap_mp(sent, 1), swap_dp(self_low[1], 1), swap_dp(feed_sum[1], 1)
    image_kept, image_sent = parts(image_term)
    image_sent = swap_mp(image_sent, 1)
    late = together(kept, sent, self_low, theirs, feed_theirs, image_kept, image_sent)
    kept, sent, self_low, theirs, feed_theirs, image_kept, image_sent = late
    image_term = added(image_kept, image_sent)

    final = from_order(rows_three).astype(BF)
    final_other = after(swap_dp(final[slot:], 1), kept)
    language_out = out_of_blocks(jnp.where(is_vis, final_other, final[:slot]), lang_rows)
    vision_out = out_of_blocks(jnp.where(is_vis, final[:slot], final_other), vis_rows)

    language_grad = out_of_blocks(lang_back, lang_rows).reshape(language.shape)
    here = (jnp.arange(2, dtype=jnp.int32) == stream).astype(F32)[:, None, None]
    norm_partial = jnp.concatenate(
        [
            jnp.concatenate([cross_gain, cross_shift], axis=0)[None],
            here * jnp.concatenate([self_gain, self_shift], axis=0)[None],
            here * jnp.concatenate([feed_gain, feed_shift], axis=0)[None],
        ],
        axis=0,
    )
    norm_partial = from_order(norm_partial.reshape(-1, dim), HIGHEST)

    totals = [kept, sent, self_low, theirs]
    sums = call(
        prepare_kernel,
        1,
        [("whole", a) for a in [norm_partial] + totals + [feed_sum, feed_theirs]],
        [("whole", (norm_partial.shape[0] + 1, dim), F32)],
        [],
        "prepare",
        8 * dim * width,
    )[0]
    sums, their_sums = sum_up(sums)
    image_term = after(image_term, kept)
    for bit in reversed(mp_bits()):
        image_term = jnp.concatenate([image_term, swap_mp(image_term, bit)], axis=0)
    for b in range(n_bits):
        shape = (1 << b, 2, -1, part, dim)
        flipped = image_term.reshape(shape)[:, ::-1].reshape(image_term.shape)
        image_term = jnp.where((place_mp >> b) & 1 == 1, flipped, image_term)
    axes = tuple(reversed(range(n_bits))) + (n_bits, n_bits + 1)
    image_term = image_term.reshape((2,) * n_bits + (part, dim)).transpose(axes)
    image_grad = image_term.reshape(-1, dim)[:image_count].astype(F32).reshape(images.shape)

    kinds = [("step", t) for t in (F32, F32, F32, F32, BF, F32)]
    norm_in = [
        jnp.swapaxes(a, 0, 1)
        for a in (norm_moment, norm_square, norm_weight, norm_average)
    ]
    wide_in = [jnp.swapaxes(a, 1, 2) for a in (attn_in_moment, attn_in_square, attn_in_weight, attn_in_average)]
    wide_out = [attn_out_moment, attn_out_square, attn_out_weight, attn_out_average]
    feed_in = [ffn_in_moment, ffn_in_square, ffn_in_weight, ffn_in_average]
    feed_out = [
        jnp.swapaxes(a, 1, 2)
        for a in (ffn_out_moment, ffn_out_square, ffn_out_weight, ffn_out_average)
    ]
    by_rows = "rows" if shard_rows % 48 == 0 else "whole"
    stepped = call(
        functools.partial(step_kernel, width),
        3,
        [("scalar", which)]
        + [("whole", a) for a in [sums, their_sums] + totals]
        + [(by_rows, feed_sum), (by_rows, feed_theirs)]
        + [("step", a) for a in wide_in + wide_out]
        + [(by_rows, a) for a in feed_in + feed_out]
        + [("whole", a) for a in norm_in],
        [(k, wide_in[0].shape, t) for k, t in kinds]
        + [(k, wide_out[0].shape, t) for k, t in kinds]
        + [(by_rows, feed_in[0].shape, t) for k, t in kinds * 2]
        + [("whole", norm_in[0].shape, F32)] * 5
        + [("whole", (1, 1), F32)],
        [],
        "step",
        20 * 8 * dim * width,
    )
    stepped = [jnp.swapaxes(a, 1, 2) if i < 6 or 18 <= i < 24 else a for i, a in enumerate(stepped)]
    stepped[24:29] = [jnp.swapaxes(a, 0, 1) for a in stepped[24:29]]

    results = [
        language_out.reshape(language.shape),
        vision_out.reshape(vision_cot.shape),
        language_grad,
        image_grad,
    ]
    results += stepped[:-1]
    return tuple(results) + (stepped[-1][0, 0],)


def solution(mesh):
    shape = (mesh.shape["dp"] // 4, 2, 2, mesh.shape["mp"])
    mesh = Mesh(mesh.devices.reshape(shape), DP + ("mp",))
    rows = P(DP + ("mp",), None, None)
    attn_in, attn_out = P(None, DP, None, "mp"), P(None, "mp", DP)
    ffn_in, ffn_out = P(None, DP, "mp"), P(None, "mp", DP)
    in_specs = (rows, P(DP, None, None), P(DP, None), rows, rows)
    in_specs += (attn_in,) * 4 + (attn_out,) * 4 + (ffn_in,) * 4 + (ffn_out,) * 4 + (P(),) * 4
    out_specs = (rows, rows, rows, P(DP, None, None))
    out_specs += (attn_in,) * 6 + (attn_out,) * 6 + (ffn_in,) * 6 + (ffn_out,) * 6 + (P(),) * 6
    return jax.shard_map(local, mesh=mesh, in_specs=in_specs, out_specs=out_specs, check_vma=False)
```

```python
import functools
import math

import jax
import jax.numpy as jnp
from jax import lax
from jax.experimental import pallas as pl
from jax.experimental.pallas import tpu as pltpu
from jax.sharding import Mesh
from jax.sharding import PartitionSpec as P

HEAD_DIM = 64
STEP = 10

NORM_EPS = 1e-05
CLIP_NORM = 1.0
BETA_FIRST = 0.9
BETA_SECOND = 0.999
ADAM_EPS = 1e-08
WEIGHT_DECAY = 0.01
MATRIX_RATE = 0.12
NORM_RATE = 0.8
AVERAGE_CEILING = 0.999
BF = jnp.bfloat16
F32 = jnp.float32
HIGHEST = lax.Precision.HIGHEST
SCALE = 1.0 / math.sqrt(HEAD_DIM)
DP = ("dq", "stream", "core")
VMEM_LIMIT = 56 * 1024 * 1024
GROUP = 3
MOST_ITEMS = 6


def dot_nn(a, b):
    return lax.dot_general(a, b, (((1,), (0,)), ((), ())), preferred_element_type=F32)


def dot_nt(a, b):
    return lax.dot_general(a, b, (((1,), (1,)), ((), ())), preferred_element_type=F32)


def dot_tn(a, b):
    return lax.dot_general(a, b, (((0,), (0,)), ((), ())), preferred_element_type=F32)


def norm_forward(summed, gain, shift):
    centre = jnp.mean(summed, axis=-1, keepdims=True)
    offset = summed - centre
    spread = jnp.mean(offset * offset, axis=-1, keepdims=True)
    inverse = lax.rsqrt(spread + NORM_EPS)
    normed = offset * inverse
    return normed * gain + shift, normed, inverse


def norm_backward(upstream, gain, normed, inverse):
    scaled = upstream * gain
    first_mean = jnp.mean(scaled, axis=-1, keepdims=True)
    second_mean = jnp.mean(scaled * normed, axis=-1, keepdims=True)
    inward = inverse * (scaled - first_mean - normed * second_mean)
    gain_term = jnp.sum(upstream * normed, axis=0, keepdims=True)
    shift_term = jnp.sum(upstream, axis=0, keepdims=True)
    return inward, gain_term, shift_term


def cut(block, blocks):
    rows = block.shape[0] // blocks
    return [block[i * rows : (i + 1) * rows] for i in range(blocks)]


def stack_rows(parts):
    return jnp.concatenate(parts, axis=0)


def thirds(triple, width):
    return [triple[:, i * width : (i + 1) * width] for i in range(triple.shape[1] // width)]


def lane_head(block):
    return lax.broadcasted_iota(jnp.int32, block.shape, 1) // HEAD_DIM


def spread(block):
    lanes = lane_head(block)
    zero = jnp.zeros_like(block)
    heads = block.shape[1] // HEAD_DIM
    return stack_rows([jnp.where(lanes == h, block, zero) for h in range(heads)])


def gathered(block):
    parts = cut(block, block.shape[1] // HEAD_DIM)
    lanes = lane_head(parts[0])
    out = parts[0]
    for h in range(1, len(parts)):
        out = jnp.where(lanes == h, parts[h], out)
    return out


def item_of(shape, axis, rows):
    place = lax.broadcasted_iota(jnp.int32, shape, axis)
    item = jnp.zeros(shape, jnp.int32)
    for border in range(1, MOST_ITEMS):
        item += (place >= border * rows).astype(jnp.int32)
    return item


def same_item(shape, query_rows, key_rows, heads):
    mask = item_of(shape, 0, query_rows) == item_of(shape, 1, key_rows)
    return stack_rows([mask] * heads)


def attend(query, key, value, mask, blocks):
    pairs = zip(cut(query, blocks), cut(key, blocks))
    scores = stack_rows([jnp.where(mask, dot_nt(spread(q), k) * SCALE, -1e30) for q, k in pairs])
    powered = jnp.exp(scores - jnp.max(scores, axis=-1, keepdims=True))
    probs = (powered * (1.0 / jnp.sum(powered, axis=-1, keepdims=True))).astype(BF)
    mixed = [gathered(dot_nn(p, v)) for p, v in zip(cut(probs, blocks), cut(value, blocks))]
    return probs, stack_rows(mixed).astype(BF)


def attend_back(query, key, value, probs, grad_context, blocks):
    queries, keys, values = cut(query, blocks), cut(key, blocks), cut(value, blocks)
    contexts, weights = [spread(g) for g in cut(grad_context, blocks)], cut(probs, blocks)
    grad_probs = stack_rows([dot_nt(g, v) for g, v in zip(contexts, values)])
    grad_value = stack_rows([dot_tn(p, g) for p, g in zip(weights, contexts)]).astype(BF)
    wide = probs.astype(F32)
    inner = jnp.sum(grad_probs * wide, axis=-1, keepdims=True)
    grad_scores = cut((wide * (grad_probs - inner) * SCALE).astype(BF), blocks)
    grad_query = stack_rows([gathered(dot_nn(s, k)) for s, k in zip(grad_scores, keys)])
    grad_key = stack_rows([dot_tn(s, spread(q)) for s, q in zip(grad_scores, queries)])
    return grad_query.astype(BF), grad_key.astype(BF), grad_value


def load_weight(pieces, weight, column=0):
    row = 0
    for piece in pieces:
        for part in range(piece.shape[1]):
            rows, columns = piece.shape[2:]
            weight[row : row + rows, column : column + columns] = piece[0, part]
            row += rows


def load_halves(pieces, weight):
    middle = len(pieces) // 2
    lower = pl.program_id(0) < pl.num_programs(0) // 2

    @pl.when(lower)
    def _():
        load_weight(pieces[:middle], weight)

    @pl.when(jnp.logical_not(lower))
    def _():
        load_weight(pieces[middle:], weight)


def store_pair(value, near, far, by_group=False):
    rows = near.shape[3]
    for high in range(2):
        for core, piece in enumerate((near, far)):
            for mid in range(2):
                row = (4 * high + 2 * core + mid) * rows
                spot = (high, 0, mid) if by_group else (high, mid, 0)
                piece[spot] = value[row : row + rows, :].astype(piece.dtype)


def wide_spots(place, piece, shard_rows):
    groups, _, _, streams = piece.shape[:4]
    inner = max(groups // 2, 1)
    row = 0
    for high in range(groups // inner):
        for core in range(2):
            for part in range(streams):
                for sub in range(inner):
                    group = (sub * (groups // inner) + high) ^ place[0, 0]
                    yield row, (group, core ^ place[0, 1], 0, part)
                    row += shard_rows


def load_wide(place, piece, kind, weight):
    rows = piece.shape[5]
    for row, spot in wide_spots(place, piece, rows):
        weight[row : row + rows, :] = piece[spot + (kind,)]


def store_wide(place, value, piece, kind):
    rows = piece.shape[5]
    for row, spot in wide_spots(place, piece, rows):
        piece[spot + (kind,)] = value[row : row + rows, :].astype(piece.dtype)


def partner_order(value):
    dim = value.shape[1]
    eighth = dim // 8
    row = lax.broadcasted_iota(jnp.int32, (dim, dim), 0)
    column = lax.broadcasted_iota(jnp.int32, (dim, dim), 1)
    same = jnp.ones((dim, dim), jnp.bool_)
    for border in range(2 * eighth, dim, 2 * eighth):
        same &= (row >= border) == (column >= border)
    pick = same & (jnp.abs(row - column) == eighth)
    return dot_nn(value, jnp.where(pick, 1.0, 0.0).astype(BF)).astype(BF)


def widen(value, blocks, rows):
    empty = jnp.zeros((rows - value.shape[0] // blocks, value.shape[1]), value.dtype)
    return stack_rows([part for block in cut(value, blocks) for part in (block, empty)])


def cross_forward_kernel(width, blocks, words, regions, stream, lang, vis, norm, *refs):
    first, second, refs = refs[:8], refs[8:16], refs[16:]
    own_one, other_one, lang_n, lang_r, vis_n, vis_r = refs[:6]
    lang_qkv, vis_qkv, lang_ctx, vis_ctx, lang_p, vis_p = refs[6:12]
    weight, lang_acc, vis_acc = refs[12:]
    load_weight(first, weight)
    load_weight(second, weight, first[0].shape[3])
    step = pl.program_id(0)

    @pl.when(step == 0)
    def _():
        lang_acc[...] = lang[...].astype(F32)
        vis_acc[...] = vis[...].astype(F32)

    full = weight[...]
    in_part, out_part = full[:, : 3 * width], full[:, 3 * width :]
    lang_triple = dot_nn(lang[...], in_part).astype(BF)
    vis_triple = dot_nn(vis[...], in_part).astype(BF)
    lang_qkv[0] = lang_triple
    vis_qkv[0] = vis_triple
    lang_query, lang_key, lang_value = thirds(lang_triple, width)
    vis_query, vis_key, vis_value = thirds(vis_triple, width)
    heads = width // HEAD_DIM
    lang_block, vis_block = lang.shape[0] // blocks, vis.shape[0] // blocks
    lang_mask = same_item((lang_block, vis_block), words, regions, heads)
    vis_mask = same_item((vis_block, lang_block), regions, words, heads)
    for query, key, value, probs_ref, ctx_ref, acc, mask in (
        (lang_query, vis_key, vis_value, lang_p, lang_ctx, lang_acc, lang_mask),
        (vis_query, lang_key, lang_value, vis_p, vis_ctx, vis_acc, vis_mask),
    ):
        probs, context = attend(query, key, value, mask, blocks)
        probs_ref[0] = probs
        ctx_ref[0] = context
        acc[...] += dot_nt(context, out_part)

    @pl.when(step == pl.num_programs(0) - 1)
    def _():
        ones = []
        for acc, n_ref, r_ref in ((lang_acc, lang_n, lang_r), (vis_acc, vis_n, vis_r)):
            out, normed, inverse = norm_forward(acc[...], norm[0:1, :], norm[1:2, :])
            ones.append(out.astype(BF))
            n_ref[...] = normed
            r_ref[...] = inverse
        lang_one, vis_one = widen(ones[0], blocks, vis_block), ones[1]
        is_vis = stream[0, 0] == 1
        own_one[...] = jnp.where(is_vis, vis_one, lang_one)
        other_one[...] = partner_order(jnp.where(is_vis, lang_one, vis_one))


def self_forward_step(width, blocks, length, rows, pieces, weight, qkv, ctx, probs_ref):
    load_weight(pieces, weight)
    full = weight[...]
    in_part, out_part = full[:, : 3 * width], full[:, 3 * width :]
    triple = dot_nn(rows[...], in_part).astype(BF)
    qkv[0] = triple
    block = rows.shape[0] // blocks
    mask = same_item((block, block), length[0, 0], length[0, 0], width // HEAD_DIM)
    probs, context = attend(*thirds(triple, width), mask, blocks)
    probs_ref[0] = probs
    ctx[0] = context
    return dot_nt(context, out_part)


def self_first_kernel(width, blocks, length, own, other, *refs):
    pieces, (acc, qkv, ctx, probs, weight, rows) = refs[:4], refs[4:]

    @pl.when(pl.program_id(0) == 0)
    def _():
        rows[...] = stack_rows([own[...], other[...]])
        acc[...] = rows[...].astype(F32)

    acc[...] += self_forward_step(width, blocks, length, rows, pieces, weight, qkv, ctx, probs)


def self_second_kernel(width, blocks, length, own, other, norm, summed, *refs):
    pieces, refs = refs[:4], refs[7:]
    two, n_ref, r_ref, qkv, ctx, probs, weight, acc, rows = refs
    step = pl.program_id(0)

    @pl.when(step == 0)
    def _():
        rows[...] = stack_rows([own[...], other[...]])
        acc[...] = summed[...]

    acc[...] += self_forward_step(width, blocks, length, rows, pieces, weight, qkv, ctx, probs)

    @pl.when(step == pl.num_programs(0) - 1)
    def _():
        out, normed, inverse = norm_forward(acc[...], norm[0:1, :], norm[1:2, :])
        two[...] = out.astype(BF)
        n_ref[...] = normed
        r_ref[...] = inverse


def feed_kernel(place, rows, normed_two, inverse, cot, norm, piece, *refs):
    three, grads, down_ref, self_gain, self_shift, feed_gain, feed_shift, refs = refs[:7] + (refs[7:],)
    weight_in, weight_out, active, slope, acc, branch, branch_turned, turned = refs
    step, groups = pl.program_id(0), pl.num_programs(0) // 2
    group = lax.rem(step, groups)

    @pl.when(step == 0)
    def _():
        acc[...] = normed_two[...] * norm[0:1, :] + norm[1:2, :]
        turned[...] = rows[...].T

    @pl.when(step < groups)
    def _():
        load_wide(place, piece, 0, weight_in.at[group])
        load_wide(place, piece, 1, weight_out.at[group])
        hidden = dot_nn(rows[...], weight_in[group])
        normal = 0.5 * (1.0 + lax.erf(hidden * 0.7071067811865476))
        slopes = normal + hidden * jnp.exp(-0.5 * hidden * hidden) * 0.3989422804014327
        actives = (hidden * normal).astype(BF)
        active[group] = actives
        slope[group] = slopes.astype(BF)
        acc[...] += dot_nt(actives, weight_out[group])

    @pl.when(step == groups - 1)
    def _():
        gain = norm[2:3, :]
        out, normed, inverse_three = norm_forward(acc[...], gain, norm[3:4, :])
        three[...] = out.astype(BF)
        inward, gain_term, shift_term = norm_backward(
            cot[...].astype(F32), gain, normed, inverse_three
        )
        acc[...] = inward
        branch[...] = inward.astype(BF)
        branch_turned[...] = inward.astype(BF).T
        feed_gain[...] = gain_term
        feed_shift[...] = shift_term

    @pl.when(step >= groups)
    def _():
        store_wide(place, dot_nn(branch_turned[...], active[group]), grads, 1)
        grad_active = dot_nn(branch[...], weight_out[group])
        grad_hidden = (grad_active * slope[group].astype(F32)).astype(BF)
        store_wide(place, dot_nn(turned[...], grad_hidden), grads, 0)
        acc[...] += dot_nt(grad_hidden, weight_in[group])

    @pl.when(step == 2 * groups - 1)
    def _():
        down, gain_term, shift_term = norm_backward(
            acc[...], norm[0:1, :], normed_two[...], inverse[...]
        )
        down_ref[...] = down
        self_gain[...] = gain_term
        self_shift[...] = shift_term


def self_other_kernel(width, blocks, inward, qkv, probs, *refs):
    pieces, (triple_ref, down, weight, acc, branch) = refs[:8], refs[8:]
    load_halves(pieces, weight)
    step = pl.program_id(0)

    @pl.when(step == 0)
    def _():
        acc[...] = inward[...]
        branch[...] = inward[...].astype(BF)

    full = weight[...]
    in_part, out_part = full[:, : 3 * width], full[:, 3 * width :]
    grad_context = dot_nn(branch[...], out_part).astype(BF)
    grads_of = attend_back(*thirds(qkv[0], width), probs[0], grad_context, blocks)
    grad_triple = jnp.concatenate(grads_of, axis=1)
    triple_ref[0] = grad_triple
    acc[...] += dot_nt(grad_triple, in_part)

    @pl.when(step == pl.num_programs(0) - 1)
    def _():
        down[...] = partner_order(acc[...].astype(BF))


def self_own_kernel(width, blocks, inward, own, other, qkv, ctx, probs, other_triple, *refs):
    pieces, near, far, refs = refs[:8], refs[8], refs[9], refs[10:]
    down, weight, acc, branch, turned, branch_turned = refs
    load_halves(pieces, weight)
    step = pl.program_id(0)

    @pl.when(step == 0)
    def _():
        slot = own.shape[0]
        acc[...] = inward[:slot, :]
        gradient = inward[...].astype(BF)
        branch[...] = gradient[:slot]
        branch_turned[...] = gradient.T
        turned[...] = stack_rows([own[...], other[...]]).T

    full = weight[...]
    in_part, out_part = full[:, : 3 * width], full[:, 3 * width :]
    grad_context = dot_nn(branch[...], out_part).astype(BF)
    grads_of = attend_back(*thirds(qkv[0], width), probs[0], grad_context, blocks)
    grad_triple = jnp.concatenate(grads_of, axis=1)
    in_grad = dot_nn(turned[...], stack_rows([grad_triple, other_triple[0]])).astype(BF)
    out_grad = dot_nn(branch_turned[...], ctx[0]).astype(BF)
    store_pair(jnp.concatenate([in_grad, out_grad], axis=1), near, far, True)
    acc[...] += dot_nt(grad_triple, in_part)

    @pl.when(step == pl.num_programs(0) - 1)
    def _():
        down[...] = acc[...].astype(BF)


def cross_backward_kernel(
    width,
    blocks,
    stream,
    own_up,
    other_up,
    lang,
    vis,
    lang_n,
    lang_r,
    vis_n,
    vis_r,
    norm,
    order,
    source,
    targets,
    *refs,
):
    lang_qkv, vis_qkv, lang_ctx, vis_ctx, lang_p, vis_p = refs[:6]
    first, second, refs = refs[6:14], refs[14:22], refs[22:]
    near, far, lang_out, image_out, gain_ref, shift_ref = refs[:6]
    weight, lang_acc, vis_acc, lang_branch, vis_branch, turned, branch_turned = refs[6:]
    load_weight(first, weight)
    load_weight(second, weight, first[0].shape[3])
    step = pl.program_id(0)

    @pl.when(step == 0)
    def _():
        is_vis = stream[0, 0] == 1
        own, other = own_up[...].astype(F32), other_up[...].astype(F32)
        lang_block = lang.shape[0] // blocks
        lang_up = cut(jnp.where(is_vis, other, own), blocks)
        lang_up = stack_rows([block[:lang_block] for block in lang_up])
        vis_up = jnp.where(is_vis, own, other)
        gain_total, shift_total = 0.0, 0.0
        for up, n_ref, r_ref, acc, branch in (
            (lang_up, lang_n, lang_r, lang_acc, lang_branch),
            (vis_up, vis_n, vis_r, vis_acc, vis_branch),
        ):
            inward, gain_term, shift_term = norm_backward(
                up, norm[0:1, :], n_ref[...], r_ref[...]
            )
            acc[...] = inward
            branch[...] = inward.astype(BF)
            gain_total += gain_term
            shift_total += shift_term
        gain_ref[...] = gain_total
        shift_ref[...] = shift_total
        turned[...] = stack_rows([lang[...], vis[...]]).T
        branch_turned[...] = stack_rows([lang_branch[...], vis_branch[...]]).T

    full = weight[...]
    in_part, out_part = full[:, : 3 * width], full[:, 3 * width :]
    lang_gc = dot_nn(lang_branch[...], out_part).astype(BF)
    vis_gc = dot_nn(vis_branch[...], out_part).astype(BF)
    lang_query, lang_key, lang_value = thirds(lang_qkv[0], width)
    vis_query, vis_key, vis_value = thirds(vis_qkv[0], width)
    lang_dq, vis_dk, vis_dv = attend_back(
        lang_query, vis_key, vis_value, lang_p[0], lang_gc, blocks
    )
    vis_dq, lang_dk, lang_dv = attend_back(
        vis_query, lang_key, lang_value, vis_p[0], vis_gc, blocks
    )
    lang_grad = jnp.concatenate([lang_dq, lang_dk, lang_dv], axis=1)
    vis_grad = jnp.concatenate([vis_dq, vis_dk, vis_dv], axis=1)
    in_grad = dot_nn(turned[...], stack_rows([lang_grad, vis_grad]))
    out_grad = dot_nn(branch_turned[...], stack_rows([lang_ctx[0], vis_ctx[0]]))
    grad = jnp.concatenate([in_grad.astype(BF), out_grad.astype(BF)], axis=1)
    store_pair(grad, near, far)
    lang_acc[...] += dot_nt(lang_grad, in_part)
    vis_acc[...] += dot_nt(vis_grad, in_part)

    @pl.when(step == pl.num_programs(0) - 1)
    def _():
        lang_out[...] = dot_nt(lang_acc[...].astype(BF), order[...])
        chooser = jnp.where(source[...] == targets[...], 1.0, 0.0).astype(BF)
        image = dot_tn(chooser, vis_acc[...].astype(BF)).astype(BF)
        image_out[...] = dot_nt(image, order[...]).astype(BF)


def store_step(state, clip, outs):
    new = adamw_step(*state, MATRIX_RATE, clip)
    for (ref, place), value in zip(outs, new[:4] + (new[3], new[4])):
        ref[place] = value.astype(ref.dtype)


def prepare_kernel(norms, kept, sent, self_low, self_theirs, feed_sum, feed_theirs, sums):
    home = kept[...].astype(F32) + sent[...].astype(F32)
    squares = jnp.sum(home * home, keepdims=True)[0]
    for value in (self_low[0], self_theirs[...]):
        wide = value.astype(F32)
        squares += jnp.sum(wide * wide, keepdims=True)
    for kind in range(feed_theirs.shape[0]):
        for value in (feed_sum[0, kind], feed_theirs[kind]):
            wide = value.astype(F32)
            squares += jnp.sum(wide * wide, keepdims=True)
    count = norms.shape[0]
    sums[:count, :] = norms[...]
    sums[count:, :] = jnp.broadcast_to(squares, (1, norms.shape[1]))


def step_kernel(
    width, stream, sums, theirs, kept, sent, self_low, self_theirs, feed_sum, feed_theirs, *refs
):
    ins, outs, feed_in, feed_out, norm_in = (refs[4 * i : 4 * i + 4] for i in range(5))
    refs = refs[20:]
    step = pl.program_id(0)
    total = sums[...] + theirs[...]
    norm_grad = total[:-1]
    squares = jnp.sum(norm_grad * norm_grad, keepdims=True) + total[-1:, 0:1]
    grad_norm = jnp.sqrt(squares)
    clip = CLIP_NORM / jnp.maximum(grad_norm, CLIP_NORM)
    refs[-1][...] = grad_norm
    for place in range(norm_in[0].shape[0]):
        state = [ref[place] for ref in norm_in]
        new = adamw_step(norm_grad[2 * place : 2 * place + 2], *state, NORM_RATE, clip)
        for ref, value in zip(refs[24:29], new):
            ref[place] = value
    is_vis = stream[0, 0] == 1

    def by_stream(mine, other):
        mine, other = mine.astype(F32), other.astype(F32)
        return jnp.where(is_vis, other, mine), jnp.where(is_vis, mine, other)

    home = kept[0].astype(F32) + sent[0].astype(F32)
    one, two = by_stream(self_low[0], self_theirs[...])
    grad = jnp.where(step == 0, home, jnp.where(step == 1, one, two))
    for kind in range(3):
        part = grad[:, kind * width : (kind + 1) * width]
        store_step([part] + [ref[0, kind] for ref in ins], clip, [(r, (0, kind)) for r in refs[:6]])
    part = grad[:, 3 * width :].T
    store_step([part] + [ref[0] for ref in outs], clip, [(r, 0) for r in refs[6:12]])
    for kind, state_in, first in ((0, feed_in, 12), (1, feed_out, 18)):
        for place, part in enumerate(by_stream(feed_sum[0, kind], feed_theirs[kind])):
            state = [part] + [ref[place] for ref in state_in]
            store_step(state, clip, [(r, place) for r in refs[first : first + 6]])


def whole(shape):
    return pl.BlockSpec(shape, lambda m: (0,) * len(shape))


def per_step(shape):
    rest = (0,) * (len(shape) - 1)
    return pl.BlockSpec((1,) + tuple(shape[1:]), lambda m: (m,) + rest)


def part_of(shape, pick):
    rest = (0,) * (len(shape) - 1)
    return pl.BlockSpec((1,) + tuple(shape[1:]), lambda m: (pick(m),) + rest)


def group_of(shape, pick):
    block = (shape[0], shape[1], 1) + tuple(shape[3:])
    return pl.BlockSpec(block, lambda m: (0, 0, pick(m), 0, 0, 0, 0))


def call(kernel, steps, ins, outs, scratch, name, flops, aliases=()):
    spec = {
        "whole": lambda s: whole(s),
        "step": lambda s: per_step(s),
        "early": lambda s: group_of(s, lambda m: jnp.minimum(m, s[2] - 1)),
        "late": lambda s: group_of(s, lambda m: jnp.maximum(m - s[2], 0)),
        "low": lambda s: part_of(s, lambda m: jnp.minimum(m, s[0] - 1)),
        "high": lambda s: part_of(s, lambda m: jnp.maximum(m - s[0], 0)),
        "rows": lambda s: pl.BlockSpec(
            tuple(s[:-2]) + (s[-2] // steps, s[-1]), lambda m: (0,) * (len(s) - 2) + (m, 0)
        ),
        "pair": lambda s: pl.BlockSpec(
            tuple(s[:2]) + (1,) + tuple(s[3:]), lambda m: (0, 0, m, 0, 0)
        ),
        "groups": lambda s: pl.BlockSpec(
            (s[0], 1) + tuple(s[2:]), lambda m: (0, m, 0, 0, 0)
        ),
        "upper": lambda s: part_of(s, lambda m: m + s[0] // 2),
        "own": lambda s: pl.BlockSpec((1, s[1] // 2, s[2]), lambda m: (m, 0, 0)),
        "other": lambda s: pl.BlockSpec((1, s[1] // 2, s[2]), lambda m: (m, 1, 0)),
        "other_rows": lambda s: pl.BlockSpec((s[0] // 2, s[1]), lambda m: (1, 0)),
        "kept": lambda s: pl.BlockSpec(memory_space=pl.ANY),
        "scalar": lambda s: pl.BlockSpec(memory_space=pltpu.SMEM),
    }
    moved = sum(a.size * a.dtype.itemsize for _, a in ins)
    moved += sum(math.prod(s) * jnp.dtype(t).itemsize for _, s, t in outs)
    return pl.pallas_call(
        kernel,
        grid=(steps,),
        in_specs=[spec[kind](a.shape) for kind, a in ins],
        out_specs=[spec[kind](s) for kind, s, _ in outs],
        out_shape=[jax.ShapeDtypeStruct(s, t) for _, s, t in outs],
        scratch_shapes=[pltpu.VMEM(s, t) for s, t in scratch],
        input_output_aliases=dict(aliases),
        compiler_params=pltpu.CompilerParams(
            vmem_limit_bytes=VMEM_LIMIT, dimension_semantics=("arbitrary",)
        ),
        cost_estimate=pl.CostEstimate(flops=flops, bytes_accessed=moved, transcendentals=0),
        name=name,
    )(*[a for _, a in ins])


def swap_dp(value, bit):
    axis, place = (("core", 0), ("stream", 0), ("dq", bit - 2))[min(bit, 2)]
    count = lax.axis_size(axis)
    return lax.ppermute(value, axis, [(i, i ^ (1 << place)) for i in range(count)])


def swap_mp(value, bit):
    count = lax.axis_size("mp")
    return lax.ppermute(value, "mp", [(i, i ^ (1 << bit)) for i in range(count)])


def after(value, *others):
    flat, tree = jax.tree.flatten(value)
    kept = lax.optimization_barrier((flat, jax.tree.leaves(others)))[0]
    return jax.tree.unflatten(tree, kept)


def together(*values):
    return lax.optimization_barrier(values)


def swap_mask(value, axis, mask):
    count = lax.axis_size(axis)
    return lax.ppermute(value, axis, [(i, i ^ mask) for i in range(count)])


def sum_up(value):
    count = lax.axis_size("mp")
    mask = 1
    while mask < count:
        if 2 * mask < count:
            theirs = [swap_mask(value, "mp", mask * k) for k in (1, 2, 3)]
            value = (value + theirs[0]) + (theirs[1] + theirs[2])
            mask *= 4
        else:
            value += swap_mask(value, "mp", mask)
            mask *= 2
    both = ("dq", "stream")
    count = lax.axis_size(both)
    mask = 1
    while mask < count:
        if 2 * mask < count:
            theirs = [swap_mask(value, both, mask * k) for k in (1, 2, 3)]
            value = (value + theirs[0]) + (theirs[1] + theirs[2])
            mask *= 4
        else:
            value += swap_mask(value, both, mask)
            mask *= 2
    return value, swap_dp(value, 0)


def extra_bits():
    return range(3, 2 + int(math.log2(lax.axis_size("dq"))))


def mp_bits():
    return range(int(math.log2(lax.axis_size("mp"))))


def gather_mp(current):
    for bit in reversed(mp_bits()):
        current = jnp.concatenate([current, swap_mp(current, bit)], axis=0)
    return current


def gather_extra(current):
    for bit in extra_bits():
        current = jnp.concatenate([current, swap_dp(current, bit)], axis=2)
    return current


def scatter_mp(current):
    for bit in mp_bits():
        half = current.shape[0] // 2
        current = added(current[:half], swap_mp(current[half:], bit))
    return current


def scatter_extra(current):
    for bit in reversed(extra_bits()):
        low, high = jnp.split(current, 2, axis=-2)
        current = added(low, swap_dp(high, bit))
    return current


def added(mine, theirs):
    return (mine.astype(F32) + theirs.astype(F32)).astype(BF)


def grow(found, place, bit):
    for key in list(found):
        new = list(key)
        new[place] = 1
        found[tuple(new)] = swap_dp(found[key], bit)


def shrink(found, place, bit):
    for key in [k for k in found if k[place] == 0]:
        far = list(key)
        far[place] = 1
        found[key] = added(found[key], swap_dp(found.pop(tuple(far)), bit))


def home_list(found):
    return [found[(hi, mid, lo)] for hi in (0, 1) for lo in (0, 1) for mid in (0, 1)]


def stream_list(found):
    return [found[(hi, lo)] for hi in (0, 1) for lo in (0, 1)]


def home_keys(arrays):
    return {(i >> 2, i & 1, (i >> 1) & 1): a for i, a in enumerate(arrays)}


def stream_keys(arrays):
    return {(i >> 1, i & 1): a for i, a in enumerate(arrays)}


def adamw_step(gradient, moment, square, weight, average, rate, clip_scale):
    average_decay = min(AVERAGE_CEILING, (1.0 + STEP) / (10.0 + STEP))
    clipped = gradient * clip_scale
    moment_new = BETA_FIRST * moment + (1.0 - BETA_FIRST) * clipped
    square_new = BETA_SECOND * square + (1.0 - BETA_SECOND) * clipped * clipped
    corrected = moment_new / (1.0 - BETA_FIRST**STEP)
    denominator = jnp.sqrt(square_new / (1.0 - BETA_SECOND**STEP)) + ADAM_EPS
    weight_new = weight - rate * (corrected / denominator + WEIGHT_DECAY * weight)
    average_new = average_decay * average + (1.0 - average_decay) * weight_new
    return (clipped, moment_new, square_new, weight_new, average_new)


def pad_rows(block, rows):
    return jnp.pad(block, ((0, rows - block.shape[0]), (0, 0)))


def local(
    language,
    images,
    counts,
    language_cot,
    vision_cot,
    attn_in_weight,
    attn_in_moment,
    attn_in_square,
    attn_in_average,
    attn_out_weight,
    attn_out_moment,
    attn_out_square,
    attn_out_average,
    ffn_in_weight,
    ffn_in_moment,
    ffn_in_square,
    ffn_in_average,
    ffn_out_weight,
    ffn_out_moment,
    ffn_out_square,
    ffn_out_average,
    norm_weight,
    norm_moment,
    norm_square,
    norm_average,
):
    n_dp, n_mp = lax.axis_size(DP), lax.axis_size("mp")
    me = lax.axis_index(DP)
    stream = (me >> 1) & 1
    is_vis = stream == 1
    own_items, words, dim = language.shape
    regions = images.shape[1]
    blocks = own_items // GROUP
    lang_block, vis_block = (-(-GROUP * rows // 16) * 16 for rows in (words, regions))
    lang_pad, slot = blocks * lang_block, blocks * vis_block
    total = 2 * slot
    shard_rows = attn_in_weight.shape[1]
    width = attn_in_weight.shape[3]
    units = ffn_in_weight.shape[2]
    heads = width // HEAD_DIM
    half = 2 * width
    eighth = dim // 8

    def mine_first(pair):
        return jnp.where(is_vis, pair[1], pair[0]), jnp.where(is_vis, pair[0], pair[1])

    attn_shards = [
        jnp.concatenate(
            [attn_in_weight[b].reshape(shard_rows, 3 * width), attn_out_weight[b].T], axis=1
        ).astype(BF)[None, None]
        for b in range(3)
    ]
    def pair_up(shards, *pins):
        own, other = mine_first(shards)
        return jnp.concatenate([own, swap_dp(after(other, *pins), 1)], axis=1)

    halves = [attn_shards[0][..., c : c + half] for c in (0, half)]
    self_pair = pair_up(attn_shards[1:])
    for bit in reversed(mp_bits()):
        halves = [jnp.concatenate([h, swap_mp(h, bit)], axis=0) for h in halves]
        if bit == mp_bits()[-1]:
            feed_own, feed_other = mine_first(
                [jnp.stack([ffn_in_weight[s].astype(BF), ffn_out_weight[s].T.astype(BF)]) for s in range(2)]
            )
            feed_pair = jnp.stack([feed_own, swap_dp(feed_other, 1)])
            feed_w = lax.all_gather(after(feed_pair, halves), ("dq", "core", "mp"), axis=0)
            feed_w = feed_w.reshape((n_dp // 4, 2, n_mp) + feed_pair.shape)
    first, second = ({(0, 0, 0): gather_extra(h)} for h in halves)

    def gather_step(current, index):
        return jnp.concatenate([current, swap_mp(current, mp_bits()[-1 - index])], axis=0)

    n_bits = len(mp_bits())
    self_low = self_pair
    for index in range(n_bits - 1):
        self_low = gather_step(self_low, index)
    grow(first, 0, 2)
    grow(second, 1, 1)

    place = jnp.arange(dim, dtype=jnp.int32)
    block = place // shard_rows
    sub, high = block % (n_dp // 8), block // (n_dp // 8)
    relative = 8 * sub + 4 * (high >> 2) + ((high >> 1) & 1) + 2 * (high & 1)
    origin = (relative ^ me) * shard_rows + place % shard_rows
    order = (place[:, None] == origin[None, :]).astype(BF)

    def to_order(value):
        return dot_nn(value, order).astype(BF)

    def from_order(value, precision=None):
        return lax.dot_general(
            value, order, (((1,), (1,)), ((), ())), preferred_element_type=F32, precision=precision
        )

    norm_ordered = lax.dot_general(
        norm_weight.reshape(-1, dim),
        order.astype(F32),
        (((1,), (0,)), ((), ())),
        precision=HIGHEST,
        preferred_element_type=F32,
    ).reshape(norm_weight.shape)
    norm_cross = norm_ordered[:, 0]
    norm_self = jnp.where(is_vis, norm_ordered[:, 2], norm_ordered[:, 1])
    norm_feed = jnp.where(is_vis, norm_ordered[:, 4], norm_ordered[:, 3])
    norm_pair = jnp.concatenate([norm_self, norm_feed], axis=0)

    def in_blocks(value, rows, target):
        value = value.reshape(blocks, rows, dim)
        value = jnp.pad(value, ((0, 0), (0, target - rows), (0, 0)))
        return value.reshape(blocks * target, dim)

    def out_of_blocks(value, rows):
        return value.reshape(blocks, -1, dim)[:, :rows].reshape(blocks * rows, dim)

    lang_rows, vis_rows = GROUP * words, GROUP * regions
    first_item = lax.axis_index("mp") * own_items
    bounds = jnp.cumsum(counts[0])
    positions = first_item + jnp.arange(own_items, dtype=jnp.int32)
    item_image = jnp.sum((bounds[None, :] <= positions[:, None]).astype(jnp.int32), axis=1)
    region = jnp.arange(regions, dtype=jnp.int32)
    row_source = (item_image[:, None] * regions + region[None, :]).reshape(blocks, vis_rows) + 1
    row_source = jnp.pad(row_source, ((0, 0), (0, vis_block - vis_rows))).reshape(slot, 1)
    image_count = images.shape[0] * regions
    picker = (row_source == 1 + jnp.arange(image_count, dtype=jnp.int32)[None, :]).astype(BF)
    lang = to_order(in_blocks(language, lang_rows, lang_block))
    image_rows = to_order(images.reshape(-1, dim))
    vis = dot_nn(picker, image_rows).astype(BF)

    lang_cot = in_blocks(language_cot, lang_rows, vis_block)
    vis_cot = in_blocks(vision_cot, vis_rows, vis_block)
    cot_own, cot_other = mine_first((lang_cot, vis_cot))

    length = jnp.where(is_vis, regions, words).astype(jnp.int32).reshape(1, 1)

    first, second = after((first, second), lang, vis)
    grow(first, 1, 1)
    grow(second, 0, 2)
    self_low = {(0, 0): gather_extra(self_low)}
    self_high = {(0, 0): swap_mp(self_low[(0, 0)], 0)}
    grow(first, 2, 0)
    grow(second, 2, 0)
    pieces = lambda arrays: [("step", a) for a in arrays]
    which = stream.astype(jnp.int32).reshape(1, 1)
    ins = [("scalar", which)] + [("whole", a) for a in (lang, vis, norm_cross)]
    outs = [("whole", (slot, dim), BF)] * 2
    for rows in (lang_pad, slot):
        outs += [("whole", (rows, dim), F32), ("whole", (rows, 1), F32)]
    outs += [("step", (n_mp, rows, 3 * width), BF) for rows in (lang_pad, slot)]
    outs += [("step", (n_mp, rows, width), BF) for rows in (lang_pad, slot)]
    outs += [
        ("step", (n_mp, heads * lang_pad, vis_block), BF),
        ("step", (n_mp, heads * slot, lang_block), BF),
    ]
    both = lang_pad + slot
    cross_w = home_list(first) + home_list(second)
    cross_w = after(cross_w, self_low)
    grow(self_low, 0, 2)
    found = call(
        functools.partial(cross_forward_kernel, width, blocks, words, regions),
        n_mp,
        ins + pieces(cross_w),
        outs,
        [((dim, 4 * width), BF), ((lang_pad, dim), F32), ((slot, dim), F32)],
        "cross_forward",
        12 * both * dim * 4 * width * n_mp,
    )
    own_one, other_one, lang_n, lang_r, vis_n, vis_r = found[:6]
    cross_saved = found[6:]

    other_one = swap_dp(other_one, 1)
    self_high, self_low, cot_other = after((self_high, self_low, cot_other), other_one)
    grow(self_high, 0, 2)
    grow(self_low, 1, 0)
    half_groups = n_mp // 2
    saved = [
        (n_mp, total, 3 * width),
        (n_mp, total, width),
        (n_mp, heads * total, vis_block),
    ]
    first_half = call(
        functools.partial(self_first_kernel, width, 2 * blocks),
        half_groups,
        [("scalar", length)]
        + [("whole", a) for a in (own_one, other_one)]
        + [("step", a) for a in stream_list(self_low)],
        [("whole", (total, dim), F32)] + [("step", a, BF) for a in saved],
        [((dim, 4 * width), BF), ((total, dim), BF)],
        "self_first",
        6 * total * dim * 4 * width * n_mp,
    )
    self_high, cot_theirs = after((self_high, swap_dp(cot_other, 1)), first_half[0])
    grow(self_high, 1, 0)
    self_pieces = [("low", a) for a in stream_list(self_low)]
    self_pieces += [("high", a) for a in stream_list(self_high)]
    rows_two, normed_two, inverse_two, self_qkv, self_ctx, self_probs = call(
        functools.partial(self_second_kernel, width, 2 * blocks),
        half_groups,
        [("scalar", length)]
        + [("whole", a) for a in (own_one, other_one, norm_self, first_half[0])]
        + [("step", a) for a in stream_list(self_high)]
        + [("kept", a) for a in first_half[1:]],
        [("whole", (total, dim), BF), ("whole", (total, dim), F32), ("whole", (total, 1), F32)]
        + [("upper", a, BF) for a in saved],
        [((dim, 4 * width), BF), ((total, dim), F32), ((total, dim), BF)],
        "self_second",
        6 * total * dim * 4 * width * n_mp,
        [(9 + i, 3 + i) for i in range(3)],
    )
    cot = to_order(jnp.concatenate([cot_own, cot_theirs], axis=0))
    spot = jnp.stack([me >> 2, me & 1]).astype(jnp.int32).reshape(1, 2)

    whole_row = ("whole", (1, dim), F32)
    rows_three, feed_g, inward, self_gain, self_shift, feed_gain, feed_shift = call(
        feed_kernel,
        2 * n_mp,
        [("scalar", spot)]
        + [("whole", a) for a in (rows_two, normed_two, inverse_two, cot, norm_pair)]
        + [("early", feed_w)],
        [("whole", (total, dim), BF), ("late", feed_w.shape, BF), ("whole", (total, dim), F32)]
        + [whole_row] * 4,
        [((n_mp, dim, units), BF)] * 2
        + [((n_mp, total, units), BF)] * 2
        + [((total, dim), F32), ((total, dim), BF), ((dim, total), BF), ((dim, total), BF)],
        "feed",
        24 * total * dim * units * n_mp,
    )

    feed_sum = lax.psum_scatter(
        (feed_g * (1 + 0 * (me < 0)).astype(BF)).reshape((-1,) + feed_pair.shape), ("dq", "core", "mp"), scatter_dimension=0, tiled=True
    )[0]

    def core_step(found, *pins):
        theirs = [swap_dp(found[(hi, 1)], 0) for hi in (0, 1)]
        return [found[(hi, 0)] for hi in (0, 1)], after(theirs, *pins)

    def split(mine, theirs):
        middle = mine.shape[0] // 2
        return added(mine[:middle], theirs[:middle]), added(mine[middle:], theirs[middle:])

    def send_mp(parts, bit):
        return [(keep, swap_mp(far, bit)) for keep, far in parts]

    other_triple, other_up = call(
        functools.partial(self_other_kernel, width, blocks),
        n_mp,
        [("other_rows", inward), ("other", self_qkv), ("other", self_probs)] + self_pieces,
        [("step", (n_mp, slot, 3 * width), BF), ("whole", (slot, dim), BF)],
        [((dim, 4 * width), BF), ((slot, dim), F32), ((slot, dim), BF)],
        "self_other",
        2 * total * dim * 4 * width * n_mp,
    )
    other_up = swap_dp(other_up, 1)
    self_near, self_far, own_up = call(
        functools.partial(self_own_kernel, width, blocks),
        n_mp,
        [("whole", a) for a in (inward, own_one, other_one)]
        + [("own", self_qkv), ("step", self_ctx), ("own", self_probs), ("step", other_triple)]
        + self_pieces,
        [("groups", (2, n_mp, 2, eighth, 4 * width), BF)] * 2 + [("whole", (slot, dim), BF)],
        [((dim, 4 * width), BF), ((slot, dim), F32), ((slot, dim), BF)] + [((dim, total), BF)] * 2,
        "self_own",
        2 * total * dim * 4 * width * n_mp,
    )
    self_near, self_far, own_up, other_up = together(self_near, self_far, own_up, other_up)
    self_far = swap_dp(self_far, 0)
    self_sums = [scatter_extra(added(self_near[hi], self_far[hi])) for hi in (0, 1)]
    own_up = after(own_up, self_sums)
    place_mp = lax.axis_index("mp")
    part = -(-image_count // n_mp // 16) * 16
    index = jnp.arange(n_mp, dtype=jnp.int32)
    far = sum(((index >> b) & 1) << (n_bits - 1 - b) for b in range(n_bits))
    rows = ((far ^ place_mp)[:, None] * part + jnp.arange(part, dtype=jnp.int32)[None, :]).reshape(1, -1)
    found = call(
        functools.partial(cross_backward_kernel, width, blocks),
        n_mp,
        [("scalar", which)]
        + [("whole", a) for a in (own_up, other_up, lang, vis)]
        + [("whole", a) for a in (lang_n, lang_r, vis_n, vis_r, norm_cross)]
        + [("whole", a) for a in (order, row_source, 1 + rows)]
        + [("step", a) for a in cross_saved]
        + pieces(cross_w),
        [("pair", (2, 2, n_mp, eighth, 4 * width), BF)] * 2
        + [
            ("whole", (lang_pad, dim), F32),
            ("whole", (n_mp * part, dim), BF),
            ("whole", (1, dim), F32),
            ("whole", (1, dim), F32),
        ],
        [
            ((dim, 4 * width), BF),
            ((lang_pad, dim), F32),
            ((slot, dim), F32),
            ((lang_pad, dim), BF),
            ((slot, dim), BF),
            ((dim, both), BF),
            ((dim, both), BF),
        ],
        "cross_backward",
        6 * both * dim * 4 * width * n_mp,
    )
    near, far, lang_back, image_term, cross_gain, cross_shift = found

    def parts(value):
        middle = value.shape[0] // 2
        return value[:middle], value[middle:]

    def total_of(*terms):
        return functools.reduce(jnp.add, [t.astype(F32) for t in terms]).astype(BF)

    self_kept = self_sums[0]
    self_far = swap_dp(self_sums[1][1:], 2)
    late = together(near, far, lang_back, image_term, self_far, cross_gain, cross_shift)
    near, far, lang_back, image_term, self_far, cross_gain, cross_shift = late
    far = swap_dp(far, 0)
    self_sent = total_of(self_kept[2:], self_far[1:])
    left, right = (slice(c, c + half) for c in (0, half))
    first = [added(near[:, mid, ..., left], far[:, mid, ..., left]) for mid in (0, 1)]
    second = [added(near[hi, ..., right], far[hi, ..., right]) for hi in (0, 1)]
    first, second, self_sent, lang_back = together(first, second, self_sent, lang_back)

    first_far, second_far, self_sent = swap_dp(first[1], 1), swap_dp(second[1], 2), swap_mp(self_sent, 0)
    late = together(first, second, first_far, second_far, self_sent, rows_three, image_term)
    first, second, first_far, second_far, self_sent, rows_three, image_term = late
    first = [added(first[0][i], first_far[i]) for i in (0, 1)]
    second = [added(second[0][i], second_far[i]) for i in (0, 1)]
    first, second, self_sent = together(first, second, self_sent)
    self_one = total_of(self_kept[1], self_far[0], self_sent[1])

    here = (jnp.arange(2, dtype=jnp.int32) == stream).astype(F32)[:, None, None]
    norm_partial = jnp.concatenate(
        [
            jnp.concatenate([cross_gain, cross_shift], axis=0)[None],
            here * jnp.concatenate([self_gain, self_shift], axis=0)[None],
            here * jnp.concatenate([feed_gain, feed_shift], axis=0)[None],
        ],
        axis=0,
    )
    norm_partial = from_order(norm_partial.reshape(-1, dim), HIGHEST)

    final = from_order(rows_three).astype(BF)

    first_far, second_far = swap_dp(first[1], 2), swap_dp(second[1], 1)
    self_ones = [swap_mp(self_one[1:], 1)]
    self_near = swap_dp(self_sums[1][:1], 2)
    extras = image_term, norm_partial, final
    late = together(first[0], second[0], first_far, second_far, self_ones, self_near, extras)
    first, second, first_far, second_far, self_ones, self_near, extras = late
    image_term, norm_partial, final = extras
    home = jnp.concatenate([added(first, first_far), added(second, second_far)], axis=-1)
    home = scatter_extra(home)
    self_low = total_of(self_kept[0], self_near[0], self_sent[0])

    kept, sent = parts(home)
    sent = swap_mp(sent, 0)
    self_ones = [swap_mp(after(self_one[:1], home), 1)] + self_ones
    final_other = swap_dp(final[slot:], 1)
    late = together(kept, sent, self_low, self_ones, image_term, final_other)
    kept, sent, self_low, self_ones, image_term, final_other = late
    self_low = added(self_low, jnp.concatenate(self_ones, axis=0))
    home = added(kept, sent)

    kept, sent = parts(home)
    sent, theirs, feed_theirs = swap_mp(sent, 1), swap_dp(self_low[1], 1), swap_dp(feed_sum[1], 1)
    image_kept, image_sent = parts(image_term.reshape(n_mp, part, dim))
    image_sent = swap_mp(image_sent, 0)
    late = together(kept, sent, self_low, theirs, feed_theirs, image_kept, image_sent)
    kept, sent, self_low, theirs, feed_theirs, image_kept, image_sent = late
    image_term = added(image_kept, image_sent)

    final_other = after(final_other, kept)
    language_out = out_of_blocks(jnp.where(is_vis, final_other, final[:slot]), lang_rows)
    vision_out = out_of_blocks(jnp.where(is_vis, final[:slot], final_other), vis_rows)

    language_grad = out_of_blocks(lang_back, lang_rows).reshape(language.shape)
    totals = [kept, sent, self_low, theirs]
    sums = call(
        prepare_kernel,
        1,
        [("whole", a) for a in [norm_partial] + totals + [feed_sum, feed_theirs]],
        [("whole", (norm_partial.shape[0] + 1, dim), F32)],
        [],
        "prepare",
        8 * dim * width,
    )[0]
    sums, their_sums = sum_up(sums)
    image_term = after(image_term, kept)
    for bit in range(1, n_bits):
        kept_part, sent_part = parts(image_term)
        image_term = added(kept_part, swap_mp(sent_part, bit))
    for bit in reversed(mp_bits()):
        image_term = jnp.concatenate([image_term, swap_mp(image_term, bit)], axis=0)
    for b in range(n_bits):
        shape = (1 << b, 2, -1, part, dim)
        flipped = image_term.reshape(shape)[:, ::-1].reshape(image_term.shape)
        image_term = jnp.where((place_mp >> b) & 1 == 1, flipped, image_term)
    axes = tuple(reversed(range(n_bits))) + (n_bits, n_bits + 1)
    image_term = image_term.reshape((2,) * n_bits + (part, dim)).transpose(axes)
    image_grad = image_term.reshape(-1, dim)[:image_count].astype(F32).reshape(images.shape)

    kinds = [("step", t) for t in (F32, F32, F32, F32, BF, F32)]
    norm_in = [
        jnp.swapaxes(a, 0, 1)
        for a in (norm_moment, norm_square, norm_weight, norm_average)
    ]
    wide_in = [jnp.swapaxes(a, 1, 2) for a in (attn_in_moment, attn_in_square, attn_in_weight, attn_in_average)]
    wide_out = [attn_out_moment, attn_out_square, attn_out_weight, attn_out_average]
    feed_in = [ffn_in_moment, ffn_in_square, ffn_in_weight, ffn_in_average]
    feed_out = [
        jnp.swapaxes(a, 1, 2)
        for a in (ffn_out_moment, ffn_out_square, ffn_out_weight, ffn_out_average)
    ]
    by_rows = "rows" if shard_rows % 48 == 0 else "whole"
    stepped = call(
        functools.partial(step_kernel, width),
        3,
        [("scalar", which)]
        + [("whole", a) for a in [sums, their_sums] + totals]
        + [(by_rows, feed_sum), (by_rows, feed_theirs)]
        + [("step", a) for a in wide_in + wide_out]
        + [(by_rows, a) for a in feed_in + feed_out]
        + [("whole", a) for a in norm_in],
        [(k, wide_in[0].shape, t) for k, t in kinds]
        + [(k, wide_out[0].shape, t) for k, t in kinds]
        + [(by_rows, feed_in[0].shape, t) for k, t in kinds * 2]
        + [("whole", norm_in[0].shape, F32)] * 5
        + [("whole", (1, 1), F32)],
        [],
        "step",
        20 * 8 * dim * width,
    )
    stepped = [jnp.swapaxes(a, 1, 2) if i < 6 or 18 <= i < 24 else a for i, a in enumerate(stepped)]
    stepped[24:29] = [jnp.swapaxes(a, 0, 1) for a in stepped[24:29]]

    results = [
        language_out.reshape(language.shape),
        vision_out.reshape(vision_cot.shape),
        language_grad,
        image_grad,
    ]
    results += stepped[:-1]
    return tuple(results) + (stepped[-1][0, 0],)


def solution(mesh):
    shape = (mesh.shape["dp"] // 4, 2, 2, mesh.shape["mp"])
    mesh = Mesh(mesh.devices.reshape(shape), DP + ("mp",))
    rows = P(DP + ("mp",), None, None)
    attn_in, attn_out = P(None, DP, None, "mp"), P(None, "mp", DP)
    ffn_in, ffn_out = P(None, DP, "mp"), P(None, "mp", DP)
    in_specs = (rows, P(DP, None, None), P(DP, None), rows, rows)
    in_specs += (attn_in,) * 4 + (attn_out,) * 4 + (ffn_in,) * 4 + (ffn_out,) * 4 + (P(),) * 4
    out_specs = (rows, rows, rows, P(DP, None, None))
    out_specs += (attn_in,) * 6 + (attn_out,) * 6 + (ffn_in,) * 6 + (ffn_out,) * 6 + (P(),) * 6
    return jax.shard_map(local, mesh=mesh, in_specs=in_specs, out_specs=out_specs, check_vma=False)
```

```python
import functools
import math

import jax
import jax.numpy as jnp
from jax import lax
from jax.experimental import pallas as pl
from jax.experimental.pallas import tpu as pltpu
from jax.sharding import Mesh
from jax.sharding import PartitionSpec as P

HEAD_DIM = 64
STEP = 10

NORM_EPS = 1e-05
CLIP_NORM = 1.0
BETA_FIRST = 0.9
BETA_SECOND = 0.999
ADAM_EPS = 1e-08
WEIGHT_DECAY = 0.01
MATRIX_RATE = 0.12
NORM_RATE = 0.8
AVERAGE_CEILING = 0.999
BF = jnp.bfloat16
F32 = jnp.float32
HIGHEST = lax.Precision.HIGHEST
SCALE = 1.0 / math.sqrt(HEAD_DIM)
DP = ("dq", "stream", "core")
VMEM_LIMIT = 56 * 1024 * 1024
GROUP = 3
MOST_ITEMS = 6


def dot_nn(a, b):
    return lax.dot_general(a, b, (((1,), (0,)), ((), ())), preferred_element_type=F32)


def dot_nt(a, b):
    return lax.dot_general(a, b, (((1,), (1,)), ((), ())), preferred_element_type=F32)


def dot_tn(a, b):
    return lax.dot_general(a, b, (((0,), (0,)), ((), ())), preferred_element_type=F32)


def norm_forward(summed, gain, shift):
    centre = jnp.mean(summed, axis=-1, keepdims=True)
    offset = summed - centre
    spread = jnp.mean(offset * offset, axis=-1, keepdims=True)
    inverse = lax.rsqrt(spread + NORM_EPS)
    normed = offset * inverse
    return normed * gain + shift, normed, inverse


def norm_backward(upstream, gain, normed, inverse):
    scaled = upstream * gain
    first_mean = jnp.mean(scaled, axis=-1, keepdims=True)
    second_mean = jnp.mean(scaled * normed, axis=-1, keepdims=True)
    inward = inverse * (scaled - first_mean - normed * second_mean)
    gain_term = jnp.sum(upstream * normed, axis=0, keepdims=True)
    shift_term = jnp.sum(upstream, axis=0, keepdims=True)
    return inward, gain_term, shift_term


def cut(block, blocks):
    rows = block.shape[0] // blocks
    return [block[i * rows : (i + 1) * rows] for i in range(blocks)]


def stack_rows(parts):
    return jnp.concatenate(parts, axis=0)


def thirds(triple, width):
    return [triple[:, i * width : (i + 1) * width] for i in range(triple.shape[1] // width)]


def lane_head(block):
    return lax.broadcasted_iota(jnp.int32, block.shape, 1) // HEAD_DIM


def spread(block):
    lanes = lane_head(block)
    zero = jnp.zeros_like(block)
    heads = block.shape[1] // HEAD_DIM
    return stack_rows([jnp.where(lanes == h, block, zero) for h in range(heads)])


def gathered(block):
    parts = cut(block, block.shape[1] // HEAD_DIM)
    lanes = lane_head(parts[0])
    out = parts[0]
    for h in range(1, len(parts)):
        out = jnp.where(lanes == h, parts[h], out)
    return out


def item_of(shape, axis, rows):
    place = lax.broadcasted_iota(jnp.int32, shape, axis)
    item = jnp.zeros(shape, jnp.int32)
    for border in range(1, MOST_ITEMS):
        item += (place >= border * rows).astype(jnp.int32)
    return item


def same_item(shape, query_rows, key_rows, heads):
    mask = item_of(shape, 0, query_rows) == item_of(shape, 1, key_rows)
    return stack_rows([mask] * heads)


def attend(query, key, value, mask, blocks):
    pairs = zip(cut(query, blocks), cut(key, blocks))
    scores = stack_rows([jnp.where(mask, dot_nt(spread(q), k) * SCALE, -1e30) for q, k in pairs])
    powered = jnp.exp(scores - jnp.max(scores, axis=-1, keepdims=True))
    probs = (powered * (1.0 / jnp.sum(powered, axis=-1, keepdims=True))).astype(BF)
    mixed = [gathered(dot_nn(p, v)) for p, v in zip(cut(probs, blocks), cut(value, blocks))]
    return probs, stack_rows(mixed).astype(BF)


def attend_back(query, key, value, probs, grad_context, blocks):
    queries, keys, values = cut(query, blocks), cut(key, blocks), cut(value, blocks)
    contexts, weights = [spread(g) for g in cut(grad_context, blocks)], cut(probs, blocks)
    grad_probs = stack_rows([dot_nt(g, v) for g, v in zip(contexts, values)])
    grad_value = stack_rows([dot_tn(p, g) for p, g in zip(weights, contexts)]).astype(BF)
    wide = probs.astype(F32)
    inner = jnp.sum(grad_probs * wide, axis=-1, keepdims=True)
    grad_scores = cut((wide * (grad_probs - inner) * SCALE).astype(BF), blocks)
    grad_query = stack_rows([gathered(dot_nn(s, k)) for s, k in zip(grad_scores, keys)])
    grad_key = stack_rows([dot_tn(s, spread(q)) for s, q in zip(grad_scores, queries)])
    return grad_query.astype(BF), grad_key.astype(BF), grad_value


def load_weight(pieces, weight, column=0):
    row = 0
    for piece in pieces:
        for part in range(piece.shape[1]):
            rows, columns = piece.shape[2:]
            weight[row : row + rows, column : column + columns] = piece[0, part]
            row += rows


def load_halves(pieces, weight):
    middle = len(pieces) // 2
    lower = pl.program_id(0) < pl.num_programs(0) // 2

    @pl.when(lower)
    def _():
        load_weight(pieces[:middle], weight)

    @pl.when(jnp.logical_not(lower))
    def _():
        load_weight(pieces[middle:], weight)


def store_pair(value, near, far, by_group=False):
    rows = near.shape[3]
    for high in range(2):
        for core, piece in enumerate((near, far)):
            for mid in range(2):
                row = (4 * high + 2 * core + mid) * rows
                spot = (high, 0, mid) if by_group else (high, mid, 0)
                piece[spot] = value[row : row + rows, :].astype(piece.dtype)


def wide_spots(place, piece, shard_rows):
    groups, _, _, streams = piece.shape[:4]
    inner = max(groups // 2, 1)
    row = 0
    for high in range(groups // inner):
        for core in range(2):
            for part in range(streams):
                for sub in range(inner):
                    group = (sub * (groups // inner) + high) ^ place[0, 0]
                    yield row, (group, core ^ place[0, 1], 0, part)
                    row += shard_rows


def load_wide(place, piece, kind, weight):
    rows = piece.shape[5]
    for row, spot in wide_spots(place, piece, rows):
        weight[row : row + rows, :] = piece[spot + (kind,)]


def store_wide(place, value, piece, kind):
    rows = piece.shape[5]
    for row, spot in wide_spots(place, piece, rows):
        piece[spot + (kind,)] = value[row : row + rows, :].astype(piece.dtype)


def partner_order(value):
    dim = value.shape[1]
    eighth = dim // 8
    row = lax.broadcasted_iota(jnp.int32, (dim, dim), 0)
    column = lax.broadcasted_iota(jnp.int32, (dim, dim), 1)
    same = jnp.ones((dim, dim), jnp.bool_)
    for border in range(2 * eighth, dim, 2 * eighth):
        same &= (row >= border) == (column >= border)
    pick = same & (jnp.abs(row - column) == eighth)
    return dot_nn(value, jnp.where(pick, 1.0, 0.0).astype(BF)).astype(BF)


def widen(value, blocks, rows):
    empty = jnp.zeros((rows - value.shape[0] // blocks, value.shape[1]), value.dtype)
    return stack_rows([part for block in cut(value, blocks) for part in (block, empty)])


def cross_forward_kernel(width, blocks, words, regions, stream, lang, vis, norm, *refs):
    first, second, refs = refs[:8], refs[8:16], refs[16:]
    own_one, other_one, lang_n, lang_r, vis_n, vis_r = refs[:6]
    lang_qkv, vis_qkv, lang_ctx, vis_ctx, lang_p, vis_p = refs[6:12]
    weight, lang_acc, vis_acc = refs[12:]
    load_weight(first, weight)
    load_weight(second, weight, first[0].shape[3])
    step = pl.program_id(0)

    @pl.when(step == 0)
    def _():
        lang_acc[...] = lang[...].astype(F32)
        vis_acc[...] = vis[...].astype(F32)

    full = weight[...]
    in_part, out_part = full[:, : 3 * width], full[:, 3 * width :]
    lang_triple = dot_nn(lang[...], in_part).astype(BF)
    vis_triple = dot_nn(vis[...], in_part).astype(BF)
    lang_qkv[0] = lang_triple
    vis_qkv[0] = vis_triple
    lang_query, lang_key, lang_value = thirds(lang_triple, width)
    vis_query, vis_key, vis_value = thirds(vis_triple, width)
    heads = width // HEAD_DIM
    lang_block, vis_block = lang.shape[0] // blocks, vis.shape[0] // blocks
    lang_mask = same_item((lang_block, vis_block), words, regions, heads)
    vis_mask = same_item((vis_block, lang_block), regions, words, heads)
    for query, key, value, probs_ref, ctx_ref, acc, mask in (
        (lang_query, vis_key, vis_value, lang_p, lang_ctx, lang_acc, lang_mask),
        (vis_query, lang_key, lang_value, vis_p, vis_ctx, vis_acc, vis_mask),
    ):
        probs, context = attend(query, key, value, mask, blocks)
        probs_ref[0] = probs
        ctx_ref[0] = context
        acc[...] += dot_nt(context, out_part)

    @pl.when(step == pl.num_programs(0) - 1)
    def _():
        ones = []
        for acc, n_ref, r_ref in ((lang_acc, lang_n, lang_r), (vis_acc, vis_n, vis_r)):
            out, normed, inverse = norm_forward(acc[...], norm[0:1, :], norm[1:2, :])
            ones.append(out.astype(BF))
            n_ref[...] = normed
            r_ref[...] = inverse
        lang_one, vis_one = widen(ones[0], blocks, vis_block), ones[1]
        is_vis = stream[0, 0] == 1
        own_one[...] = jnp.where(is_vis, vis_one, lang_one)
        other_one[...] = partner_order(jnp.where(is_vis, lang_one, vis_one))


def self_forward_step(width, blocks, length, rows, pieces, weight, qkv, ctx, probs_ref):
    load_weight(pieces, weight)
    full = weight[...]
    in_part, out_part = full[:, : 3 * width], full[:, 3 * width :]
    triple = dot_nn(rows[...], in_part).astype(BF)
    qkv[0] = triple
    block = rows.shape[0] // blocks
    mask = same_item((block, block), length[0, 0], length[0, 0], width // HEAD_DIM)
    probs, context = attend(*thirds(triple, width), mask, blocks)
    probs_ref[0] = probs
    ctx[0] = context
    return dot_nt(context, out_part)


def self_first_kernel(width, blocks, length, own, other, *refs):
    pieces, (acc, qkv, ctx, probs, weight, rows) = refs[:4], refs[4:]

    @pl.when(pl.program_id(0) == 0)
    def _():
        rows[...] = stack_rows([own[...], other[...]])
        acc[...] = rows[...].astype(F32)

    acc[...] += self_forward_step(width, blocks, length, rows, pieces, weight, qkv, ctx, probs)


def self_second_kernel(width, blocks, length, own, other, norm, summed, *refs):
    pieces, refs = refs[:4], refs[7:]
    two, n_ref, r_ref, qkv, ctx, probs, weight, acc, rows = refs
    step = pl.program_id(0)

    @pl.when(step == 0)
    def _():
        rows[...] = stack_rows([own[...], other[...]])
        acc[...] = summed[...]

    acc[...] += self_forward_step(width, blocks, length, rows, pieces, weight, qkv, ctx, probs)

    @pl.when(step == pl.num_programs(0) - 1)
    def _():
        out, normed, inverse = norm_forward(acc[...], norm[0:1, :], norm[1:2, :])
        two[...] = out.astype(BF)
        n_ref[...] = normed
        r_ref[...] = inverse


def feed_kernel(place, rows, normed_two, inverse, cot, norm, piece, *refs):
    three, grads, down_ref, self_gain, self_shift, feed_gain, feed_shift, refs = refs[:7] + (refs[7:],)
    weight_in, weight_out, active, slope, acc, branch, branch_turned, turned = refs
    step, groups = pl.program_id(0), pl.num_programs(0) // 2
    group = lax.rem(step, groups)

    @pl.when(step == 0)
    def _():
        acc[...] = normed_two[...] * norm[0:1, :] + norm[1:2, :]
        turned[...] = rows[...].T

    @pl.when(step < groups)
    def _():
        load_wide(place, piece, 0, weight_in.at[group])
        load_wide(place, piece, 1, weight_out.at[group])
        hidden = dot_nn(rows[...], weight_in[group])
        normal = 0.5 * (1.0 + lax.erf(hidden * 0.7071067811865476))
        slopes = normal + hidden * jnp.exp(-0.5 * hidden * hidden) * 0.3989422804014327
        actives = (hidden * normal).astype(BF)
        active[group] = actives
        slope[group] = slopes.astype(BF)
        acc[...] += dot_nt(actives, weight_out[group])

    @pl.when(step == groups - 1)
    def _():
        gain = norm[2:3, :]
        out, normed, inverse_three = norm_forward(acc[...], gain, norm[3:4, :])
        three[...] = out.astype(BF)
        inward, gain_term, shift_term = norm_backward(
            cot[...].astype(F32), gain, normed, inverse_three
        )
        acc[...] = inward
        branch[...] = inward.astype(BF)
        branch_turned[...] = inward.astype(BF).T
        feed_gain[...] = gain_term
        feed_shift[...] = shift_term

    @pl.when(step >= groups)
    def _():
        store_wide(place, dot_nn(branch_turned[...], active[group]), grads, 1)
        grad_active = dot_nn(branch[...], weight_out[group])
        grad_hidden = (grad_active * slope[group].astype(F32)).astype(BF)
        store_wide(place, dot_nn(turned[...], grad_hidden), grads, 0)
        acc[...] += dot_nt(grad_hidden, weight_in[group])

    @pl.when(step == 2 * groups - 1)
    def _():
        down, gain_term, shift_term = norm_backward(
            acc[...], norm[0:1, :], normed_two[...], inverse[...]
        )
        down_ref[...] = down
        self_gain[...] = gain_term
        self_shift[...] = shift_term


def self_other_kernel(width, blocks, inward, qkv, probs, *refs):
    pieces, (triple_ref, down, weight, acc, branch) = refs[:8], refs[8:]
    load_halves(pieces, weight)
    step = pl.program_id(0)

    @pl.when(step == 0)
    def _():
        acc[...] = inward[...]
        branch[...] = inward[...].astype(BF)

    full = weight[...]
    in_part, out_part = full[:, : 3 * width], full[:, 3 * width :]
    grad_context = dot_nn(branch[...], out_part).astype(BF)
    grads_of = attend_back(*thirds(qkv[0], width), probs[0], grad_context, blocks)
    grad_triple = jnp.concatenate(grads_of, axis=1)
    triple_ref[0] = grad_triple
    acc[...] += dot_nt(grad_triple, in_part)

    @pl.when(step == pl.num_programs(0) - 1)
    def _():
        down[...] = partner_order(acc[...].astype(BF))


def self_own_kernel(width, blocks, inward, own, other, qkv, ctx, probs, other_triple, *refs):
    pieces, near, far, refs = refs[:8], refs[8], refs[9], refs[10:]
    down, weight, acc, branch, turned, branch_turned = refs
    load_halves(pieces, weight)
    step = pl.program_id(0)

    @pl.when(step == 0)
    def _():
        slot = own.shape[0]
        acc[...] = inward[:slot, :]
        gradient = inward[...].astype(BF)
        branch[...] = gradient[:slot]
        branch_turned[...] = gradient.T
        turned[...] = stack_rows([own[...], other[...]]).T

    full = weight[...]
    in_part, out_part = full[:, : 3 * width], full[:, 3 * width :]
    grad_context = dot_nn(branch[...], out_part).astype(BF)
    grads_of = attend_back(*thirds(qkv[0], width), probs[0], grad_context, blocks)
    grad_triple = jnp.concatenate(grads_of, axis=1)
    in_grad = dot_nn(turned[...], stack_rows([grad_triple, other_triple[0]])).astype(BF)
    out_grad = dot_nn(branch_turned[...], ctx[0]).astype(BF)
    store_pair(jnp.concatenate([in_grad, out_grad], axis=1), near, far, True)
    acc[...] += dot_nt(grad_triple, in_part)

    @pl.when(step == pl.num_programs(0) - 1)
    def _():
        down[...] = acc[...].astype(BF)


def cross_backward_kernel(
    width,
    blocks,
    stream,
    own_up,
    other_up,
    lang,
    vis,
    lang_n,
    lang_r,
    vis_n,
    vis_r,
    norm,
    order,
    source,
    targets,
    *refs,
):
    lang_qkv, vis_qkv, lang_ctx, vis_ctx, lang_p, vis_p = refs[:6]
    first, second, refs = refs[6:14], refs[14:22], refs[22:]
    near, far, lang_out, image_out, gain_ref, shift_ref = refs[:6]
    weight, lang_acc, vis_acc, lang_branch, vis_branch, turned, branch_turned = refs[6:]
    load_weight(first, weight)
    load_weight(second, weight, first[0].shape[3])
    step = pl.program_id(0)

    @pl.when(step == 0)
    def _():
        is_vis = stream[0, 0] == 1
        own, other = own_up[...].astype(F32), other_up[...].astype(F32)
        lang_block = lang.shape[0] // blocks
        lang_up = cut(jnp.where(is_vis, other, own), blocks)
        lang_up = stack_rows([block[:lang_block] for block in lang_up])
        vis_up = jnp.where(is_vis, own, other)
        gain_total, shift_total = 0.0, 0.0
        for up, n_ref, r_ref, acc, branch in (
            (lang_up, lang_n, lang_r, lang_acc, lang_branch),
            (vis_up, vis_n, vis_r, vis_acc, vis_branch),
        ):
            inward, gain_term, shift_term = norm_backward(
                up, norm[0:1, :], n_ref[...], r_ref[...]
            )
            acc[...] = inward
            branch[...] = inward.astype(BF)
            gain_total += gain_term
            shift_total += shift_term
        gain_ref[...] = gain_total
        shift_ref[...] = shift_total
        turned[...] = stack_rows([lang[...], vis[...]]).T
        branch_turned[...] = stack_rows([lang_branch[...], vis_branch[...]]).T

    full = weight[...]
    in_part, out_part = full[:, : 3 * width], full[:, 3 * width :]
    lang_gc = dot_nn(lang_branch[...], out_part).astype(BF)
    vis_gc = dot_nn(vis_branch[...], out_part).astype(BF)
    lang_query, lang_key, lang_value = thirds(lang_qkv[0], width)
    vis_query, vis_key, vis_value = thirds(vis_qkv[0], width)
    lang_dq, vis_dk, vis_dv = attend_back(
        lang_query, vis_key, vis_value, lang_p[0], lang_gc, blocks
    )
    vis_dq, lang_dk, lang_dv = attend_back(
        vis_query, lang_key, lang_value, vis_p[0], vis_gc, blocks
    )
    lang_grad = jnp.concatenate([lang_dq, lang_dk, lang_dv], axis=1)
    vis_grad = jnp.concatenate([vis_dq, vis_dk, vis_dv], axis=1)
    in_grad = dot_nn(turned[...], stack_rows([lang_grad, vis_grad]))
    out_grad = dot_nn(branch_turned[...], stack_rows([lang_ctx[0], vis_ctx[0]]))
    grad = jnp.concatenate([in_grad.astype(BF), out_grad.astype(BF)], axis=1)
    store_pair(grad, near, far)
    lang_acc[...] += dot_nt(lang_grad, in_part)
    vis_acc[...] += dot_nt(vis_grad, in_part)

    @pl.when(step == pl.num_programs(0) - 1)
    def _():
        lang_out[...] = dot_nt(lang_acc[...].astype(BF), order[...])
        chooser = jnp.where(source[...] == targets[...], 1.0, 0.0).astype(BF)
        image = dot_tn(chooser, vis_acc[...].astype(BF)).astype(BF)
        image_out[...] = dot_nt(image, order[...]).astype(BF)


def store_step(state, clip, outs):
    new = adamw_step(*state, MATRIX_RATE, clip)
    for (ref, place), value in zip(outs, new[:4] + (new[3], new[4])):
        ref[place] = value.astype(ref.dtype)


def prepare_kernel(norms, kept, sent, self_low, self_theirs, feed_sum, feed_theirs, sums):
    home = kept[...].astype(F32) + sent[...].astype(F32)
    squares = jnp.sum(home * home, keepdims=True)[0]
    for value in (self_low[0], self_theirs[...]):
        wide = value.astype(F32)
        squares += jnp.sum(wide * wide, keepdims=True)
    for kind in range(feed_theirs.shape[0]):
        for value in (feed_sum[0, kind], feed_theirs[kind]):
            wide = value.astype(F32)
            squares += jnp.sum(wide * wide, keepdims=True)
    count = norms.shape[0]
    sums[:count, :] = norms[...]
    sums[count:, :] = jnp.broadcast_to(squares, (1, norms.shape[1]))


def step_kernel(
    width, stream, sums, theirs, kept, sent, self_low, self_theirs, feed_sum, feed_theirs, *refs
):
    ins, outs, feed_in, feed_out, norm_in = (refs[4 * i : 4 * i + 4] for i in range(5))
    refs = refs[20:]
    step = pl.program_id(0)
    @pl.when(step == 0)
    def _():
        total = sums[...] + theirs[...]
        norm_grad = total[:-1]
        squares = jnp.sum(norm_grad * norm_grad, keepdims=True) + total[-1:, 0:1]
        grad_norm = jnp.sqrt(squares)
        clip = CLIP_NORM / jnp.maximum(grad_norm, CLIP_NORM)
        refs[-2][...] = grad_norm
        refs[-1][...] = clip
        for place in range(norm_in[0].shape[0]):
            state = [ref[place] for ref in norm_in]
            new = adamw_step(norm_grad[2 * place : 2 * place + 2], *state, NORM_RATE, clip)
            for ref, value in zip(refs[24:29], new):
                ref[place] = value

    clip = refs[-1][...]
    is_vis = stream[0, 0] == 1

    def by_stream(mine, other):
        mine, other = mine.astype(F32), other.astype(F32)
        return jnp.where(is_vis, other, mine), jnp.where(is_vis, mine, other)

    home = kept[0].astype(F32) + sent[0].astype(F32)
    one, two = by_stream(self_low[0], self_theirs[...])
    grad = jnp.where(step == 0, home, jnp.where(step == 1, one, two))
    for kind in range(3):
        part = grad[:, kind * width : (kind + 1) * width]
        store_step([part] + [ref[0, kind] for ref in ins], clip, [(r, (0, kind)) for r in refs[:6]])
    part = grad[:, 3 * width :].T
    store_step([part] + [ref[0] for ref in outs], clip, [(r, 0) for r in refs[6:12]])
    for kind, state_in, first in ((0, feed_in, 12), (1, feed_out, 18)):
        for place, part in enumerate(by_stream(feed_sum[0, kind], feed_theirs[kind])):
            state = [part] + [ref[place] for ref in state_in]
            store_step(state, clip, [(r, place) for r in refs[first : first + 6]])


def whole(shape):
    return pl.BlockSpec(shape, lambda m: (0,) * len(shape))


def per_step(shape):
    rest = (0,) * (len(shape) - 1)
    return pl.BlockSpec((1,) + tuple(shape[1:]), lambda m: (m,) + rest)


def part_of(shape, pick):
    rest = (0,) * (len(shape) - 1)
    return pl.BlockSpec((1,) + tuple(shape[1:]), lambda m: (pick(m),) + rest)


def group_of(shape, pick):
    block = (shape[0], shape[1], 1) + tuple(shape[3:])
    return pl.BlockSpec(block, lambda m: (0, 0, pick(m), 0, 0, 0, 0))


def call(kernel, steps, ins, outs, scratch, name, flops, aliases=()):
    spec = {
        "whole": lambda s: whole(s),
        "step": lambda s: per_step(s),
        "early": lambda s: group_of(s, lambda m: jnp.minimum(m, s[2] - 1)),
        "late": lambda s: group_of(s, lambda m: jnp.maximum(m - s[2], 0)),
        "low": lambda s: part_of(s, lambda m: jnp.minimum(m, s[0] - 1)),
        "high": lambda s: part_of(s, lambda m: jnp.maximum(m - s[0], 0)),
        "rows": lambda s: pl.BlockSpec(
            tuple(s[:-2]) + (s[-2] // steps, s[-1]), lambda m: (0,) * (len(s) - 2) + (m, 0)
        ),
        "pair": lambda s: pl.BlockSpec(
            tuple(s[:2]) + (1,) + tuple(s[3:]), lambda m: (0, 0, m, 0, 0)
        ),
        "groups": lambda s: pl.BlockSpec(
            (s[0], 1) + tuple(s[2:]), lambda m: (0, m, 0, 0, 0)
        ),
        "upper": lambda s: part_of(s, lambda m: m + s[0] // 2),
        "own": lambda s: pl.BlockSpec((1, s[1] // 2, s[2]), lambda m: (m, 0, 0)),
        "other": lambda s: pl.BlockSpec((1, s[1] // 2, s[2]), lambda m: (m, 1, 0)),
        "other_rows": lambda s: pl.BlockSpec((s[0] // 2, s[1]), lambda m: (1, 0)),
        "kept": lambda s: pl.BlockSpec(memory_space=pl.ANY),
        "scalar": lambda s: pl.BlockSpec(memory_space=pltpu.SMEM),
    }
    moved = sum(a.size * a.dtype.itemsize for _, a in ins)
    moved += sum(math.prod(s) * jnp.dtype(t).itemsize for _, s, t in outs)
    return pl.pallas_call(
        kernel,
        grid=(steps,),
        in_specs=[spec[kind](a.shape) for kind, a in ins],
        out_specs=[spec[kind](s) for kind, s, _ in outs],
        out_shape=[jax.ShapeDtypeStruct(s, t) for _, s, t in outs],
        scratch_shapes=[pltpu.VMEM(s, t) for s, t in scratch],
        input_output_aliases=dict(aliases),
        compiler_params=pltpu.CompilerParams(
            vmem_limit_bytes=VMEM_LIMIT, dimension_semantics=("arbitrary",)
        ),
        cost_estimate=pl.CostEstimate(flops=flops, bytes_accessed=moved, transcendentals=0),
        name=name,
    )(*[a for _, a in ins])


def swap_dp(value, bit):
    axis, place = (("core", 0), ("stream", 0), ("dq", bit - 2))[min(bit, 2)]
    count = lax.axis_size(axis)
    return lax.ppermute(value, axis, [(i, i ^ (1 << place)) for i in range(count)])


def swap_mp(value, bit):
    count = lax.axis_size("mp")
    return lax.ppermute(value, "mp", [(i, i ^ (1 << bit)) for i in range(count)])


def after(value, *others):
    flat, tree = jax.tree.flatten(value)
    kept = lax.optimization_barrier((flat, jax.tree.leaves(others)))[0]
    return jax.tree.unflatten(tree, kept)


def together(*values):
    return lax.optimization_barrier(values)


def swap_mask(value, axis, mask):
    count = lax.axis_size(axis)
    return lax.ppermute(value, axis, [(i, i ^ mask) for i in range(count)])


def sum_up(value):
    count = lax.axis_size("mp")
    mask = 1
    while mask < count:
        if 2 * mask < count:
            theirs = [swap_mask(value, "mp", mask * k) for k in (1, 2, 3)]
            value = (value + theirs[0]) + (theirs[1] + theirs[2])
            mask *= 4
        else:
            value += swap_mask(value, "mp", mask)
            mask *= 2
    both = ("dq", "stream")
    count = lax.axis_size(both)
    mask = 1
    while mask < count:
        if 2 * mask < count:
            theirs = [swap_mask(value, both, mask * k) for k in (1, 2, 3)]
            value = (value + theirs[0]) + (theirs[1] + theirs[2])
            mask *= 4
        else:
            value += swap_mask(value, both, mask)
            mask *= 2
    return value, swap_dp(value, 0)


def extra_bits():
    return range(3, 2 + int(math.log2(lax.axis_size("dq"))))


def mp_bits():
    return range(int(math.log2(lax.axis_size("mp"))))


def gather_mp(current):
    for bit in reversed(mp_bits()):
        current = jnp.concatenate([current, swap_mp(current, bit)], axis=0)
    return current


def gather_extra(current):
    for bit in extra_bits():
        current = jnp.concatenate([current, swap_dp(current, bit)], axis=2)
    return current


def scatter_mp(current):
    for bit in mp_bits():
        half = current.shape[0] // 2
        current = added(current[:half], swap_mp(current[half:], bit))
    return current


def scatter_extra(current):
    for bit in reversed(extra_bits()):
        low, high = jnp.split(current, 2, axis=-2)
        current = added(low, swap_dp(high, bit))
    return current


def added(mine, theirs):
    return (mine.astype(F32) + theirs.astype(F32)).astype(BF)


def grow(found, place, bit):
    for key in list(found):
        new = list(key)
        new[place] = 1
        found[tuple(new)] = swap_dp(found[key], bit)


def shrink(found, place, bit):
    for key in [k for k in found if k[place] == 0]:
        far = list(key)
        far[place] = 1
        found[key] = added(found[key], swap_dp(found.pop(tuple(far)), bit))


def home_list(found):
    return [found[(hi, mid, lo)] for hi in (0, 1) for lo in (0, 1) for mid in (0, 1)]


def stream_list(found):
    return [found[(hi, lo)] for hi in (0, 1) for lo in (0, 1)]


def home_keys(arrays):
    return {(i >> 2, i & 1, (i >> 1) & 1): a for i, a in enumerate(arrays)}


def stream_keys(arrays):
    return {(i >> 1, i & 1): a for i, a in enumerate(arrays)}


def adamw_step(gradient, moment, square, weight, average, rate, clip_scale):
    average_decay = min(AVERAGE_CEILING, (1.0 + STEP) / (10.0 + STEP))
    clipped = gradient * clip_scale
    moment_new = BETA_FIRST * moment + (1.0 - BETA_FIRST) * clipped
    square_new = BETA_SECOND * square + (1.0 - BETA_SECOND) * clipped * clipped
    corrected = moment_new / (1.0 - BETA_FIRST**STEP)
    denominator = jnp.sqrt(square_new / (1.0 - BETA_SECOND**STEP)) + ADAM_EPS
    weight_new = weight - rate * (corrected / denominator + WEIGHT_DECAY * weight)
    average_new = average_decay * average + (1.0 - average_decay) * weight_new
    return (clipped, moment_new, square_new, weight_new, average_new)


def pad_rows(block, rows):
    return jnp.pad(block, ((0, rows - block.shape[0]), (0, 0)))


def local(
    language,
    images,
    counts,
    language_cot,
    vision_cot,
    attn_in_weight,
    attn_in_moment,
    attn_in_square,
    attn_in_average,
    attn_out_weight,
    attn_out_moment,
    attn_out_square,
    attn_out_average,
    ffn_in_weight,
    ffn_in_moment,
    ffn_in_square,
    ffn_in_average,
    ffn_out_weight,
    ffn_out_moment,
    ffn_out_square,
    ffn_out_average,
    norm_weight,
    norm_moment,
    norm_square,
    norm_average,
):
    n_dp, n_mp = lax.axis_size(DP), lax.axis_size("mp")
    me = lax.axis_index(DP)
    stream = (me >> 1) & 1
    is_vis = stream == 1
    own_items, words, dim = language.shape
    regions = images.shape[1]
    blocks = own_items // GROUP
    lang_block, vis_block = (-(-GROUP * rows // 16) * 16 for rows in (words, regions))
    lang_pad, slot = blocks * lang_block, blocks * vis_block
    total = 2 * slot
    shard_rows = attn_in_weight.shape[1]
    width = attn_in_weight.shape[3]
    units = ffn_in_weight.shape[2]
    heads = width // HEAD_DIM
    half = 2 * width
    eighth = dim // 8

    def mine_first(pair):
        return jnp.where(is_vis, pair[1], pair[0]), jnp.where(is_vis, pair[0], pair[1])

    attn_shards = [
        jnp.concatenate(
            [attn_in_weight[b].reshape(shard_rows, 3 * width), attn_out_weight[b].T], axis=1
        ).astype(BF)[None, None]
        for b in range(3)
    ]
    def pair_up(shards, *pins):
        own, other = mine_first(shards)
        return jnp.concatenate([own, swap_dp(after(other, *pins), 1)], axis=1)

    halves = [attn_shards[0][..., c : c + half] for c in (0, half)]
    self_pair = pair_up(attn_shards[1:])
    for bit in reversed(mp_bits()):
        halves = [jnp.concatenate([h, swap_mp(h, bit)], axis=0) for h in halves]
        if bit == mp_bits()[-1]:
            feed_own, feed_other = mine_first(
                [jnp.stack([ffn_in_weight[s].astype(BF), ffn_out_weight[s].T.astype(BF)]) for s in range(2)]
            )
            feed_pair = jnp.stack([feed_own, swap_dp(feed_other, 1)])
            feed_w = lax.all_gather(after(feed_pair, halves), ("dq", "core", "mp"), axis=0)
            feed_w = feed_w.reshape((n_dp // 4, 2, n_mp) + feed_pair.shape)
    first, second = ({(0, 0, 0): gather_extra(h)} for h in halves)

    def gather_step(current, index):
        return jnp.concatenate([current, swap_mp(current, mp_bits()[-1 - index])], axis=0)

    n_bits = len(mp_bits())
    self_low = self_pair
    for index in range(n_bits - 1):
        self_low = gather_step(self_low, index)
    grow(first, 0, 2)
    grow(second, 1, 1)

    place = jnp.arange(dim, dtype=jnp.int32)
    block = place // shard_rows
    sub, high = block % (n_dp // 8), block // (n_dp // 8)
    relative = 8 * sub + 4 * (high >> 2) + ((high >> 1) & 1) + 2 * (high & 1)
    origin = (relative ^ me) * shard_rows + place % shard_rows
    order = (place[:, None] == origin[None, :]).astype(BF)

    def to_order(value):
        return dot_nn(value, order).astype(BF)

    def from_order(value, precision=None):
        return lax.dot_general(
            value, order, (((1,), (1,)), ((), ())), preferred_element_type=F32, precision=precision
        )

    norm_ordered = lax.dot_general(
        norm_weight.reshape(-1, dim),
        order.astype(F32),
        (((1,), (0,)), ((), ())),
        precision=HIGHEST,
        preferred_element_type=F32,
    ).reshape(norm_weight.shape)
    norm_cross = norm_ordered[:, 0]
    norm_self = jnp.where(is_vis, norm_ordered[:, 2], norm_ordered[:, 1])
    norm_feed = jnp.where(is_vis, norm_ordered[:, 4], norm_ordered[:, 3])
    norm_pair = jnp.concatenate([norm_self, norm_feed], axis=0)

    def in_blocks(value, rows, target):
        value = value.reshape(blocks, rows, dim)
        value = jnp.pad(value, ((0, 0), (0, target - rows), (0, 0)))
        return value.reshape(blocks * target, dim)

    def out_of_blocks(value, rows):
        return value.reshape(blocks, -1, dim)[:, :rows].reshape(blocks * rows, dim)

    lang_rows, vis_rows = GROUP * words, GROUP * regions
    first_item = lax.axis_index("mp") * own_items
    bounds = jnp.cumsum(counts[0])
    positions = first_item + jnp.arange(own_items, dtype=jnp.int32)
    item_image = jnp.sum((bounds[None, :] <= positions[:, None]).astype(jnp.int32), axis=1)
    region = jnp.arange(regions, dtype=jnp.int32)
    row_source = (item_image[:, None] * regions + region[None, :]).reshape(blocks, vis_rows) + 1
    row_source = jnp.pad(row_source, ((0, 0), (0, vis_block - vis_rows))).reshape(slot, 1)
    image_count = images.shape[0] * regions
    picker = (row_source == 1 + jnp.arange(image_count, dtype=jnp.int32)[None, :]).astype(BF)
    lang = to_order(in_blocks(language, lang_rows, lang_block))
    image_rows = to_order(images.reshape(-1, dim))
    vis = dot_nn(picker, image_rows).astype(BF)

    lang_cot = in_blocks(language_cot, lang_rows, vis_block)
    vis_cot = in_blocks(vision_cot, vis_rows, vis_block)
    cot_own, cot_other = mine_first((lang_cot, vis_cot))

    length = jnp.where(is_vis, regions, words).astype(jnp.int32).reshape(1, 1)

    first, second = after((first, second), lang, vis)
    grow(first, 1, 1)
    grow(second, 0, 2)
    self_low = {(0, 0): gather_extra(self_low)}
    self_high = {(0, 0): swap_mp(self_low[(0, 0)], 0)}
    grow(first, 2, 0)
    grow(second, 2, 0)
    pieces = lambda arrays: [("step", a) for a in arrays]
    which = stream.astype(jnp.int32).reshape(1, 1)
    ins = [("scalar", which)] + [("whole", a) for a in (lang, vis, norm_cross)]
    outs = [("whole", (slot, dim), BF)] * 2
    for rows in (lang_pad, slot):
        outs += [("whole", (rows, dim), F32), ("whole", (rows, 1), F32)]
    outs += [("step", (n_mp, rows, 3 * width), BF) for rows in (lang_pad, slot)]
    outs += [("step", (n_mp, rows, width), BF) for rows in (lang_pad, slot)]
    outs += [
        ("step", (n_mp, heads * lang_pad, vis_block), BF),
        ("step", (n_mp, heads * slot, lang_block), BF),
    ]
    both = lang_pad + slot
    cross_w = home_list(first) + home_list(second)
    cross_w = after(cross_w, self_low)
    grow(self_low, 0, 2)
    found = call(
        functools.partial(cross_forward_kernel, width, blocks, words, regions),
        n_mp,
        ins + pieces(cross_w),
        outs,
        [((dim, 4 * width), BF), ((lang_pad, dim), F32), ((slot, dim), F32)],
        "cross_forward",
        12 * both * dim * 4 * width * n_mp,
    )
    own_one, other_one, lang_n, lang_r, vis_n, vis_r = found[:6]
    cross_saved = found[6:]

    other_one = swap_dp(other_one, 1)
    self_high, self_low, cot_other = after((self_high, self_low, cot_other), other_one)
    grow(self_high, 0, 2)
    grow(self_low, 1, 0)
    half_groups = n_mp // 2
    saved = [
        (n_mp, total, 3 * width),
        (n_mp, total, width),
        (n_mp, heads * total, vis_block),
    ]
    first_half = call(
        functools.partial(self_first_kernel, width, 2 * blocks),
        half_groups,
        [("scalar", length)]
        + [("whole", a) for a in (own_one, other_one)]
        + [("step", a) for a in stream_list(self_low)],
        [("whole", (total, dim), F32)] + [("step", a, BF) for a in saved],
        [((dim, 4 * width), BF), ((total, dim), BF)],
        "self_first",
        6 * total * dim * 4 * width * n_mp,
    )
    self_high, cot_theirs = after((self_high, swap_dp(cot_other, 1)), first_half[0])
    grow(self_high, 1, 0)
    self_pieces = [("low", a) for a in stream_list(self_low)]
    self_pieces += [("high", a) for a in stream_list(self_high)]
    rows_two, normed_two, inverse_two, self_qkv, self_ctx, self_probs = call(
        functools.partial(self_second_kernel, width, 2 * blocks),
        half_groups,
        [("scalar", length)]
        + [("whole", a) for a in (own_one, other_one, norm_self, first_half[0])]
        + [("step", a) for a in stream_list(self_high)]
        + [("kept", a) for a in first_half[1:]],
        [("whole", (total, dim), BF), ("whole", (total, dim), F32), ("whole", (total, 1), F32)]
        + [("upper", a, BF) for a in saved],
        [((dim, 4 * width), BF), ((total, dim), F32), ((total, dim), BF)],
        "self_second",
        6 * total * dim * 4 * width * n_mp,
        [(9 + i, 3 + i) for i in range(3)],
    )
    cot = to_order(jnp.concatenate([cot_own, cot_theirs], axis=0))
    spot = jnp.stack([me >> 2, me & 1]).astype(jnp.int32).reshape(1, 2)

    whole_row = ("whole", (1, dim), F32)
    rows_three, feed_g, inward, self_gain, self_shift, feed_gain, feed_shift = call(
        feed_kernel,
        2 * n_mp,
        [("scalar", spot)]
        + [("whole", a) for a in (rows_two, normed_two, inverse_two, cot, norm_pair)]
        + [("early", feed_w)],
        [("whole", (total, dim), BF), ("late", feed_w.shape, BF), ("whole", (total, dim), F32)]
        + [whole_row] * 4,
        [((n_mp, dim, units), BF)] * 2
        + [((n_mp, total, units), BF)] * 2
        + [((total, dim), F32), ((total, dim), BF), ((dim, total), BF), ((dim, total), BF)],
        "feed",
        24 * total * dim * units * n_mp,
    )

    feed_sum = lax.psum_scatter(
        (feed_g * (1 + 0 * (me < 0)).astype(BF)).reshape((-1,) + feed_pair.shape), ("dq", "core", "mp"), scatter_dimension=0, tiled=True
    )[0]

    def core_step(found, *pins):
        theirs = [swap_dp(found[(hi, 1)], 0) for hi in (0, 1)]
        return [found[(hi, 0)] for hi in (0, 1)], after(theirs, *pins)

    def split(mine, theirs):
        middle = mine.shape[0] // 2
        return added(mine[:middle], theirs[:middle]), added(mine[middle:], theirs[middle:])

    def send_mp(parts, bit):
        return [(keep, swap_mp(far, bit)) for keep, far in parts]

    other_triple, other_up = call(
        functools.partial(self_other_kernel, width, blocks),
        n_mp,
        [("other_rows", inward), ("other", self_qkv), ("other", self_probs)] + self_pieces,
        [("step", (n_mp, slot, 3 * width), BF), ("whole", (slot, dim), BF)],
        [((dim, 4 * width), BF), ((slot, dim), F32), ((slot, dim), BF)],
        "self_other",
        2 * total * dim * 4 * width * n_mp,
    )
    other_up = swap_dp(other_up, 1)
    self_near, self_far, own_up = call(
        functools.partial(self_own_kernel, width, blocks),
        n_mp,
        [("whole", a) for a in (inward, own_one, other_one)]
        + [("own", self_qkv), ("step", self_ctx), ("own", self_probs), ("step", other_triple)]
        + self_pieces,
        [("groups", (2, n_mp, 2, eighth, 4 * width), BF)] * 2 + [("whole", (slot, dim), BF)],
        [((dim, 4 * width), BF), ((slot, dim), F32), ((slot, dim), BF)] + [((dim, total), BF)] * 2,
        "self_own",
        2 * total * dim * 4 * width * n_mp,
    )
    self_near, self_far, own_up, other_up = together(self_near, self_far, own_up, other_up)
    self_far = swap_dp(self_far, 0)
    self_sums = [scatter_extra(added(self_near[hi], self_far[hi])) for hi in (0, 1)]
    own_up = after(own_up, self_sums)
    place_mp = lax.axis_index("mp")
    part = -(-image_count // n_mp // 16) * 16
    index = jnp.arange(n_mp, dtype=jnp.int32)
    far = sum(((index >> b) & 1) << (n_bits - 1 - b) for b in range(n_bits))
    rows = ((far ^ place_mp)[:, None] * part + jnp.arange(part, dtype=jnp.int32)[None, :]).reshape(1, -1)
    found = call(
        functools.partial(cross_backward_kernel, width, blocks),
        n_mp,
        [("scalar", which)]
        + [("whole", a) for a in (own_up, other_up, lang, vis)]
        + [("whole", a) for a in (lang_n, lang_r, vis_n, vis_r, norm_cross)]
        + [("whole", a) for a in (order, row_source, 1 + rows)]
        + [("step", a) for a in cross_saved]
        + pieces(cross_w),
        [("pair", (2, 2, n_mp, eighth, 4 * width), BF)] * 2
        + [
            ("whole", (lang_pad, dim), F32),
            ("whole", (n_mp * part, dim), BF),
            ("whole", (1, dim), F32),
            ("whole", (1, dim), F32),
        ],
        [
            ((dim, 4 * width), BF),
            ((lang_pad, dim), F32),
            ((slot, dim), F32),
            ((lang_pad, dim), BF),
            ((slot, dim), BF),
            ((dim, both), BF),
            ((dim, both), BF),
        ],
        "cross_backward",
        6 * both * dim * 4 * width * n_mp,
    )
    near, far, lang_back, image_term, cross_gain, cross_shift = found

    def parts(value):
        middle = value.shape[0] // 2
        return value[:middle], value[middle:]

    def total_of(*terms):
        return functools.reduce(jnp.add, [t.astype(F32) for t in terms]).astype(BF)

    self_kept = self_sums[0]
    self_far = swap_dp(self_sums[1][1:], 2)
    late = together(near, far, lang_back, image_term, self_far, cross_gain, cross_shift)
    near, far, lang_back, image_term, self_far, cross_gain, cross_shift = late
    far = swap_dp(far, 0)
    self_sent = total_of(self_kept[2:], self_far[1:])
    left, right = (slice(c, c + half) for c in (0, half))
    first = [added(near[:, mid, ..., left], far[:, mid, ..., left]) for mid in (0, 1)]
    second = [added(near[hi, ..., right], far[hi, ..., right]) for hi in (0, 1)]
    first, second, self_sent, lang_back = together(first, second, self_sent, lang_back)

    first_far, second_far, self_sent = swap_dp(first[1], 1), swap_dp(second[1], 2), swap_mp(self_sent, 0)
    late = together(first, second, first_far, second_far, self_sent, rows_three, image_term)
    first, second, first_far, second_far, self_sent, rows_three, image_term = late
    first = [added(first[0][i], first_far[i]) for i in (0, 1)]
    second = [added(second[0][i], second_far[i]) for i in (0, 1)]
    first, second, self_sent = together(first, second, self_sent)
    self_one = total_of(self_kept[1], self_far[0], self_sent[1])

    here = (jnp.arange(2, dtype=jnp.int32) == stream).astype(F32)[:, None, None]
    norm_partial = jnp.concatenate(
        [
            jnp.concatenate([cross_gain, cross_shift], axis=0)[None],
            here * jnp.concatenate([self_gain, self_shift], axis=0)[None],
            here * jnp.concatenate([feed_gain, feed_shift], axis=0)[None],
        ],
        axis=0,
    )
    norm_partial = from_order(norm_partial.reshape(-1, dim), HIGHEST)

    final = from_order(rows_three).astype(BF)

    first_far, second_far = swap_dp(first[1], 2), swap_dp(second[1], 1)
    self_near = swap_dp(self_sums[1][:1], 2)
    extras = image_term, norm_partial, final
    late = together(first[0], second[0], first_far, second_far, self_near, extras)
    first, second, first_far, second_far, self_near, extras = late
    image_term, norm_partial, final = extras
    home = jnp.concatenate([added(first, first_far), added(second, second_far)], axis=-1)
    home = scatter_extra(home)
    self_low = total_of(self_kept[0], self_near[0], self_sent[0])

    kept, sent = parts(home)
    sent = swap_mp(sent, 0)
    self_ones = swap_mp(self_one, 1)
    final_other = swap_dp(final[slot:], 1)
    late = together(kept, sent, self_low, self_ones, image_term, final_other)
    kept, sent, self_low, self_ones, image_term, final_other = late
    self_low = added(self_low, self_ones)
    home = added(kept, sent)

    kept, sent = parts(home)
    sent, theirs, feed_theirs = swap_mp(sent, 1), swap_dp(self_low[1], 1), swap_dp(feed_sum[1], 1)
    image_kept, image_sent = parts(image_term.reshape(n_mp, part, dim))
    image_sent = swap_mp(image_sent, 0)
    late = together(kept, sent, self_low, theirs, feed_theirs, image_kept, image_sent)
    kept, sent, self_low, theirs, feed_theirs, image_kept, image_sent = late
    image_term = added(image_kept, image_sent)

    final_other = after(final_other, kept)
    language_out = out_of_blocks(jnp.where(is_vis, final_other, final[:slot]), lang_rows)
    vision_out = out_of_blocks(jnp.where(is_vis, final[:slot], final_other), vis_rows)

    language_grad = out_of_blocks(lang_back, lang_rows).reshape(language.shape)
    totals = [kept, sent, self_low, theirs]
    sums = call(
        prepare_kernel,
        1,
        [("whole", a) for a in [norm_partial] + totals + [feed_sum, feed_theirs]],
        [("whole", (norm_partial.shape[0] + 1, dim), F32)],
        [],
        "prepare",
        8 * dim * width,
    )[0]
    sums, their_sums = sum_up(sums)
    image_term = after(image_term, kept)
    for bit in range(1, n_bits):
        kept_part, sent_part = parts(image_term)
        image_term = added(kept_part, swap_mp(sent_part, bit))
    for bit in reversed(mp_bits()):
        image_term = jnp.concatenate([image_term, swap_mp(image_term, bit)], axis=0)
    for b in range(n_bits):
        shape = (1 << b, 2, -1, part, dim)
        flipped = image_term.reshape(shape)[:, ::-1].reshape(image_term.shape)
        image_term = jnp.where((place_mp >> b) & 1 == 1, flipped, image_term)
    axes = tuple(reversed(range(n_bits))) + (n_bits, n_bits + 1)
    image_term = image_term.reshape((2,) * n_bits + (part, dim)).transpose(axes)
    image_grad = image_term.reshape(-1, dim)[:image_count].astype(F32).reshape(images.shape)

    kinds = [("step", t) for t in (F32, F32, F32, F32, BF, F32)]
    norm_in = [
        jnp.swapaxes(a, 0, 1)
        for a in (norm_moment, norm_square, norm_weight, norm_average)
    ]
    wide_in = [jnp.swapaxes(a, 1, 2) for a in (attn_in_moment, attn_in_square, attn_in_weight, attn_in_average)]
    wide_out = [attn_out_moment, attn_out_square, attn_out_weight, attn_out_average]
    feed_in = [ffn_in_moment, ffn_in_square, ffn_in_weight, ffn_in_average]
    feed_out = [
        jnp.swapaxes(a, 1, 2)
        for a in (ffn_out_moment, ffn_out_square, ffn_out_weight, ffn_out_average)
    ]
    by_rows = "rows" if shard_rows % 48 == 0 else "whole"
    stepped = call(
        functools.partial(step_kernel, width),
        3,
        [("scalar", which)]
        + [("whole", a) for a in [sums, their_sums] + totals]
        + [(by_rows, feed_sum), (by_rows, feed_theirs)]
        + [("step", a) for a in wide_in + wide_out]
        + [(by_rows, a) for a in feed_in + feed_out]
        + [("whole", a) for a in norm_in],
        [(k, wide_in[0].shape, t) for k, t in kinds]
        + [(k, wide_out[0].shape, t) for k, t in kinds]
        + [(by_rows, feed_in[0].shape, t) for k, t in kinds * 2]
        + [("whole", norm_in[0].shape, F32)] * 5
        + [("whole", (1, 1), F32)],
        [((1, 1), F32)],
        "step",
        20 * 8 * dim * width,
    )
    stepped = [jnp.swapaxes(a, 1, 2) if i < 6 or 18 <= i < 24 else a for i, a in enumerate(stepped)]
    stepped[24:29] = [jnp.swapaxes(a, 0, 1) for a in stepped[24:29]]

    results = [
        language_out.reshape(language.shape),
        vision_out.reshape(vision_cot.shape),
        language_grad,
        image_grad,
    ]
    results += stepped[:-1]
    return tuple(results) + (stepped[-1][0, 0],)


def solution(mesh):
    shape = (mesh.shape["dp"] // 4, 2, 2, mesh.shape["mp"])
    mesh = Mesh(mesh.devices.reshape(shape), DP + ("mp",))
    rows = P(DP + ("mp",), None, None)
    attn_in, attn_out = P(None, DP, None, "mp"), P(None, "mp", DP)
    ffn_in, ffn_out = P(None, DP, "mp"), P(None, "mp", DP)
    in_specs = (rows, P(DP, None, None), P(DP, None), rows, rows)
    in_specs += (attn_in,) * 4 + (attn_out,) * 4 + (ffn_in,) * 4 + (ffn_out,) * 4 + (P(),) * 4
    out_specs = (rows, rows, rows, P(DP, None, None))
    out_specs += (attn_in,) * 6 + (attn_out,) * 6 + (ffn_in,) * 6 + (ffn_out,) * 6 + (P(),) * 6
    return jax.shard_map(local, mesh=mesh, in_specs=in_specs, out_specs=out_specs, check_vma=False)
```
